32 devices in a mesh: grp: 2 (over y), sec: 4 (over z), mpo: 4 (over x, core).
Axes of the slice: x: 2, y: 2, z: 4, core: 2. Of those that a mesh axis runs over, the one named last changes fastest.
Arguments:
- wave_blocks: bfloat16 [8, 512, 512], P(('grp', 'sec')), parts along dimension 0, may hold values from -6 to 6
- left_env: bfloat16 [8, 12, 512, 512], P(('grp', 'sec'), 'mpo'), parts along dimension 0, may hold values from -0.25 to 0.25
- right_env: bfloat16 [8, 12, 512, 512], P(('grp', 'sec'), 'mpo'), parts along dimension 0, may hold values from -0.25 to 0.25
- term_class: int32 [8, 12], P(('grp', 'sec'), 'mpo'), parts along dimension 0, may hold values from 0 to 4
- term_id: int32 [8, 12], P(('grp', 'sec'), 'mpo'), parts along dimension 0, may hold values from 0 to 49
- block_dims: int32 [8, 2], P('grp'), parts along dimension 0, may hold values from 1 to 8, as said below
- pair_table: int32 [8, 5], P('grp'), parts along dimension 0, may hold values from 0 to 3
- mpo_coef: float32 [50], replicated, may hold values from 0.5 to 1.5
Outputs:
- sigma: bfloat16 [8, 512, 512], P('grp', 'sec', 'mpo'), parts along dimension 0
The draws below stay inside these ranges and needn't reach their ends.
There are 2 independent parts, one for each index of `grp`. The reference program is written for one: setup_inputs(seed, part) draws one part's arguments, and reference() takes and returns one part's arrays. A program takes and returns all parts, laid end to end along the dimension named above; an argument that names none is the same for every part. Nothing has to cross between parts.
Inputs may be any that keep to these rules, and one draw needn't show every extreme that they name: `block_dims`: some block has 8 units of left states and some block has 8 units of right states.
All inputs are finite; a program needn't handle non-finite values.
Results may differ from the reference program's by a relative error of at most 0.013.
Values may be sent and summed in bfloat16 or wider, within the bound.
No kernel may reach another device: no remote copies, remote signals or barrier semaphores. Data moves between devices by JAX's collectives and lax.ppermute only.
A program may use at most 64 MiB of HBM per device.

```python
import jax
import jax.numpy as jnp
from jax import lax

DMAX = 512
MPO_W = 50
NCLS = 5
TERM_DEV = 3
BLOCKS = 4
TERMS = 12
N_MPO = 4


def draw_block_dims(key, part):
    key = jax.random.fold_in(key, 11)
    key_dims, key_spot = jax.random.split(key)
    counts = jax.random.randint(key_dims, (BLOCKS, 2), 1, 9)
    largest_at = jax.random.randint(key_spot, (2,), 0, BLOCKS)
    counts = counts.at[largest_at[0], 0].set(8)
    counts = counts.at[largest_at[1], 1].set(8)
    return counts.astype(jnp.int32)


def touch_ends(entries, key, low, high):
    extent = entries.shape
    place = [jax.random.randint(jax.random.fold_in(key, axis), (), 0, extent[axis]) for axis in range(len(extent))]
    entries = entries.at[tuple(place)].set(low)
    longest = extent.index(max(extent))
    place[longest] = (place[longest] + 1) % extent[longest]
    return entries.at[tuple(place)].set(high)


def shard_levels(key, shape, pieces, low, largest):
    factor_of, own = 1.0, jax.random.fold_in(key, 6)
    for dim, shards_of in pieces:
        heights = jnp.exp(jax.random.uniform(jax.random.fold_in(own, dim), (shards_of,), jnp.float32, low / len(pieces), largest / len(pieces)))
        factor_of = factor_of * jnp.repeat(heights, shape[dim] // shards_of).reshape([-1 if axis == dim else 1 for axis in range(len(shape))])
    return factor_of


def centred(own_key, extent, spread, most, pieces=(), kind=jnp.bfloat16):
    entries = spread * jax.random.normal(own_key, extent, jnp.float32)
    if pieces:
        entries = entries * shard_levels(own_key, extent, pieces, -0.22, 0.18)
    return jnp.clip(entries, -most, most).astype(kind)


def setup_inputs(seed: int = 0, part: int = 0) -> dict:
    streams_of = jax.random.split(jax.random.key(seed), 9)
    part_splits = jax.random.split(jax.random.fold_in(streams_of[8], part), 9)
    wave_blocks = centred(part_splits[0], (BLOCKS, DMAX, DMAX), 1.0, 6.0, ((0, 4),))
    left_env = centred(part_splits[1], (BLOCKS, TERMS, DMAX, DMAX), DMAX ** -0.5, 0.25, ((0, 4), (1, 4)))
    right_env = centred(part_splits[2], (BLOCKS, TERMS, DMAX, DMAX), DMAX ** -0.5, 0.25, ((0, 4), (1, 4)))
    term_class = touch_ends(jax.random.randint(part_splits[3], (BLOCKS, TERMS), 0, NCLS), jax.random.fold_in(part_splits[3], 1), 0, NCLS - 1).astype(jnp.int32)
    term_id = touch_ends(jax.random.randint(part_splits[4], (BLOCKS, TERMS), 0, MPO_W), jax.random.fold_in(part_splits[4], 1), 0, MPO_W - 1).astype(jnp.int32)
    block_dims = draw_block_dims(jax.random.fold_in(jax.random.fold_in(streams_of[8], part), 71), part)
    pair_table = touch_ends(jax.random.randint(part_splits[6], (BLOCKS, NCLS), 0, BLOCKS), jax.random.fold_in(part_splits[6], 1), 0, BLOCKS - 1).astype(jnp.int32)
    mpo_coef = jnp.clip(jax.random.uniform(streams_of[7], (MPO_W,), jnp.float32, 0.5, 1.5), 0.5, 1.5)
    return dict(wave_blocks=wave_blocks, left_env=left_env, right_env=right_env, term_class=term_class, term_id=term_id, block_dims=block_dims, pair_table=pair_table, mpo_coef=mpo_coef)


def block_masks(block_dims):
    tile_states = DMAX // 8
    positions = jnp.arange(DMAX)
    row_ok = positions[None, :] < block_dims[:, 0:1] * tile_states
    col_ok = positions[None, :] < block_dims[:, 1:2] * tile_states
    return row_ok[:, :, None] & col_ok[:, None, :]


def reference(wave_blocks, left_env, right_env, term_class, term_id, block_dims, pair_table, mpo_coef):
    inside = block_masks(block_dims)
    masked = jnp.where(inside, wave_blocks, jnp.zeros_like(wave_blocks))
    weights = mpo_coef[term_id]
    picks = (term_class[:, :, None] == jnp.arange(NCLS)[None, None, :]).astype(jnp.float32) * weights[:, :, None]

    def per_block(items):
        lefts, rights, single, pick_row = items
        left_part = jnp.einsum("jxy,yz->jxz", lefts.astype(jnp.float32), single.astype(jnp.float32),
                               precision=lax.Precision.HIGHEST).astype(jnp.bfloat16)
        contrib = jnp.einsum("jxz,jwz->jxw", left_part.astype(jnp.float32), rights.astype(jnp.float32),
                             precision=lax.Precision.HIGHEST)
        contrib = contrib.reshape(N_MPO, TERM_DEV, DMAX, DMAX)
        pick_row = pick_row.reshape(N_MPO, TERM_DEV, NCLS)
        grouped = jnp.einsum("gjc,gjxw->gcxw", pick_row, contrib,
                             precision=lax.Precision.HIGHEST).astype(jnp.bfloat16)
        return jnp.sum(grouped.astype(jnp.float32), axis=0)

    parts = lax.map(per_block, (left_env, right_env, masked, picks))
    totals = jnp.zeros((BLOCKS, DMAX, DMAX), jnp.float32)
    totals = totals.at[pair_table.reshape(-1)].add(parts.reshape(BLOCKS * NCLS, DMAX, DMAX))
    return jnp.where(inside, totals, jnp.zeros_like(totals)).astype(jnp.bfloat16)
```

```python
import functools

import jax
import jax.numpy as jnp
from jax import lax
from jax.experimental import pallas as pl
from jax.experimental.pallas import tpu as pltpu
from jax.sharding import PartitionSpec as P

CHUNKS = 2
COLUMN_ORDER = (3, 1, 2, 0)


def term_kernel(
    cls_ref,
    tid_ref,
    pair_ref,
    dims_ref,
    coef_ref,
    wave_hbm,
    left_hbm,
    right_hbm,
    *rest,
    chunks,
    terms,
    targets,
):
    outs, (wave, left, right, wave_sem, left_sem, right_sem) = rest[:-6], rest[-6:]
    width = wave.shape[0]
    strip = width // 4
    rows = strip // chunks
    sec = lax.axis_index("sec")
    mpo = lax.axis_index("mpo")

    wave_copy = pltpu.make_async_copy(wave_hbm.at[0], wave, wave_sem)
    wave_copy.start()
    left_copies, right_copies = [], []
    for j in range(terms):
        for q in range(4):
            src = pl.multiple_of((sec ^ q) * strip, strip)
            copy = pltpu.make_async_copy(
                left_hbm.at[0, j, pl.ds(src, strip)],
                left.at[j, pl.ds(q * strip, strip)],
                left_sem.at[j, q],
            )
            copy.start()
            left_copies.append(copy)
    for j in range(terms):
        for p, r in enumerate(COLUMN_ORDER):
            src = pl.multiple_of((mpo ^ r) * strip, strip)
            copy = pltpu.make_async_copy(
                right_hbm.at[0, j, pl.ds(src, strip)],
                right.at[j, pl.ds(p * strip, strip)],
                right_sem.at[j, p],
            )
            copy.start()
            right_copies.append(copy)

    unit = width // 8
    weights, target = [], []
    for j in range(terms):
        weights.append(coef_ref[tid_ref[0, j]])
        target.append(pair_ref[sec, cls_ref[0, j]])
    scale = [
        [jnp.where(target[j] == t, weights[j], 0.0) for j in range(terms)] for t in range(targets)
    ]

    wave_copy.wait()
    row_pos = lax.broadcasted_iota(jnp.int32, (width, width), 0)
    col_pos = lax.broadcasted_iota(jnp.int32, (width, width), 1)
    inside = (row_pos < dims_ref[sec, 0] * unit) & (col_pos < dims_ref[sec, 1] * unit)
    wave[...] = jnp.where(inside, wave[...].astype(jnp.float32), 0.0).astype(jnp.bfloat16)
    for copy in left_copies:
        copy.wait()
    for h in range(chunks):
        parts = []
        for j in range(terms):
            own = jnp.concatenate(
                [left[j, q * strip + h * rows : q * strip + (h + 1) * rows, :] for q in range(4)],
                axis=0,
            )
            half = jnp.dot(own, wave[...], preferred_element_type=jnp.float32).astype(jnp.bfloat16)
            if h == 0:
                for copy in right_copies[4 * j : 4 * j + 4]:
                    copy.wait()
            parts.append(
                lax.dot_general(
                    half, right[j], (((1,), (1,)), ((), ())), preferred_element_type=jnp.float32
                )
            )
        for p in range(4):
            for t in range(targets):
                total = scale[t][0] * parts[0][:, p * strip : (p + 1) * strip]
                for j in range(1, terms):
                    total += scale[t][j] * parts[j][:, p * strip : (p + 1) * strip]
                outs[4 * h + p][:, t] = total.astype(jnp.bfloat16).reshape(4, rows, strip)


def final_kernel(dims_ref, *rest, chunks):
    pieces, out_ref = rest[:-1], rest[-1]
    targets, strip, _ = out_ref.shape
    rows = strip // chunks
    per = len(pieces) // chunks
    unit = dims_ref.shape[0] * strip // 8
    sec = lax.axis_index("sec")
    mpo = lax.axis_index("mpo")
    col_pos = mpo * strip + lax.broadcasted_iota(jnp.int32, (rows, strip), 1)
    for h in range(chunks):
        row_pos = sec * strip + h * rows + lax.broadcasted_iota(jnp.int32, (rows, strip), 0)
        for t in range(targets):
            total = pieces[per * h][t].astype(jnp.float32)
            for piece in pieces[per * h + 1 : per * (h + 1)]:
                total += piece[t].astype(jnp.float32)
            inside = (row_pos < dims_ref[t, 0] * unit) & (col_pos < dims_ref[t, 1] * unit)
            out_ref[t, h * rows : (h + 1) * rows, :] = jnp.where(inside, total, 0.0).astype(
                jnp.bfloat16
            )


def add(*arrays):
    total = arrays[0].astype(jnp.float32)
    for array in arrays[1:]:
        total = total + array.astype(jnp.float32)
    return total.astype(jnp.bfloat16)


def swap(array, axis, mask):
    return lax.ppermute(array, axis, [(i, i ^ mask) for i in range(lax.axis_size(axis))])


def by_targets(
    wave_blocks, left_env, right_env, term_class, term_id, block_dims, pair_table, mpo_coef
):
    width = wave_blocks.shape[1]
    terms = left_env.shape[1]
    targets = block_dims.shape[0]
    strip = width // 4
    rows = strip // CHUNKS
    smem = pl.BlockSpec(memory_space=pltpu.SMEM)
    vmem = pl.BlockSpec(memory_space=pltpu.VMEM)
    hbm = pl.BlockSpec(memory_space=pl.ANY)
    shape = jax.ShapeDtypeStruct((4, targets, rows, strip), jnp.bfloat16)
    outs = pl.pallas_call(
        functools.partial(term_kernel, chunks=CHUNKS, terms=terms, targets=targets),
        out_shape=[shape] * (4 * CHUNKS),
        in_specs=[smem] * 5 + [hbm] * 3,
        out_specs=[vmem] * (4 * CHUNKS),
        scratch_shapes=[
            pltpu.VMEM((width, width), jnp.bfloat16),
            pltpu.VMEM((terms, width, width), jnp.bfloat16),
            pltpu.VMEM((terms, width, width), jnp.bfloat16),
            pltpu.SemaphoreType.DMA,
            pltpu.SemaphoreType.DMA((terms, 4)),
            pltpu.SemaphoreType.DMA((terms, 4)),
        ],
        compiler_params=pltpu.CompilerParams(vmem_limit_bytes=40 * 1024 * 1024),
        cost_estimate=pl.CostEstimate(
            flops=4 * terms * width**3, bytes_accessed=6 * 1024 * 1024, transcendentals=0
        ),
        name="terms",
    )(term_class, term_id, pair_table, block_dims, mpo_coef, wave_blocks, left_env, right_env)
    pieces = []
    for h in range(CHUNKS):
        far_send, near_send, far_keep, near_keep = outs[4 * h : 4 * h + 4]
        far = add(far_keep, swap(far_send, "mpo", 1))
        near = swap(near_send, "mpo", 1)
        crossed = swap(far, "mpo", 2)
        own = [add(near_keep[q], near[q], crossed[q]) for q in range(4)]
        pieces.append(own[0])
        for q in (2, 3, 1):
            pieces.append(swap(own[q], "sec", q))
    return pl.pallas_call(
        functools.partial(final_kernel, chunks=CHUNKS),
        out_shape=jax.ShapeDtypeStruct((targets, strip, strip), jnp.bfloat16),
        in_specs=[smem] + [vmem] * len(pieces),
        out_specs=vmem,
        name="final",
    )(block_dims, *pieces)


def by_classes(
    wave_blocks, left_env, right_env, term_class, term_id, block_dims, pair_table, mpo_coef
):
    sec_count = lax.axis_size("sec")
    mpo_count = lax.axis_size("mpo")
    local_blocks = wave_blocks.shape[0]
    block_width = wave_blocks.shape[1]
    total_blocks = block_dims.shape[0]
    classes = pair_table.shape[1]
    tile_states = block_width // 8
    positions = jnp.arange(block_width)
    first = lax.axis_index("sec") * local_blocks
    own_dims = lax.dynamic_slice_in_dim(block_dims, first, local_blocks, 0)
    row_ok = positions[None, :] < own_dims[:, 0:1] * tile_states
    col_ok = positions[None, :] < own_dims[:, 1:2] * tile_states
    masked = jnp.where(
        row_ok[:, :, None] & col_ok[:, None, :], wave_blocks, jnp.zeros_like(wave_blocks)
    )
    left_part = jnp.einsum(
        "bjxy,byz->bjxz", left_env, masked, preferred_element_type=jnp.float32
    ).astype(jnp.bfloat16)
    contrib = jnp.einsum(
        "bjxz,bjwz->bjxw", left_part, right_env, preferred_element_type=jnp.float32
    )
    weights = jnp.sum(
        jnp.where(
            term_id[:, :, None] == jnp.arange(mpo_coef.shape[0])[None, None, :],
            mpo_coef[None, None, :],
            0.0,
        ),
        axis=-1,
    )
    picks = (term_class[:, :, None] == jnp.arange(classes)[None, None, :]).astype(
        jnp.float32
    ) * weights[:, :, None]
    grouped = jnp.einsum("bjc,bjxw->bcxw", picks, contrib, precision=lax.Precision.HIGHEST).astype(
        jnp.bfloat16
    )
    targets = pair_table.reshape(-1)
    routing = targets[None, :] == jnp.arange(total_blocks)[:, None]
    strip_rows = block_width // sec_count
    strip_cols = block_width // mpo_count
    outgoing = grouped.reshape(local_blocks * classes, block_width, block_width)
    arrived = lax.all_to_all(
        lax.all_to_all(outgoing, "sec", split_axis=1, concat_axis=0, tiled=True),
        "mpo",
        split_axis=2,
        concat_axis=0,
        tiled=True,
    )
    arrived = arrived.reshape(mpo_count, total_blocks * classes, strip_rows, strip_cols)
    summed = jnp.einsum(
        "tk,mkrw->trw", routing.astype(jnp.bfloat16), arrived, preferred_element_type=jnp.float32
    )
    row_index = lax.axis_index("sec") * strip_rows + jnp.arange(strip_rows)
    col_index = lax.axis_index("mpo") * strip_cols + jnp.arange(strip_cols)
    rows_in = row_index[None, :] < block_dims[:, 0:1] * tile_states
    cols_in = col_index[None, :] < block_dims[:, 1:2] * tile_states
    inside = rows_in[:, :, None] & cols_in[:, None, :]
    return jnp.where(inside, summed, 0.0).astype(jnp.bfloat16)


def solution(mesh):
    placed = (
        P(("grp", "sec"), None, None),
        P(("grp", "sec"), "mpo", None, None),
        P(("grp", "sec"), "mpo", None, None),
        P(("grp", "sec"), "mpo"),
        P(("grp", "sec"), "mpo"),
        P("grp", None),
        P("grp", None),
        P(),
    )

    def on_device(*arrays):
        wave_blocks, block_dims = arrays[0], arrays[5]
        small = wave_blocks.shape[0] == 1 and block_dims.shape[0] == 4
        if small and mesh.shape["sec"] == 4 and mesh.shape["mpo"] == 4:
            return by_targets(*arrays)
        return by_classes(*arrays)

    return jax.shard_map(
        on_device, mesh=mesh, in_specs=placed, out_specs=P("grp", "sec", "mpo"), check_vma=False
    )
```

```python
import functools

import jax
import jax.numpy as jnp
from jax import lax
from jax.experimental import pallas as pl
from jax.experimental.pallas import tpu as pltpu
from jax.sharding import PartitionSpec as P

CALLS = 2
SPLIT = 2
COLUMN_ORDER = (3, 1, 2, 0)
SMALL = pltpu.CompilerParams(vmem_limit_bytes=4 * 1024 * 1024)


def term_kernel(
    cls_hbm,
    tid_hbm,
    pair_hbm,
    dims_hbm,
    coef_hbm,
    wave_hbm,
    left_hbm,
    right_hbm,
    send_ref,
    keep_ref,
    cls,
    tid,
    pair,
    dims,
    coef,
    wave,
    left,
    right,
    total,
    scalar_sems,
    wave_sem,
    left_sems,
    right_sems,
    *,
    call,
):
    width = wave.shape[0]
    terms = left.shape[0]
    targets = total.shape[0]
    strip = width // 4
    share = left.shape[1] // 4
    split = send_ref.shape[1]
    rows = share // split
    unit = width // 8
    sec = lax.axis_index("sec")
    mpo = lax.axis_index("mpo")

    scalars = [
        pltpu.make_async_copy(src, dst, scalar_sems.at[n])
        for n, (src, dst) in enumerate(
            ((cls_hbm, cls), (tid_hbm, tid), (pair_hbm, pair), (dims_hbm, dims), (coef_hbm, coef))
        )
    ]
    for copy in scalars:
        copy.start()
    wave_copy = pltpu.make_async_copy(wave_hbm.at[0], wave, wave_sem)
    wave_copy.start()

    def fetch(j, carry):
        for q in range(4):
            src = pl.multiple_of((sec ^ q) * strip + call * share, 16)
            pltpu.make_async_copy(
                left_hbm.at[0, j, pl.ds(src, share)],
                left.at[j, pl.ds(q * share, share)],
                left_sems.at[j],
            ).start()
        for p, r in enumerate(COLUMN_ORDER):
            src = pl.multiple_of((mpo ^ r) * strip, strip)
            pltpu.make_async_copy(
                right_hbm.at[0, j, pl.ds(src, strip)],
                right.at[j, pl.ds(p * strip, strip)],
                right_sems.at[j],
            ).start()
        return carry

    lax.fori_loop(0, terms, fetch, 0)
    total[...] = jnp.zeros_like(total)
    for copy in scalars:
        copy.wait()
    wave_copy.wait()
    row_limit = dims[0, sec] * unit
    col_limit = dims[1, sec] * unit

    def mask(i, carry):
        base = pl.multiple_of(i * 64, 64)
        row_pos = base + lax.broadcasted_iota(jnp.int32, (64, width), 0)
        col_pos = lax.broadcasted_iota(jnp.int32, (64, width), 1)
        inside = (row_pos < row_limit) & (col_pos < col_limit)
        band = wave[pl.ds(base, 64), :].astype(jnp.float32)
        wave[pl.ds(base, 64), :] = jnp.where(inside, band, 0.0).astype(jnp.bfloat16)
        return carry

    lax.fori_loop(0, width // 64, mask, 0)

    def term(j, carry):
        pltpu.make_async_copy(
            left_hbm.at[0, j, pl.ds(0, 4 * share)], left.at[j], left_sems.at[j]
        ).wait()
        half = jnp.dot(left[j], wave[...], preferred_element_type=jnp.float32)
        half = half.astype(jnp.bfloat16)
        pltpu.make_async_copy(right_hbm.at[0, j], right.at[j], right_sems.at[j]).wait()
        contrib = lax.dot_general(
            half, right[j], (((1,), (1,)), ((), ())), preferred_element_type=jnp.float32
        )
        target = pair[sec, cls[0, j]]
        total[target] += coef[tid[0, j]] * contrib
        return carry

    lax.fori_loop(0, terms, term, 0)

    lane = lax.broadcasted_iota(jnp.int32, (rows, strip), 1)
    line = lax.broadcasted_iota(jnp.int32, (rows, strip), 0)

    def store(t, carry):
        for p, r in enumerate(COLUMN_ORDER):
            out_ref = send_ref if p < 2 else keep_ref
            cols_in = (mpo ^ r) * strip + lane < dims[1, t] * unit
            for q in range(4):
                for g in range(split):
                    first = (sec ^ q) * strip + call * share + g * rows
                    inside = cols_in & (first + line < dims[0, t] * unit)
                    at = q * share + g * rows
                    value = total[t, at : at + rows, p * strip : (p + 1) * strip]
                    out_ref[p % 2, g, q, t] = jnp.where(inside, value, 0.0).astype(jnp.bfloat16)
        return carry

    lax.fori_loop(0, targets, store, 0)


def far_kernel(keep_ref, recv_ref, *rest, piece):
    far_ref = rest[-1]
    far_ref[...] = add(keep_ref[0, piece], recv_ref[0, piece])


def own_kernel(keep_ref, recv_ref, cross_ref, *own_refs, piece):
    for q, own_ref in enumerate(own_refs):
        own_ref[...] = add(keep_ref[1, piece, q], recv_ref[1, piece, q], cross_ref[q])


def final_kernel(*refs):
    pieces, out_ref = refs[:-1], refs[-1]
    rows = pieces[0].shape[1]
    for h in range(out_ref.shape[1] // rows):
        out_ref[:, h * rows : (h + 1) * rows, :] = add(
            *[piece[...] for piece in pieces[4 * h : 4 * h + 4]]
        )


def add(*arrays):
    total = arrays[0].astype(jnp.float32)
    for array in arrays[1:]:
        total = total + array.astype(jnp.float32)
    return total.astype(jnp.bfloat16)


def swap(array, axis, mask):
    return lax.ppermute(array, axis, [(i, i ^ mask) for i in range(lax.axis_size(axis))])


def by_targets(
    wave_blocks, left_env, right_env, term_class, term_id, block_dims, pair_table, mpo_coef
):
    width = wave_blocks.shape[1]
    terms = left_env.shape[1]
    targets = block_dims.shape[0]
    strip = width // 4
    share = strip // CALLS
    rows = share // SPLIT
    vmem = pl.BlockSpec(memory_space=pltpu.VMEM)
    hbm = pl.BlockSpec(memory_space=pltpu.HBM)
    anywhere = pl.BlockSpec(memory_space=pl.ANY)
    block = jax.ShapeDtypeStruct((4, targets, rows, strip), jnp.bfloat16)
    part = jax.ShapeDtypeStruct((targets, rows, strip), jnp.bfloat16)
    pair_out = jax.ShapeDtypeStruct((2, SPLIT) + block.shape, jnp.bfloat16)
    scalars = (term_class, term_id, pair_table, block_dims.T, mpo_coef)
    operands = [
        pltpu.with_memory_space_constraint(x, pltpu.HBM)
        for x in (*scalars, wave_blocks, left_env, right_env)
    ]
    kept, received = [], []
    for call in range(CALLS):
        send, keep = pl.pallas_call(
            functools.partial(term_kernel, call=call),
            out_shape=[pair_out] * 2,
            in_specs=[hbm] * 8,
            out_specs=[vmem] * 2,
            scratch_shapes=[pltpu.SMEM(scalar.shape, scalar.dtype) for scalar in scalars]
            + [
                pltpu.VMEM((width, width), jnp.bfloat16),
                pltpu.VMEM((terms, 4 * share, width), jnp.bfloat16),
                pltpu.VMEM((terms, width, width), jnp.bfloat16),
                pltpu.VMEM((targets, 4 * share, width), jnp.float32),
                pltpu.SemaphoreType.DMA((len(scalars),)),
                pltpu.SemaphoreType.DMA,
                pltpu.SemaphoreType.DMA((terms,)),
                pltpu.SemaphoreType.DMA((terms,)),
            ],
            compiler_params=pltpu.CompilerParams(vmem_limit_bytes=20 * 1024 * 1024),
            cost_estimate=pl.CostEstimate(
                flops=4 * terms * width**3 // CALLS,
                bytes_accessed=4 * 1024 * 1024,
                transcendentals=0,
            ),
            name=f"terms_{call}",
        )(*operands)
        kept.append(keep)
        received.append(swap(send, "mpo", 1))
    pieces = []
    after = []
    for h in range(CALLS * SPLIT):
        keep, recv = kept[h // SPLIT], received[h // SPLIT]
        far = pl.pallas_call(
            functools.partial(far_kernel, piece=h % SPLIT),
            out_shape=block,
            in_specs=[vmem, vmem] + [anywhere] * len(after),
            out_specs=vmem,
            compiler_params=SMALL,
            name=f"far_{h}",
        )(keep, recv, *after)
        crossed = swap(far, "mpo", 2)
        after = [crossed]
        own = pl.pallas_call(
            functools.partial(own_kernel, piece=h % SPLIT),
            out_shape=[part] * 4,
            in_specs=[vmem] * 3,
            out_specs=[vmem] * 4,
            compiler_params=SMALL,
            name=f"own_{h}",
        )(keep, recv, crossed)
        pieces.append(own[0])
        for q in (1, 2, 3):
            pieces.append(swap(own[q], "sec", q))
    return pl.pallas_call(
        final_kernel,
        out_shape=jax.ShapeDtypeStruct((targets, strip, strip), jnp.bfloat16),
        in_specs=[vmem] * len(pieces),
        out_specs=vmem,
        compiler_params=SMALL,
        name="final",
    )(*pieces)


def by_classes(
    wave_blocks, left_env, right_env, term_class, term_id, block_dims, pair_table, mpo_coef
):
    sec_count = lax.axis_size("sec")
    mpo_count = lax.axis_size("mpo")
    local_blocks = wave_blocks.shape[0]
    block_width = wave_blocks.shape[1]
    total_blocks = block_dims.shape[0]
    classes = pair_table.shape[1]
    tile_states = block_width // 8
    positions = jnp.arange(block_width)
    first = lax.axis_index("sec") * local_blocks
    own_dims = lax.dynamic_slice_in_dim(block_dims, first, local_blocks, 0)
    row_ok = positions[None, :] < own_dims[:, 0:1] * tile_states
    col_ok = positions[None, :] < own_dims[:, 1:2] * tile_states
    masked = jnp.where(
        row_ok[:, :, None] & col_ok[:, None, :], wave_blocks, jnp.zeros_like(wave_blocks)
    )
    left_part = jnp.einsum(
        "bjxy,byz->bjxz", left_env, masked, preferred_element_type=jnp.float32
    ).astype(jnp.bfloat16)
    contrib = jnp.einsum(
        "bjxz,bjwz->bjxw", left_part, right_env, preferred_element_type=jnp.float32
    )
    weights = jnp.sum(
        jnp.where(
            term_id[:, :, None] == jnp.arange(mpo_coef.shape[0])[None, None, :],
            mpo_coef[None, None, :],
            0.0,
        ),
        axis=-1,
    )
    picks = (term_class[:, :, None] == jnp.arange(classes)[None, None, :]).astype(
        jnp.float32
    ) * weights[:, :, None]
    grouped = jnp.einsum("bjc,bjxw->bcxw", picks, contrib, precision=lax.Precision.HIGHEST).astype(
        jnp.bfloat16
    )
    targets = pair_table.reshape(-1)
    routing = targets[None, :] == jnp.arange(total_blocks)[:, None]
    strip_rows = block_width // sec_count
    strip_cols = block_width // mpo_count
    outgoing = grouped.reshape(local_blocks * classes, block_width, block_width)
    arrived = lax.all_to_all(
        lax.all_to_all(outgoing, "sec", split_axis=1, concat_axis=0, tiled=True),
        "mpo",
        split_axis=2,
        concat_axis=0,
        tiled=True,
    )
    arrived = arrived.reshape(mpo_count, total_blocks * classes, strip_rows, strip_cols)
    summed = jnp.einsum(
        "tk,mkrw->trw", routing.astype(jnp.bfloat16), arrived, preferred_element_type=jnp.float32
    )
    row_index = lax.axis_index("sec") * strip_rows + jnp.arange(strip_rows)
    col_index = lax.axis_index("mpo") * strip_cols + jnp.arange(strip_cols)
    rows_in = row_index[None, :] < block_dims[:, 0:1] * tile_states
    cols_in = col_index[None, :] < block_dims[:, 1:2] * tile_states
    inside = rows_in[:, :, None] & cols_in[:, None, :]
    return jnp.where(inside, summed, 0.0).astype(jnp.bfloat16)


def solution(mesh):
    placed = (
        P(("grp", "sec"), None, None),
        P(("grp", "sec"), "mpo", None, None),
        P(("grp", "sec"), "mpo", None, None),
        P(("grp", "sec"), "mpo"),
        P(("grp", "sec"), "mpo"),
        P("grp", None),
        P("grp", None),
        P(),
    )

    def on_device(*arrays):
        wave_blocks, block_dims = arrays[0], arrays[5]
        small = wave_blocks.shape[0] == 1 and block_dims.shape[0] == 4
        if small and mesh.shape["sec"] == 4 and mesh.shape["mpo"] == 4:
            return by_targets(*arrays)
        return by_classes(*arrays)

    return jax.shard_map(
        on_device, mesh=mesh, in_specs=placed, out_specs=P("grp", "sec", "mpo"), check_vma=False
    )
```

```python
import functools

import jax
import jax.numpy as jnp
from jax import lax
from jax.experimental import pallas as pl
from jax.experimental.pallas import tpu as pltpu
from jax.sharding import PartitionSpec as P


def term_kernel(
    cls_hbm,
    tid_hbm,
    pair_hbm,
    dims_hbm,
    coef_hbm,
    wave_hbm,
    left_hbm,
    right_hbm,
    out_ref,
    cls,
    tid,
    pair,
    dims,
    coef,
    wave,
    left,
    right,
    total,
    scalar_sems,
    wave_sem,
    left_sems,
    right_sems,
    *,
    call,
):
    width = wave.shape[0]
    terms = left.shape[0]
    targets = total.shape[0]
    strip = width // 4
    share = left.shape[1] // 4
    split = 1
    rows = share // split
    unit = width // 8
    sec = lax.axis_index("sec")
    mpo = lax.axis_index("mpo")

    scalars = [
        pltpu.make_async_copy(src, dst, scalar_sems.at[n])
        for n, (src, dst) in enumerate(
            ((cls_hbm, cls), (tid_hbm, tid), (pair_hbm, pair), (dims_hbm, dims), (coef_hbm, coef))
        )
    ]
    for copy in scalars:
        copy.start()
    wave_copy = pltpu.make_async_copy(wave_hbm.at[0], wave, wave_sem)
    wave_copy.start()

    def fetch(j, carry):
        for q in range(4):
            src = q * strip + call * share
            pltpu.make_async_copy(
                left_hbm.at[0, j, pl.ds(src, share)],
                left.at[j, pl.ds(q * share, share)],
                left_sems.at[j],
            ).start()
        for p in range(4):
            src = p * strip
            pltpu.make_async_copy(
                right_hbm.at[0, j, pl.ds(src, strip)],
                right.at[j, pl.ds(p * strip, strip)],
                right_sems.at[j],
            ).start()
        return carry

    lax.fori_loop(0, terms, fetch, 0)
    total[...] = jnp.zeros_like(total)
    for copy in scalars:
        copy.wait()
    wave_copy.wait()
    row_limit = dims[0, sec] * unit
    col_limit = dims[1, sec] * unit

    def mask(i, carry):
        base = pl.multiple_of(i * 64, 64)
        row_pos = base + lax.broadcasted_iota(jnp.int32, (64, width), 0)
        col_pos = lax.broadcasted_iota(jnp.int32, (64, width), 1)
        inside = (row_pos < row_limit) & (col_pos < col_limit)
        band = wave[pl.ds(base, 64), :].astype(jnp.float32)
        wave[pl.ds(base, 64), :] = jnp.where(inside, band, 0.0).astype(jnp.bfloat16)
        return carry

    lax.fori_loop(0, width // 64, mask, 0)

    def term(j, carry):
        pltpu.make_async_copy(
            left_hbm.at[0, j, pl.ds(0, 4 * share)], left.at[j], left_sems.at[j]
        ).wait()
        half = jnp.dot(left[j], wave[...], preferred_element_type=jnp.float32)
        half = half.astype(jnp.bfloat16)
        pltpu.make_async_copy(right_hbm.at[0, j], right.at[j], right_sems.at[j]).wait()
        contrib = lax.dot_general(
            half, right[j], (((1,), (1,)), ((), ())), preferred_element_type=jnp.float32
        )
        target = pair[sec, cls[0, j]]
        total[target] += coef[tid[0, j]] * contrib
        return carry

    lax.fori_loop(0, terms, term, 0)

    lane = lax.broadcasted_iota(jnp.int32, (rows, strip), 1)
    line = lax.broadcasted_iota(jnp.int32, (rows, strip), 0)

    def store(t, carry):
        for p in range(4):
            cols_in = p * strip + lane < dims[1, t] * unit
            for q in range(4):
                for g in range(split):
                    first = q * strip + call * share + g * rows
                    inside = cols_in & (first + line < dims[0, t] * unit)
                    at = q * share + g * rows
                    value = total[t, at : at + rows, p * strip : (p + 1) * strip]
                    out_ref[p, q, t] = jnp.where(inside, value, 0.0).astype(jnp.bfloat16)
        return carry

    lax.fori_loop(0, targets, store, 0)


def by_targets(
    wave_blocks, left_env, right_env, term_class, term_id, block_dims, pair_table, mpo_coef
):
    width = wave_blocks.shape[1]
    terms = left_env.shape[1]
    targets = block_dims.shape[0]
    strip = width // 4
    vmem = pl.BlockSpec(memory_space=pltpu.VMEM)
    hbm = pl.BlockSpec(memory_space=pltpu.HBM)
    scalars = (term_class, term_id, pair_table, block_dims.T, mpo_coef)
    operands = [
        pltpu.with_memory_space_constraint(x, pltpu.HBM)
        for x in (*scalars, wave_blocks, left_env, right_env)
    ]
    out = pl.pallas_call(
        functools.partial(term_kernel, call=0),
        out_shape=jax.ShapeDtypeStruct((4, 4, targets, strip, strip), jnp.bfloat16),
        in_specs=[hbm] * 8,
        out_specs=vmem,
        scratch_shapes=[pltpu.SMEM(scalar.shape, scalar.dtype) for scalar in scalars]
        + [
            pltpu.VMEM((width, width), jnp.bfloat16),
            pltpu.VMEM((terms, width, width), jnp.bfloat16),
            pltpu.VMEM((terms, width, width), jnp.bfloat16),
            pltpu.VMEM((targets, width, width), jnp.float32),
            pltpu.SemaphoreType.DMA((len(scalars),)),
            pltpu.SemaphoreType.DMA,
            pltpu.SemaphoreType.DMA((terms,)),
            pltpu.SemaphoreType.DMA((terms,)),
        ],
        compiler_params=pltpu.CompilerParams(vmem_limit_bytes=20 * 1024 * 1024),
        cost_estimate=pl.CostEstimate(
            flops=4 * terms * width**3, bytes_accessed=4 * 1024 * 1024, transcendentals=0
        ),
        name="terms",
    )(*operands)
    out = lax.psum_scatter(out, "mpo", scatter_dimension=0, tiled=False)
    return lax.psum_scatter(out, "sec", scatter_dimension=0, tiled=False)


def by_classes(
    wave_blocks, left_env, right_env, term_class, term_id, block_dims, pair_table, mpo_coef
):
    sec_count = lax.axis_size("sec")
    mpo_count = lax.axis_size("mpo")
    local_blocks = wave_blocks.shape[0]
    block_width = wave_blocks.shape[1]
    total_blocks = block_dims.shape[0]
    classes = pair_table.shape[1]
    tile_states = block_width // 8
    positions = jnp.arange(block_width)
    first = lax.axis_index("sec") * local_blocks
    own_dims = lax.dynamic_slice_in_dim(block_dims, first, local_blocks, 0)
    row_ok = positions[None, :] < own_dims[:, 0:1] * tile_states
    col_ok = positions[None, :] < own_dims[:, 1:2] * tile_states
    masked = jnp.where(
        row_ok[:, :, None] & col_ok[:, None, :], wave_blocks, jnp.zeros_like(wave_blocks)
    )
    left_part = jnp.einsum(
        "bjxy,byz->bjxz", left_env, masked, preferred_element_type=jnp.float32
    ).astype(jnp.bfloat16)
    contrib = jnp.einsum(
        "bjxz,bjwz->bjxw", left_part, right_env, preferred_element_type=jnp.float32
    )
    weights = jnp.sum(
        jnp.where(
            term_id[:, :, None] == jnp.arange(mpo_coef.shape[0])[None, None, :],
            mpo_coef[None, None, :],
            0.0,
        ),
        axis=-1,
    )
    picks = (term_class[:, :, None] == jnp.arange(classes)[None, None, :]).astype(
        jnp.float32
    ) * weights[:, :, None]
    grouped = jnp.einsum("bjc,bjxw->bcxw", picks, contrib, precision=lax.Precision.HIGHEST).astype(
        jnp.bfloat16
    )
    targets = pair_table.reshape(-1)
    routing = targets[None, :] == jnp.arange(total_blocks)[:, None]
    strip_rows = block_width // sec_count
    strip_cols = block_width // mpo_count
    outgoing = grouped.reshape(local_blocks * classes, block_width, block_width)
    arrived = lax.all_to_all(
        lax.all_to_all(outgoing, "sec", split_axis=1, concat_axis=0, tiled=True),
        "mpo",
        split_axis=2,
        concat_axis=0,
        tiled=True,
    )
    arrived = arrived.reshape(mpo_count, total_blocks * classes, strip_rows, strip_cols)
    summed = jnp.einsum(
        "tk,mkrw->trw", routing.astype(jnp.bfloat16), arrived, preferred_element_type=jnp.float32
    )
    row_index = lax.axis_index("sec") * strip_rows + jnp.arange(strip_rows)
    col_index = lax.axis_index("mpo") * strip_cols + jnp.arange(strip_cols)
    rows_in = row_index[None, :] < block_dims[:, 0:1] * tile_states
    cols_in = col_index[None, :] < block_dims[:, 1:2] * tile_states
    inside = rows_in[:, :, None] & cols_in[:, None, :]
    return jnp.where(inside, summed, 0.0).astype(jnp.bfloat16)


def solution(mesh):
    placed = (
        P(("grp", "sec"), None, None),
        P(("grp", "sec"), "mpo", None, None),
        P(("grp", "sec"), "mpo", None, None),
        P(("grp", "sec"), "mpo"),
        P(("grp", "sec"), "mpo"),
        P("grp", None),
        P("grp", None),
        P(),
    )

    def on_device(*arrays):
        wave_blocks, block_dims = arrays[0], arrays[5]
        small = wave_blocks.shape[0] == 1 and block_dims.shape[0] == 4
        if small and mesh.shape["sec"] == 4 and mesh.shape["mpo"] == 4:
            return by_targets(*arrays)
        return by_classes(*arrays)

    return jax.shard_map(
        on_device, mesh=mesh, in_specs=placed, out_specs=P("grp", "sec", "mpo"), check_vma=False
    )
```

```python
import functools

import jax
import jax.numpy as jnp
from jax import lax
from jax.experimental import pallas as pl
from jax.experimental.pallas import tpu as pltpu
from jax.sharding import PartitionSpec as P

SPLIT = 2
COLUMN_ORDER = (3, 1, 2, 0)
SMALL = pltpu.CompilerParams(vmem_limit_bytes=4 * 1024 * 1024)


def term_kernel(
    cls_hbm,
    tid_hbm,
    pair_hbm,
    dims_hbm,
    coef_hbm,
    wave_hbm,
    left_hbm,
    right_hbm,
    far_send,
    near_send,
    far_keep,
    near_keep,
    cls,
    tid,
    pair,
    dims,
    coef,
    wave,
    left,
    right,
    total,
    scalar_sems,
    wave_sem,
    left_sems,
    right_sems,
):
    width = wave.shape[0]
    terms = left.shape[0]
    targets = total.shape[0]
    strip = width // 4
    split, _, _, rows, _ = far_send.shape
    unit = width // 8
    sec = lax.axis_index("sec")
    mpo = lax.axis_index("mpo")

    scalars = [
        pltpu.make_async_copy(src, dst, scalar_sems.at[n])
        for n, (src, dst) in enumerate(
            ((cls_hbm, cls), (tid_hbm, tid), (pair_hbm, pair), (dims_hbm, dims), (coef_hbm, coef))
        )
    ]
    for copy in scalars:
        copy.start()
    wave_copy = pltpu.make_async_copy(wave_hbm.at[0], wave, wave_sem)
    wave_copy.start()

    def fetch(j, carry):
        pltpu.make_async_copy(left_hbm.at[0, j], left.at[j], left_sems.at[j]).start()
        for p, r in enumerate(COLUMN_ORDER):
            src = pl.multiple_of((mpo ^ r) * strip, strip)
            pltpu.make_async_copy(
                right_hbm.at[0, j, pl.ds(src, strip)],
                right.at[j, pl.ds(p * strip, strip)],
                right_sems.at[j],
            ).start()
        return carry

    lax.fori_loop(0, terms, fetch, 0)
    total[...] = jnp.zeros_like(total)
    for copy in scalars:
        copy.wait()
    wave_copy.wait()
    row_limit = dims[0, sec] * unit
    col_limit = dims[1, sec] * unit

    def mask(i, carry):
        base = pl.multiple_of(i * 64, 64)
        row_pos = base + lax.broadcasted_iota(jnp.int32, (64, width), 0)
        col_pos = lax.broadcasted_iota(jnp.int32, (64, width), 1)
        inside = (row_pos < row_limit) & (col_pos < col_limit)
        band = wave[pl.ds(base, 64), :].astype(jnp.float32)
        wave[pl.ds(base, 64), :] = jnp.where(inside, band, 0.0).astype(jnp.bfloat16)
        return carry

    lax.fori_loop(0, width // 64, mask, 0)

    def term(j, carry):
        pltpu.make_async_copy(left_hbm.at[0, j], left.at[j], left_sems.at[j]).wait()
        half = jnp.dot(left[j], wave[...], preferred_element_type=jnp.float32)
        half = half.astype(jnp.bfloat16)
        pltpu.make_async_copy(right_hbm.at[0, j], right.at[j], right_sems.at[j]).wait()
        contrib = lax.dot_general(
            half, right[j], (((1,), (1,)), ((), ())), preferred_element_type=jnp.float32
        )
        target = pair[sec, cls[0, j]]
        total[target] += coef[tid[0, j]] * contrib
        return carry

    lax.fori_loop(0, terms, term, 0)

    lane = lax.broadcasted_iota(jnp.int32, (rows, strip), 1)
    line = lax.broadcasted_iota(jnp.int32, (rows, strip), 0)

    def store(t, carry):
        for p, r in enumerate(COLUMN_ORDER):
            out_ref = (far_send, near_send, far_keep, near_keep)[p]
            cols_in = (mpo ^ r) * strip + lane < dims[1, t] * unit
            for q in range(4):
                for g in range(split):
                    at = q * strip + g * rows
                    inside = cols_in & (at + line < dims[0, t] * unit)
                    value = total[t, at : at + rows, p * strip : (p + 1) * strip]
                    out_ref[g, q, t] = jnp.where(inside, value, 0.0).astype(jnp.bfloat16)
        return carry

    lax.fori_loop(0, targets, store, 0)


def far_kernel(keep_ref, recv_ref, far_ref, *, piece):
    far_ref[...] = add(keep_ref[piece], recv_ref[piece])


def own_kernel(keep_ref, recv_ref, cross_ref, own_ref, *, piece):
    own_ref[...] = add(keep_ref[piece], recv_ref[piece], cross_ref[...])


def final_kernel(*refs):
    pieces, out_ref = refs[:-1], refs[-1]
    rows = pieces[0].shape[2]
    for h, piece in enumerate(pieces):
        out_ref[:, h * rows : (h + 1) * rows, :] = add(*[piece[k] for k in range(4)])


def add(*arrays):
    total = arrays[0].astype(jnp.float32)
    for array in arrays[1:]:
        total = total + array.astype(jnp.float32)
    return total.astype(jnp.bfloat16)


def swap(array, axis, mask):
    return lax.ppermute(array, axis, [(i, i ^ mask) for i in range(lax.axis_size(axis))])


def by_targets(
    wave_blocks, left_env, right_env, term_class, term_id, block_dims, pair_table, mpo_coef
):
    width = wave_blocks.shape[1]
    terms = left_env.shape[1]
    targets = block_dims.shape[0]
    strip = width // 4
    rows = strip // SPLIT
    vmem = pl.BlockSpec(memory_space=pltpu.VMEM)
    hbm = pl.BlockSpec(memory_space=pltpu.HBM)
    piece = jax.ShapeDtypeStruct((4, targets, rows, strip), jnp.bfloat16)
    pieces = jax.ShapeDtypeStruct((SPLIT,) + piece.shape, jnp.bfloat16)
    scalars = (term_class, term_id, pair_table, block_dims.T, mpo_coef)
    operands = [
        pltpu.with_memory_space_constraint(x, pltpu.HBM)
        for x in (*scalars, wave_blocks, left_env, right_env)
    ]
    far_send, near_send, far_keep, near_keep = pl.pallas_call(
        term_kernel,
        out_shape=[pieces] * 4,
        in_specs=[hbm] * 8,
        out_specs=[vmem] * 4,
        scratch_shapes=[pltpu.SMEM(scalar.shape, scalar.dtype) for scalar in scalars]
        + [
            pltpu.VMEM((width, width), jnp.bfloat16),
            pltpu.VMEM((terms, width, width), jnp.bfloat16),
            pltpu.VMEM((terms, width, width), jnp.bfloat16),
            pltpu.VMEM((targets, width, width), jnp.float32),
            pltpu.SemaphoreType.DMA((len(scalars),)),
            pltpu.SemaphoreType.DMA,
            pltpu.SemaphoreType.DMA((terms,)),
            pltpu.SemaphoreType.DMA((terms,)),
        ],
        compiler_params=pltpu.CompilerParams(vmem_limit_bytes=20 * 1024 * 1024),
        cost_estimate=pl.CostEstimate(
            flops=4 * terms * width**3, bytes_accessed=4 * 1024 * 1024, transcendentals=0
        ),
        name="terms",
    )(*operands)
    far_recv = swap(far_send, "mpo", 1)
    near_recv = swap(near_send, "mpo", 1)
    arrived = []
    for h in range(SPLIT):
        far = pl.pallas_call(
            functools.partial(far_kernel, piece=h),
            out_shape=piece,
            in_specs=[vmem] * 2,
            out_specs=vmem,
            compiler_params=SMALL,
            name=f"far_{h}",
        )(far_keep, far_recv)
        crossed = swap(far, "mpo", 2)
        own = pl.pallas_call(
            functools.partial(own_kernel, piece=h),
            out_shape=piece,
            in_specs=[vmem] * 3,
            out_specs=vmem,
            compiler_params=SMALL,
            name=f"own_{h}",
        )(near_keep, near_recv, crossed)
        arrived.append(lax.all_to_all(own, "sec", split_axis=0, concat_axis=0, tiled=True))
    return pl.pallas_call(
        final_kernel,
        out_shape=jax.ShapeDtypeStruct((targets, strip, strip), jnp.bfloat16),
        in_specs=[vmem] * SPLIT,
        out_specs=vmem,
        compiler_params=SMALL,
        name="final",
    )(*arrived)


def by_classes(
    wave_blocks, left_env, right_env, term_class, term_id, block_dims, pair_table, mpo_coef
):
    sec_count = lax.axis_size("sec")
    mpo_count = lax.axis_size("mpo")
    local_blocks = wave_blocks.shape[0]
    block_width = wave_blocks.shape[1]
    total_blocks = block_dims.shape[0]
    classes = pair_table.shape[1]
    tile_states = block_width // 8
    positions = jnp.arange(block_width)
    first = lax.axis_index("sec") * local_blocks
    own_dims = lax.dynamic_slice_in_dim(block_dims, first, local_blocks, 0)
    row_ok = positions[None, :] < own_dims[:, 0:1] * tile_states
    col_ok = positions[None, :] < own_dims[:, 1:2] * tile_states
    masked = jnp.where(
        row_ok[:, :, None] & col_ok[:, None, :], wave_blocks, jnp.zeros_like(wave_blocks)
    )
    left_part = jnp.einsum(
        "bjxy,byz->bjxz", left_env, masked, preferred_element_type=jnp.float32
    ).astype(jnp.bfloat16)
    contrib = jnp.einsum(
        "bjxz,bjwz->bjxw", left_part, right_env, preferred_element_type=jnp.float32
    )
    weights = jnp.sum(
        jnp.where(
            term_id[:, :, None] == jnp.arange(mpo_coef.shape[0])[None, None, :],
            mpo_coef[None, None, :],
            0.0,
        ),
        axis=-1,
    )
    picks = (term_class[:, :, None] == jnp.arange(classes)[None, None, :]).astype(
        jnp.float32
    ) * weights[:, :, None]
    grouped = jnp.einsum("bjc,bjxw->bcxw", picks, contrib, precision=lax.Precision.HIGHEST).astype(
        jnp.bfloat16
    )
    targets = pair_table.reshape(-1)
    routing = targets[None, :] == jnp.arange(total_blocks)[:, None]
    strip_rows = block_width // sec_count
    strip_cols = block_width // mpo_count
    outgoing = grouped.reshape(local_blocks * classes, block_width, block_width)
    arrived = lax.all_to_all(
        lax.all_to_all(outgoing, "sec", split_axis=1, concat_axis=0, tiled=True),
        "mpo",
        split_axis=2,
        concat_axis=0,
        tiled=True,
    )
    arrived = arrived.reshape(mpo_count, total_blocks * classes, strip_rows, strip_cols)
    summed = jnp.einsum(
        "tk,mkrw->trw", routing.astype(jnp.bfloat16), arrived, preferred_element_type=jnp.float32
    )
    row_index = lax.axis_index("sec") * strip_rows + jnp.arange(strip_rows)
    col_index = lax.axis_index("mpo") * strip_cols + jnp.arange(strip_cols)
    rows_in = row_index[None, :] < block_dims[:, 0:1] * tile_states
    cols_in = col_index[None, :] < block_dims[:, 1:2] * tile_states
    inside = rows_in[:, :, None] & cols_in[:, None, :]
    return jnp.where(inside, summed, 0.0).astype(jnp.bfloat16)


def solution(mesh):
    placed = (
        P(("grp", "sec"), None, None),
        P(("grp", "sec"), "mpo", None, None),
        P(("grp", "sec"), "mpo", None, None),
        P(("grp", "sec"), "mpo"),
        P(("grp", "sec"), "mpo"),
        P("grp", None),
        P("grp", None),
        P(),
    )

    def on_device(*arrays):
        wave_blocks, block_dims = arrays[0], arrays[5]
        small = wave_blocks.shape[0] == 1 and block_dims.shape[0] == 4
        if small and mesh.shape["sec"] == 4 and mesh.shape["mpo"] == 4:
            return by_targets(*arrays)
        return by_classes(*arrays)

    return jax.shard_map(
        on_device, mesh=mesh, in_specs=placed, out_specs=P("grp", "sec", "mpo"), check_vma=False
    )
```

```python
import functools

import jax
import jax.numpy as jnp
from jax import lax
from jax.experimental import pallas as pl
from jax.experimental.pallas import tpu as pltpu
from jax.sharding import PartitionSpec as P

COLUMN_ORDER = (3, 1, 2, 0)
SMALL = pltpu.CompilerParams(vmem_limit_bytes=4 * 1024 * 1024)


def term_kernel(
    cls_hbm,
    tid_hbm,
    pair_hbm,
    dims_hbm,
    coef_hbm,
    wave_hbm,
    left_hbm,
    right_hbm,
    a_far_send,
    a_near_send,
    a_far_keep,
    a_near_keep,
    b_send,
    b_keep,
    cls,
    tid,
    pair,
    dims,
    coef,
    wave,
    left,
    right,
    total,
    scalar_sems,
    wave_sem,
    left_sems,
    right_sems,
):
    width = wave.shape[0]
    terms = left.shape[0]
    targets = total.shape[0]
    strip = width // 4
    unit = width // 8
    sec = lax.axis_index("sec")
    mpo = lax.axis_index("mpo")

    scalars = [
        pltpu.make_async_copy(src, dst, scalar_sems.at[n])
        for n, (src, dst) in enumerate(
            ((cls_hbm, cls), (tid_hbm, tid), (pair_hbm, pair), (dims_hbm, dims), (coef_hbm, coef))
        )
    ]
    for copy in scalars:
        copy.start()
    wave_copy = pltpu.make_async_copy(wave_hbm.at[0], wave, wave_sem)
    wave_copy.start()

    def fetch(j, carry):
        for q in range(4):
            src = pl.multiple_of((sec ^ q) * strip, strip)
            pltpu.make_async_copy(
                left_hbm.at[0, j, pl.ds(src, strip)],
                left.at[j, pl.ds(q * strip, strip)],
                left_sems.at[j],
            ).start()
        for p, r in enumerate(COLUMN_ORDER):
            src = pl.multiple_of((mpo ^ r) * strip, strip)
            pltpu.make_async_copy(
                right_hbm.at[0, j, pl.ds(src, strip)],
                right.at[j, pl.ds(p * strip, strip)],
                right_sems.at[j],
            ).start()
        return carry

    lax.fori_loop(0, terms, fetch, 0)
    total[...] = jnp.zeros_like(total)
    for copy in scalars:
        copy.wait()
    wave_copy.wait()
    row_limit = dims[0, sec] * unit
    col_limit = dims[1, sec] * unit

    def mask(i, carry):
        base = pl.multiple_of(i * 64, 64)
        row_pos = base + lax.broadcasted_iota(jnp.int32, (64, width), 0)
        col_pos = lax.broadcasted_iota(jnp.int32, (64, width), 1)
        inside = (row_pos < row_limit) & (col_pos < col_limit)
        band = wave[pl.ds(base, 64), :].astype(jnp.float32)
        wave[pl.ds(base, 64), :] = jnp.where(inside, band, 0.0).astype(jnp.bfloat16)
        return carry

    lax.fori_loop(0, width // 64, mask, 0)

    def term(j, carry):
        pltpu.make_async_copy(left_hbm.at[0, j], left.at[j], left_sems.at[j]).wait()
        half = jnp.dot(left[j], wave[...], preferred_element_type=jnp.float32)
        half = half.astype(jnp.bfloat16)
        pltpu.make_async_copy(right_hbm.at[0, j], right.at[j], right_sems.at[j]).wait()
        contrib = lax.dot_general(
            half, right[j], (((1,), (1,)), ((), ())), preferred_element_type=jnp.float32
        )
        target = pair[sec, cls[0, j]]
        total[target] += coef[tid[0, j]] * contrib
        return carry

    lax.fori_loop(0, terms, term, 0)

    a_rows = a_far_send.shape[2]
    lane = lax.broadcasted_iota(jnp.int32, (strip, strip), 1)
    line = lax.broadcasted_iota(jnp.int32, (strip, strip), 0)

    def store(t, carry):
        for p, r in enumerate(COLUMN_ORDER):
            a_ref = (a_far_send, a_near_send, a_far_keep, a_near_keep)[p]
            b_ref = b_send if p < 2 else b_keep
            cols_in = (mpo ^ r) * strip + lane < dims[1, t] * unit
            for q in range(4):
                inside = cols_in & ((sec ^ q) * strip + line < dims[0, t] * unit)
                value = total[t, q * strip : (q + 1) * strip, p * strip : (p + 1) * strip]
                value = jnp.where(inside, value, 0.0).astype(jnp.bfloat16)
                a_ref[q, t] = value[:a_rows]
                b_ref[p % 2, q, t] = value[a_rows:]
        return carry

    lax.fori_loop(0, targets, store, 0)


def far_kernel(keep_ref, recv_ref, far_ref):
    far_ref[...] = add(keep_ref[...], recv_ref[...])


def a_kernel(keep_ref, recv_ref, cross_ref, *own_refs):
    for q, own_ref in enumerate(own_refs):
        own_ref[...] = add(keep_ref[q], recv_ref[q], cross_ref[q])


def b_kernel(keep_ref, recv_ref, *own_refs):
    for q, own_ref in enumerate(own_refs):
        own_ref[...] = add(keep_ref[:, q], recv_ref[:, q])


def b_sum_kernel(*refs):
    pieces, (far_ref, near_ref) = refs[:-2], refs[-2:]
    far_ref[...] = add(*[piece[0] for piece in pieces])
    near_ref[...] = add(*[piece[1] for piece in pieces])


def final_kernel(near_ref, cross_ref, *refs):
    pieces, out_ref = refs[:-1], refs[-1]
    a_rows = pieces[0].shape[1]
    out_ref[:, :a_rows, :] = add(*[piece[...] for piece in pieces])
    out_ref[:, a_rows:, :] = add(near_ref[...], cross_ref[...])


def add(*arrays):
    total = arrays[0].astype(jnp.float32)
    for array in arrays[1:]:
        total = total + array.astype(jnp.float32)
    return total.astype(jnp.bfloat16)


def swap(array, axis, mask):
    return lax.ppermute(array, axis, [(i, i ^ mask) for i in range(lax.axis_size(axis))])


def by_targets(
    wave_blocks, left_env, right_env, term_class, term_id, block_dims, pair_table, mpo_coef
):
    width = wave_blocks.shape[1]
    terms = left_env.shape[1]
    targets = block_dims.shape[0]
    strip = width // 4
    a_rows = strip * 5 // 8
    b_rows = strip - a_rows
    vmem = pl.BlockSpec(memory_space=pltpu.VMEM)
    hbm = pl.BlockSpec(memory_space=pltpu.HBM)

    def like(*shape):
        return jax.ShapeDtypeStruct(shape + (strip,), jnp.bfloat16)

    def call(kernel, out_shape, *args):
        return pl.pallas_call(
            kernel,
            out_shape=out_shape,
            in_specs=[vmem] * len(args),
            out_specs=jax.tree.map(lambda _: vmem, out_shape),
            compiler_params=SMALL,
            name=kernel.__name__,
        )(*args)

    scalars = (term_class, term_id, pair_table, block_dims.T, mpo_coef)
    operands = [
        pltpu.with_memory_space_constraint(x, pltpu.HBM)
        for x in (*scalars, wave_blocks, left_env, right_env)
    ]
    a_far_send, a_near_send, a_far_keep, a_near_keep, b_send, b_keep = pl.pallas_call(
        term_kernel,
        out_shape=[like(4, targets, a_rows)] * 4 + [like(2, 4, targets, b_rows)] * 2,
        in_specs=[hbm] * 8,
        out_specs=[vmem] * 6,
        scratch_shapes=[pltpu.SMEM(scalar.shape, scalar.dtype) for scalar in scalars]
        + [
            pltpu.VMEM((width, width), jnp.bfloat16),
            pltpu.VMEM((terms, width, width), jnp.bfloat16),
            pltpu.VMEM((terms, width, width), jnp.bfloat16),
            pltpu.VMEM((targets, width, width), jnp.float32),
            pltpu.SemaphoreType.DMA((len(scalars),)),
            pltpu.SemaphoreType.DMA,
            pltpu.SemaphoreType.DMA((terms,)),
            pltpu.SemaphoreType.DMA((terms,)),
        ],
        compiler_params=pltpu.CompilerParams(vmem_limit_bytes=20 * 1024 * 1024),
        cost_estimate=pl.CostEstimate(
            flops=4 * terms * width**3, bytes_accessed=4 * 1024 * 1024, transcendentals=0
        ),
        name="terms",
    )(*operands)
    a_far_recv = swap(a_far_send, "mpo", 1)
    b_recv = swap(b_send, "mpo", 1)
    a_near_recv = swap(a_near_send, "mpo", 1)
    a_far = call(far_kernel, like(4, targets, a_rows), a_far_keep, a_far_recv)
    a_cross = swap(a_far, "mpo", 2)
    b_own = call(b_kernel, [like(2, targets, b_rows)] * 4, b_keep, b_recv)
    b_pieces = [b_own[0]] + [swap(b_own[q], "sec", q) for q in (1, 2, 3)]
    a_own = call(a_kernel, [like(targets, a_rows)] * 4, a_near_keep, a_near_recv, a_cross)
    a_pieces = [a_own[0]] + [swap(a_own[q], "sec", q) for q in (1, 2, 3)]
    b_far, b_near = call(b_sum_kernel, [like(targets, b_rows)] * 2, *b_pieces)
    b_cross = swap(b_far, "mpo", 2)
    return call(final_kernel, like(targets, strip), b_near, b_cross, *a_pieces)


def by_classes(
    wave_blocks, left_env, right_env, term_class, term_id, block_dims, pair_table, mpo_coef
):
    sec_count = lax.axis_size("sec")
    mpo_count = lax.axis_size("mpo")
    local_blocks = wave_blocks.shape[0]
    block_width = wave_blocks.shape[1]
    total_blocks = block_dims.shape[0]
    classes = pair_table.shape[1]
    tile_states = block_width // 8
    positions = jnp.arange(block_width)
    first = lax.axis_index("sec") * local_blocks
    own_dims = lax.dynamic_slice_in_dim(block_dims, first, local_blocks, 0)
    row_ok = positions[None, :] < own_dims[:, 0:1] * tile_states
    col_ok = positions[None, :] < own_dims[:, 1:2] * tile_states
    masked = jnp.where(
        row_ok[:, :, None] & col_ok[:, None, :], wave_blocks, jnp.zeros_like(wave_blocks)
    )
    left_part = jnp.einsum(
        "bjxy,byz->bjxz", left_env, masked, preferred_element_type=jnp.float32
    ).astype(jnp.bfloat16)
    contrib = jnp.einsum(
        "bjxz,bjwz->bjxw", left_part, right_env, preferred_element_type=jnp.float32
    )
    weights = jnp.sum(
        jnp.where(
            term_id[:, :, None] == jnp.arange(mpo_coef.shape[0])[None, None, :],
            mpo_coef[None, None, :],
            0.0,
        ),
        axis=-1,
    )
    picks = (term_class[:, :, None] == jnp.arange(classes)[None, None, :]).astype(
        jnp.float32
    ) * weights[:, :, None]
    grouped = jnp.einsum("bjc,bjxw->bcxw", picks, contrib, precision=lax.Precision.HIGHEST).astype(
        jnp.bfloat16
    )
    targets = pair_table.reshape(-1)
    routing = targets[None, :] == jnp.arange(total_blocks)[:, None]
    strip_rows = block_width // sec_count
    strip_cols = block_width // mpo_count
    outgoing = grouped.reshape(local_blocks * classes, block_width, block_width)
    arrived = lax.all_to_all(
        lax.all_to_all(outgoing, "sec", split_axis=1, concat_axis=0, tiled=True),
        "mpo",
        split_axis=2,
        concat_axis=0,
        tiled=True,
    )
    arrived = arrived.reshape(mpo_count, total_blocks * classes, strip_rows, strip_cols)
    summed = jnp.einsum(
        "tk,mkrw->trw", routing.astype(jnp.bfloat16), arrived, preferred_element_type=jnp.float32
    )
    row_index = lax.axis_index("sec") * strip_rows + jnp.arange(strip_rows)
    col_index = lax.axis_index("mpo") * strip_cols + jnp.arange(strip_cols)
    rows_in = row_index[None, :] < block_dims[:, 0:1] * tile_states
    cols_in = col_index[None, :] < block_dims[:, 1:2] * tile_states
    inside = rows_in[:, :, None] & cols_in[:, None, :]
    return jnp.where(inside, summed, 0.0).astype(jnp.bfloat16)


def solution(mesh):
    placed = (
        P(("grp", "sec"), None, None),
        P(("grp", "sec"), "mpo", None, None),
        P(("grp", "sec"), "mpo", None, None),
        P(("grp", "sec"), "mpo"),
        P(("grp", "sec"), "mpo"),
        P("grp", None),
        P("grp", None),
        P(),
    )

    def on_device(*arrays):
        wave_blocks, block_dims = arrays[0], arrays[5]
        small = wave_blocks.shape[0] == 1 and block_dims.shape[0] == 4
        if small and mesh.shape["sec"] == 4 and mesh.shape["mpo"] == 4:
            return by_targets(*arrays)
        return by_classes(*arrays)

    return jax.shard_map(
        on_device, mesh=mesh, in_specs=placed, out_specs=P("grp", "sec", "mpo"), check_vma=False
    )
```

```python
import functools

import jax
import jax.numpy as jnp
from jax import lax
from jax.experimental import pallas as pl
from jax.experimental.pallas import tpu as pltpu
from jax.sharding import PartitionSpec as P

COLUMN_ORDER = (3, 1, 2, 0)
SMALL = pltpu.CompilerParams(vmem_limit_bytes=4 * 1024 * 1024)


def term_kernel(
    cls_hbm,
    tid_hbm,
    pair_hbm,
    dims_hbm,
    coef_hbm,
    wave_hbm,
    left_hbm,
    right_hbm,
    first_send,
    first_keep,
    b_send,
    b_keep,
    rest_send,
    rest_keep,
    mask_ref,
    cls,
    tid,
    pair,
    dims,
    coef,
    wave,
    left,
    right,
    scalar_sems,
    wave_sem,
    left_sems,
    right_sems,
):
    width = wave.shape[0]
    terms = left.shape[0]
    targets, strip, _ = mask_ref.shape
    a_rows = first_send.shape[2]
    unit = width // 8
    sec = lax.axis_index("sec")
    mpo = lax.axis_index("mpo")

    scalars = [
        pltpu.make_async_copy(src, dst, scalar_sems.at[n])
        for n, (src, dst) in enumerate(
            ((cls_hbm, cls), (tid_hbm, tid), (pair_hbm, pair), (dims_hbm, dims), (coef_hbm, coef))
        )
    ]
    wave_copy = pltpu.make_async_copy(wave_hbm.at[0], wave, wave_sem)
    wave_copy.start()
    for copy in scalars:
        copy.start()

    def fetch(j, carry):
        for q in range(4):
            src = pl.multiple_of((sec ^ q) * strip, strip)
            pltpu.make_async_copy(
                left_hbm.at[0, j, pl.ds(src, strip)],
                left.at[j, pl.ds(q * strip, strip)],
                left_sems.at[j],
            ).start()
        for p, r in enumerate(COLUMN_ORDER):
            src = pl.multiple_of((mpo ^ r) * strip, strip)
            pltpu.make_async_copy(
                right_hbm.at[0, j, pl.ds(src, strip)],
                right.at[j, pl.ds(p * strip, strip)],
                right_sems.at[j],
            ).start()
        return carry

    lax.fori_loop(0, terms, fetch, 0)
    for ref in (first_send, first_keep, b_send, b_keep, rest_send, rest_keep):

        def clear(q, carry, ref=ref):
            if len(ref.shape) == 4:
                ref[q] = jnp.zeros(ref.shape[1:], ref.dtype)
            else:
                for n in range(ref.shape[0]):
                    ref[n, q] = jnp.zeros(ref.shape[2:], ref.dtype)
            return carry

        lax.fori_loop(0, 4, clear, 0)
    for copy in scalars:
        copy.wait()
    lane = mpo * strip + lax.broadcasted_iota(jnp.int32, (strip, strip), 1)
    line = sec * strip + lax.broadcasted_iota(jnp.int32, (strip, strip), 0)

    def target_mask(t, carry):
        inside = (line < dims[0, t] * unit) & (lane < dims[1, t] * unit)
        mask_ref[t] = jnp.where(inside, 1.0, 0.0).astype(jnp.bfloat16)
        return carry

    lax.fori_loop(0, targets, target_mask, 0)
    wave_copy.wait()
    row_limit = dims[0, sec] * unit
    col_limit = dims[1, sec] * unit

    def mask(i, carry):
        base = pl.multiple_of(i * 64, 64)
        row_pos = base + lax.broadcasted_iota(jnp.int32, (64, width), 0)
        col_pos = lax.broadcasted_iota(jnp.int32, (64, width), 1)
        inside = (row_pos < row_limit) & (col_pos < col_limit)
        band = wave[pl.ds(base, 64), :].astype(jnp.float32)
        wave[pl.ds(base, 64), :] = jnp.where(inside, band, 0.0).astype(jnp.bfloat16)
        return carry

    lax.fori_loop(0, width // 64, mask, 0)

    def term(j, carry):
        pltpu.make_async_copy(left_hbm.at[0, j], left.at[j], left_sems.at[j]).wait()
        half = jnp.dot(left[j], wave[...], preferred_element_type=jnp.float32)
        half = half.astype(jnp.bfloat16)
        pltpu.make_async_copy(right_hbm.at[0, j], right.at[j], right_sems.at[j]).wait()
        t = pair[sec, cls[0, j]]
        weight = coef[tid[0, j]]
        for side in range(2):
            contrib = lax.dot_general(
                half,
                right[j, 2 * side * strip : 2 * (side + 1) * strip, :],
                (((1,), (1,)), ((), ())),
                preferred_element_type=jnp.float32,
            )
            first, b_part, rest = (
                (first_send, b_send, rest_send) if side == 0 else (first_keep, b_keep, rest_keep)
            )
            for q in range(4):
                for n in range(2):
                    value = weight * contrib[
                        q * strip : (q + 1) * strip, n * strip : (n + 1) * strip
                    ]
                    if n == 0:
                        put(first, (q, t), value[:a_rows])
                        put(rest, (0, q, t), value[a_rows : 2 * a_rows])
                    else:
                        put(rest, (1, q, t), value[:a_rows])
                        put(rest, (2, q, t), value[a_rows : 2 * a_rows])
                    put(b_part, (n, q, t), value[2 * a_rows :])
        return carry

    lax.fori_loop(0, terms, term, 0)


def put(ref, at, value):
    ref[at] = (ref[at].astype(jnp.float32) + value).astype(jnp.bfloat16)


def far_first(keep_ref, recv_ref, far_ref):
    far_ref[...] = add(keep_ref[...], recv_ref[...])


def far_second(keep_ref, recv_ref, after_ref, far_ref):
    far_ref[...] = add(keep_ref[0], recv_ref[0])


def own_first(keep_ref, recv_ref, cross_ref, *own_refs):
    for q, own_ref in enumerate(own_refs):
        own_ref[...] = add(keep_ref[1, q], recv_ref[1, q], cross_ref[q])


def own_second(keep_ref, recv_ref, cross_ref, *own_refs):
    for q, own_ref in enumerate(own_refs):
        own_ref[...] = add(keep_ref[2, q], recv_ref[2, q], cross_ref[q])


def b_kernel(keep_ref, recv_ref, rest_in, after_ref, rest_out, *own_refs):
    del rest_in, rest_out
    for q, own_ref in enumerate(own_refs):
        own_ref[...] = add(keep_ref[:, q], recv_ref[:, q])


def b_sum_kernel(*refs):
    pieces, (far_ref, near_ref) = refs[:-2], refs[-2:]
    far_ref[...] = add(*[piece[0] for piece in pieces])
    near_ref[...] = add(*[piece[1] for piece in pieces])


def sum_first(*refs):
    pieces, sum_ref = refs[:-1], refs[-1]
    total = pieces[0][...].astype(jnp.float32)
    for piece in pieces[1:]:
        total = total + piece[...].astype(jnp.float32)
    sum_ref[...] = total


def final_kernel(mask_ref, near_ref, cross_ref, sum_ref, *refs):
    pieces, out_ref = refs[:-1], refs[-1]
    rows = sum_ref.shape[1]
    for first, group in ((0, (sum_ref,)), (rows, pieces), (2 * rows, (near_ref, cross_ref))):
        last = first + group[0].shape[1]
        total = group[0][...].astype(jnp.float32)
        for piece in group[1:]:
            total = total + piece[...].astype(jnp.float32)
        inside = mask_ref[:, first:last, :].astype(jnp.float32) > 0.0
        out_ref[:, first:last, :] = jnp.where(inside, total, 0.0).astype(jnp.bfloat16)


def add(*arrays):
    total = arrays[0].astype(jnp.float32)
    for array in arrays[1:]:
        total = total + array.astype(jnp.float32)
    return total.astype(jnp.bfloat16)


def swap(array, axis, mask):
    return lax.ppermute(array, axis, [(i, i ^ mask) for i in range(lax.axis_size(axis))])


def by_targets(
    wave_blocks, left_env, right_env, term_class, term_id, block_dims, pair_table, mpo_coef
):
    width = wave_blocks.shape[1]
    terms = left_env.shape[1]
    targets = block_dims.shape[0]
    strip = width // 4
    a_rows = strip * 3 // 8
    b_rows = strip - 2 * a_rows
    vmem = pl.BlockSpec(memory_space=pltpu.VMEM)
    hbm = pl.BlockSpec(memory_space=pltpu.HBM)

    def like(*shape):
        return jax.ShapeDtypeStruct(shape + (strip,), jnp.bfloat16)

    def call(kernel, out_shape, *args, aliases={}, span=0.1):
        return pl.pallas_call(
            kernel,
            out_shape=out_shape,
            in_specs=[vmem] * len(args),
            out_specs=jax.tree.map(lambda _: vmem, out_shape),
            input_output_aliases=aliases,
            cost_estimate=pl.CostEstimate(
                flops=round(span * 1e9), bytes_accessed=0, transcendentals=0
            ),
            compiler_params=SMALL,
            name=kernel.__name__,
        )(*args)

    scalars = (term_class, term_id, pair_table, block_dims.T, mpo_coef)
    operands = [
        pltpu.with_memory_space_constraint(x, pltpu.HBM)
        for x in (*scalars, wave_blocks, left_env, right_env)
    ]
    across = like(4, targets, a_rows)
    b_shape = like(2, 4, targets, b_rows)
    rest_shape = like(3, 4, targets, a_rows)
    first_send, first_keep, b_send, b_keep, rest_send, rest_keep, mask = pl.pallas_call(
        term_kernel,
        out_shape=[across] * 2 + [b_shape] * 2 + [rest_shape] * 2 + [like(targets, strip)],
        in_specs=[hbm] * 8,
        out_specs=[vmem] * 7,
        scratch_shapes=[pltpu.SMEM(scalar.shape, scalar.dtype) for scalar in scalars]
        + [
            pltpu.VMEM((width, width), jnp.bfloat16),
            pltpu.VMEM((terms, width, width), jnp.bfloat16),
            pltpu.VMEM((terms, width, width), jnp.bfloat16),
            pltpu.SemaphoreType.DMA((len(scalars),)),
            pltpu.SemaphoreType.DMA,
            pltpu.SemaphoreType.DMA((terms,)),
            pltpu.SemaphoreType.DMA((terms,)),
        ],
        compiler_params=pltpu.CompilerParams(vmem_limit_bytes=20 * 1024 * 1024),
        cost_estimate=pl.CostEstimate(
            flops=4 * terms * width**3, bytes_accessed=4 * 1024 * 1024, transcendentals=0
        ),
        name="terms",
    )(*operands)
    first_recv = swap(first_send, "mpo", 1)
    b_recv = swap(b_send, "mpo", 1)
    first_far = call(far_first, across, first_keep, first_recv, span=3)
    first_cross = swap(first_far, "mpo", 2)
    rest_send, *b_own = call(
        b_kernel,
        [rest_shape] + [like(2, targets, b_rows)] * 4,
        b_keep,
        b_recv,
        rest_send,
        first_far,
        aliases={2: 0},
    )
    b_pieces = [b_own[0]] + [swap(b_own[q], "sec", q) for q in (2, 3, 1)]
    rest_recv = swap(rest_send, "mpo", 1)
    second_far = call(far_second, across, rest_keep, rest_recv, first_cross, span=3)
    second_cross = swap(second_far, "mpo", 2)
    pieces = []
    for kernel, cross in ((own_first, first_cross), (own_second, second_cross)):
        own = call(kernel, [like(targets, a_rows)] * 4, rest_keep, rest_recv, cross)
        pieces += [own[0]] + [swap(own[q], "sec", q) for q in (2, 3, 1)]
    b_far, b_near = call(b_sum_kernel, [like(targets, b_rows)] * 2, *b_pieces, span=3)
    b_cross = swap(b_far, "mpo", 2)
    first_sum = jax.ShapeDtypeStruct((targets, a_rows, strip), jnp.float32)
    first_sum = call(sum_first, first_sum, *pieces[:4], span=3)
    return call(
        final_kernel, like(targets, strip), mask, b_near, b_cross, first_sum, *pieces[4:]
    )


def by_classes(
    wave_blocks, left_env, right_env, term_class, term_id, block_dims, pair_table, mpo_coef
):
    sec_count = lax.axis_size("sec")
    mpo_count = lax.axis_size("mpo")
    local_blocks = wave_blocks.shape[0]
    block_width = wave_blocks.shape[1]
    total_blocks = block_dims.shape[0]
    classes = pair_table.shape[1]
    tile_states = block_width // 8
    positions = jnp.arange(block_width)
    first = lax.axis_index("sec") * local_blocks
    own_dims = lax.dynamic_slice_in_dim(block_dims, first, local_blocks, 0)
    row_ok = positions[None, :] < own_dims[:, 0:1] * tile_states
    col_ok = positions[None, :] < own_dims[:, 1:2] * tile_states
    masked = jnp.where(
        row_ok[:, :, None] & col_ok[:, None, :], wave_blocks, jnp.zeros_like(wave_blocks)
    )
    left_part = jnp.einsum(
        "bjxy,byz->bjxz", left_env, masked, preferred_element_type=jnp.float32
    ).astype(jnp.bfloat16)
    contrib = jnp.einsum(
        "bjxz,bjwz->bjxw", left_part, right_env, preferred_element_type=jnp.float32
    )
    weights = jnp.sum(
        jnp.where(
            term_id[:, :, None] == jnp.arange(mpo_coef.shape[0])[None, None, :],
            mpo_coef[None, None, :],
            0.0,
        ),
        axis=-1,
    )
    picks = (term_class[:, :, None] == jnp.arange(classes)[None, None, :]).astype(
        jnp.float32
    ) * weights[:, :, None]
    grouped = jnp.einsum("bjc,bjxw->bcxw", picks, contrib, precision=lax.Precision.HIGHEST).astype(
        jnp.bfloat16
    )
    targets = pair_table.reshape(-1)
    routing = targets[None, :] == jnp.arange(total_blocks)[:, None]
    strip_rows = block_width // sec_count
    strip_cols = block_width // mpo_count
    outgoing = grouped.reshape(local_blocks * classes, block_width, block_width)
    arrived = lax.all_to_all(
        lax.all_to_all(outgoing, "sec", split_axis=1, concat_axis=0, tiled=True),
        "mpo",
        split_axis=2,
        concat_axis=0,
        tiled=True,
    )
    arrived = arrived.reshape(mpo_count, total_blocks * classes, strip_rows, strip_cols)
    summed = jnp.einsum(
        "tk,mkrw->trw", routing.astype(jnp.bfloat16), arrived, preferred_element_type=jnp.float32
    )
    row_index = lax.axis_index("sec") * strip_rows + jnp.arange(strip_rows)
    col_index = lax.axis_index("mpo") * strip_cols + jnp.arange(strip_cols)
    rows_in = row_index[None, :] < block_dims[:, 0:1] * tile_states
    cols_in = col_index[None, :] < block_dims[:, 1:2] * tile_states
    inside = rows_in[:, :, None] & cols_in[:, None, :]
    return jnp.where(inside, summed, 0.0).astype(jnp.bfloat16)


def solution(mesh):
    placed = (
        P(("grp", "sec"), None, None),
        P(("grp", "sec"), "mpo", None, None),
        P(("grp", "sec"), "mpo", None, None),
        P(("grp", "sec"), "mpo"),
        P(("grp", "sec"), "mpo"),
        P("grp", None),
        P("grp", None),
        P(),
    )

    def on_device(*arrays):
        wave_blocks, block_dims = arrays[0], arrays[5]
        small = wave_blocks.shape[0] == 1 and block_dims.shape[0] == 4
        if small and mesh.shape["sec"] == 4 and mesh.shape["mpo"] == 4:
            return by_targets(*arrays)
        return by_classes(*arrays)

    return jax.shard_map(
        on_device, mesh=mesh, in_specs=placed, out_specs=P("grp", "sec", "mpo"), check_vma=False
    )
```

```python
import functools

import jax
import jax.numpy as jnp
from jax import lax
from jax.experimental import pallas as pl
from jax.experimental.pallas import tpu as pltpu
from jax.sharding import PartitionSpec as P

COLUMN_ORDER = (3, 1, 2, 0)
SMALL = pltpu.CompilerParams(vmem_limit_bytes=4 * 1024 * 1024)


def term_kernel(
    cls_hbm,
    tid_hbm,
    pair_hbm,
    dims_hbm,
    coef_hbm,
    wave_hbm,
    left_hbm,
    right_hbm,
    first_send,
    first_keep,
    soon_send,
    soon_keep,
    rest_send,
    rest_keep,
    mask_ref,
    cls,
    tid,
    pair,
    dims,
    coef,
    wave,
    left,
    right,
    scalar_sems,
    wave_sem,
    left_sems,
    right_sems,
):
    width = wave.shape[0]
    terms = left.shape[0]
    targets, strip, _ = mask_ref.shape
    a_rows = first_send.shape[1] // 2
    b_rows = strip - a_rows
    unit = width // 8
    sec = lax.axis_index("sec")
    mpo = lax.axis_index("mpo")

    scalars = [
        pltpu.make_async_copy(src, dst, scalar_sems.at[n])
        for n, (src, dst) in enumerate(
            ((cls_hbm, cls), (tid_hbm, tid), (pair_hbm, pair), (dims_hbm, dims), (coef_hbm, coef))
        )
    ]
    wave_copy = pltpu.make_async_copy(wave_hbm.at[0], wave, wave_sem)
    wave_copy.start()
    for copy in scalars:
        copy.start()

    def fetch(j, carry):
        for q in range(4):
            src = pl.multiple_of((sec ^ q) * strip, strip)
            pltpu.make_async_copy(
                left_hbm.at[0, j, pl.ds(src, strip)],
                left.at[j, pl.ds(q * strip, strip)],
                left_sems.at[j],
            ).start()
        for p, r in enumerate(COLUMN_ORDER):
            src = pl.multiple_of((mpo ^ r) * strip, strip)
            pltpu.make_async_copy(
                right_hbm.at[0, j, pl.ds(src, strip)],
                right.at[j, pl.ds(p * strip, strip)],
                right_sems.at[j],
            ).start()
        return carry

    lax.fori_loop(0, terms, fetch, 0)
    def clear(t, carry):
        for ref in (first_send, first_keep, rest_send, rest_keep):
            ref[t] = jnp.zeros(ref.shape[1:], ref.dtype)
        for ref in (soon_send, soon_keep):
            for n in range(2):
                ref[n, t] = jnp.zeros(ref.shape[2:], ref.dtype)
        return carry

    lax.fori_loop(0, targets, clear, 0)
    for copy in scalars:
        copy.wait()
    lane = mpo * strip + lax.broadcasted_iota(jnp.int32, (strip, strip), 1)
    line = sec * strip + lax.broadcasted_iota(jnp.int32, (strip, strip), 0)

    def target_mask(t, carry):
        inside = (line < dims[0, t] * unit) & (lane < dims[1, t] * unit)
        mask_ref[t] = jnp.where(inside, 1.0, 0.0).astype(jnp.bfloat16)
        return carry

    lax.fori_loop(0, targets, target_mask, 0)
    wave_copy.wait()
    row_limit = dims[0, sec] * unit
    col_limit = dims[1, sec] * unit

    def mask(i, carry):
        base = pl.multiple_of(i * 64, 64)
        row_pos = base + lax.broadcasted_iota(jnp.int32, (64, width), 0)
        col_pos = lax.broadcasted_iota(jnp.int32, (64, width), 1)
        inside = (row_pos < row_limit) & (col_pos < col_limit)
        band = wave[pl.ds(base, 64), :].astype(jnp.float32)
        wave[pl.ds(base, 64), :] = jnp.where(inside, band, 0.0).astype(jnp.bfloat16)
        return carry

    lax.fori_loop(0, width // 64, mask, 0)

    def term(j, carry):
        pltpu.make_async_copy(left_hbm.at[0, j], left.at[j], left_sems.at[j]).wait()
        half = jnp.dot(left[j], wave[...], preferred_element_type=jnp.float32)
        half = half.astype(jnp.bfloat16)
        pltpu.make_async_copy(right_hbm.at[0, j], right.at[j], right_sems.at[j]).wait()
        t = pair[sec, cls[0, j]]
        weight = coef[tid[0, j]]
        for side in range(2):
            contrib = lax.dot_general(
                half,
                right[j, 2 * side * strip : 2 * (side + 1) * strip, :],
                (((1,), (1,)), ((), ())),
                preferred_element_type=jnp.float32,
            )
            first, soon, rest = (
                (first_send, soon_send, rest_send)
                if side == 0
                else (first_keep, soon_keep, rest_keep)
            )
            for q in range(4):
                for n in range(2):
                    value = weight * contrib[
                        q * strip : (q + 1) * strip, n * strip : (n + 1) * strip
                    ]
                    if q == 0:
                        put(rest, (t,), n * strip, value)
                    elif q == 1:
                        put(soon, (n, t), 0, value)
                    else:
                        if n == 0:
                            put(first, (t,), (q - 2) * a_rows, value[:a_rows])
                        else:
                            put(rest, (t,), 2 * strip + (q - 2) * a_rows, value[:a_rows])
                        put(soon, (n, t), strip + (q - 2) * b_rows, value[a_rows:])
        return carry

    lax.fori_loop(0, terms, term, 0)


def put(ref, at, row, value):
    at = at + (slice(row, row + value.shape[0]), slice(None))
    ref[at] = (ref[at].astype(jnp.float32) + value).astype(jnp.bfloat16)


def far_kernel(keep_ref, recv_ref, far_ref):
    far_ref[...] = add(keep_ref[...], recv_ref[...])


def soon_kernel(keep_ref, recv_ref, rest_in, after_ref, rest_out, *own_refs):
    del rest_in, after_ref, rest_out
    row = 0
    for own_ref in own_refs:
        rows = own_ref.shape[2]
        own_ref[...] = add(keep_ref[:, :, row : row + rows, :], recv_ref[:, :, row : row + rows, :])
        row += rows


def own_kernel(keep_ref, recv_ref, cross_ref, *own_refs):
    rows = own_refs[0].shape[1]
    row = keep_ref.shape[1] - 2 * rows
    for n, own_ref in enumerate(own_refs):
        at = slice(row + n * rows, row + (n + 1) * rows)
        own_ref[...] = add(
            keep_ref[:, at, :], recv_ref[:, at, :], cross_ref[:, n * rows : (n + 1) * rows, :]
        )


def here_kernel(keep_ref, recv_ref, next_ref, two_ref, three_ref, after_ref, far_ref, near_ref):
    del after_ref
    strip = far_ref.shape[1]
    a_rows = strip - two_ref.shape[2]
    for n, out_ref in enumerate((far_ref, near_ref)):
        for first, last in ((0, a_rows), (a_rows, strip)):
            at = slice(n * strip + first, n * strip + last)
            parts = [keep_ref[:, at, :], recv_ref[:, at, :], next_ref[n, :, first:last, :]]
            if first:
                parts += [two_ref[n], three_ref[n]]
            out_ref[:, first:last, :] = total(*parts).astype(out_ref.dtype)


def far_sum_kernel(two_ref, three_ref, sum_ref):
    sum_ref[...] = total(two_ref[...], three_ref[...])


def final_kernel(mask_ref, near_ref, cross_ref, sum_ref, out_ref):
    a_rows, strip = sum_ref.shape[1], out_ref.shape[1]
    for first, last in ((0, a_rows), (a_rows, strip)):
        parts = [near_ref[:, first:last, :], cross_ref[:, first:last, :]]
        if not first:
            parts += [sum_ref[...]]
        inside = mask_ref[:, first:last, :].astype(jnp.float32) > 0.0
        out_ref[:, first:last, :] = jnp.where(inside, total(*parts), 0.0).astype(jnp.bfloat16)


def total(*arrays):
    result = arrays[0].astype(jnp.float32)
    for array in arrays[1:]:
        result = result + array.astype(jnp.float32)
    return result


def add(*arrays):
    return total(*arrays).astype(jnp.bfloat16)


def swap(array, axis, mask):
    return lax.ppermute(array, axis, [(i, i ^ mask) for i in range(lax.axis_size(axis))])


def by_targets(
    wave_blocks, left_env, right_env, term_class, term_id, block_dims, pair_table, mpo_coef
):
    width = wave_blocks.shape[1]
    terms = left_env.shape[1]
    targets = block_dims.shape[0]
    strip = width // 4
    a_rows = strip * 3 // 4
    b_rows = strip - a_rows
    vmem = pl.BlockSpec(memory_space=pltpu.VMEM)
    hbm = pl.BlockSpec(memory_space=pltpu.HBM)

    def like(*shape):
        return jax.ShapeDtypeStruct(shape + (strip,), jnp.bfloat16)

    def call(kernel, out_shape, *args, aliases={}, span=0.1):
        return pl.pallas_call(
            kernel,
            out_shape=out_shape,
            in_specs=[vmem] * len(args),
            out_specs=jax.tree.map(lambda _: vmem, out_shape),
            input_output_aliases=aliases,
            cost_estimate=pl.CostEstimate(
                flops=round(span * 1e9), bytes_accessed=0, transcendentals=0
            ),
            compiler_params=SMALL,
            name=kernel.__name__,
        )(*args)

    scalars = (term_class, term_id, pair_table, block_dims.T, mpo_coef)
    operands = [
        pltpu.with_memory_space_constraint(x, pltpu.HBM)
        for x in (*scalars, wave_blocks, left_env, right_env)
    ]
    first_shape = like(targets, 2 * a_rows)
    soon_shape = like(2, targets, strip + 2 * b_rows)
    rest_shape = like(targets, 2 * strip + 2 * a_rows)
    first_send, first_keep, soon_send, soon_keep, rest_send, rest_keep, mask = pl.pallas_call(
        term_kernel,
        out_shape=[first_shape] * 2
        + [soon_shape] * 2
        + [rest_shape] * 2
        + [like(targets, strip)],
        in_specs=[hbm] * 8,
        out_specs=[vmem] * 7,
        scratch_shapes=[pltpu.SMEM(scalar.shape, scalar.dtype) for scalar in scalars]
        + [
            pltpu.VMEM((width, width), jnp.bfloat16),
            pltpu.VMEM((terms, width, width), jnp.bfloat16),
            pltpu.VMEM((terms, width, width), jnp.bfloat16),
            pltpu.SemaphoreType.DMA((len(scalars),)),
            pltpu.SemaphoreType.DMA,
            pltpu.SemaphoreType.DMA((terms,)),
            pltpu.SemaphoreType.DMA((terms,)),
        ],
        compiler_params=pltpu.CompilerParams(vmem_limit_bytes=20 * 1024 * 1024),
        cost_estimate=pl.CostEstimate(
            flops=4 * terms * width**3, bytes_accessed=4 * 1024 * 1024, transcendentals=0
        ),
        name="terms",
    )(*operands)
    first_recv = swap(first_send, "mpo", 1)
    soon_recv = swap(soon_send, "mpo", 1)
    far = call(far_kernel, first_shape, first_keep, first_recv, span=3)
    cross = swap(far, "mpo", 2)
    part = like(2, targets, b_rows)
    rest_send, *soon = call(
        soon_kernel,
        [rest_shape, like(2, targets, strip), part, part],
        soon_keep,
        soon_recv,
        rest_send,
        far,
        aliases={2: 0},
        span=3,
    )
    two, three, one = [swap(soon[q - 1], "sec", q) for q in (2, 3, 1)]
    rest_recv = swap(rest_send, "mpo", 1)
    own = call(own_kernel, [like(targets, a_rows)] * 2, rest_keep, rest_recv, cross, span=3)
    near = jax.ShapeDtypeStruct((targets, strip, strip), jnp.float32)
    here, near = call(
        here_kernel,
        [like(targets, strip), near],
        rest_keep,
        rest_recv,
        one,
        two,
        three,
        own[0],
        span=3,
    )
    own = [swap(array, "sec", q) for array, q in zip(own, (2, 3))]
    here = swap(here, "mpo", 2)
    far_sum = jax.ShapeDtypeStruct((targets, a_rows, strip), jnp.float32)
    far_sum = call(far_sum_kernel, far_sum, *own, span=3)
    return call(final_kernel, like(targets, strip), mask, near, here, far_sum)


def by_classes(
    wave_blocks, left_env, right_env, term_class, term_id, block_dims, pair_table, mpo_coef
):
    sec_count = lax.axis_size("sec")
    mpo_count = lax.axis_size("mpo")
    local_blocks = wave_blocks.shape[0]
    block_width = wave_blocks.shape[1]
    total_blocks = block_dims.shape[0]
    classes = pair_table.shape[1]
    tile_states = block_width // 8
    positions = jnp.arange(block_width)
    first = lax.axis_index("sec") * local_blocks
    own_dims = lax.dynamic_slice_in_dim(block_dims, first, local_blocks, 0)
    row_ok = positions[None, :] < own_dims[:, 0:1] * tile_states
    col_ok = positions[None, :] < own_dims[:, 1:2] * tile_states
    masked = jnp.where(
        row_ok[:, :, None] & col_ok[:, None, :], wave_blocks, jnp.zeros_like(wave_blocks)
    )
    left_part = jnp.einsum(
        "bjxy,byz->bjxz", left_env, masked, preferred_element_type=jnp.float32
    ).astype(jnp.bfloat16)
    contrib = jnp.einsum(
        "bjxz,bjwz->bjxw", left_part, right_env, preferred_element_type=jnp.float32
    )
    weights = jnp.sum(
        jnp.where(
            term_id[:, :, None] == jnp.arange(mpo_coef.shape[0])[None, None, :],
            mpo_coef[None, None, :],
            0.0,
        ),
        axis=-1,
    )
    picks = (term_class[:, :, None] == jnp.arange(classes)[None, None, :]).astype(
        jnp.float32
    ) * weights[:, :, None]
    grouped = jnp.einsum("bjc,bjxw->bcxw", picks, contrib, precision=lax.Precision.HIGHEST).astype(
        jnp.bfloat16
    )
    targets = pair_table.reshape(-1)
    routing = targets[None, :] == jnp.arange(total_blocks)[:, None]
    strip_rows = block_width // sec_count
    strip_cols = block_width // mpo_count
    outgoing = grouped.reshape(local_blocks * classes, block_width, block_width)
    arrived = lax.all_to_all(
        lax.all_to_all(outgoing, "sec", split_axis=1, concat_axis=0, tiled=True),
        "mpo",
        split_axis=2,
        concat_axis=0,
        tiled=True,
    )
    arrived = arrived.reshape(mpo_count, total_blocks * classes, strip_rows, strip_cols)
    summed = jnp.einsum(
        "tk,mkrw->trw", routing.astype(jnp.bfloat16), arrived, preferred_element_type=jnp.float32
    )
    row_index = lax.axis_index("sec") * strip_rows + jnp.arange(strip_rows)
    col_index = lax.axis_index("mpo") * strip_cols + jnp.arange(strip_cols)
    rows_in = row_index[None, :] < block_dims[:, 0:1] * tile_states
    cols_in = col_index[None, :] < block_dims[:, 1:2] * tile_states
    inside = rows_in[:, :, None] & cols_in[:, None, :]
    return jnp.where(inside, summed, 0.0).astype(jnp.bfloat16)


def solution(mesh):
    placed = (
        P(("grp", "sec"), None, None),
        P(("grp", "sec"), "mpo", None, None),
        P(("grp", "sec"), "mpo", None, None),
        P(("grp", "sec"), "mpo"),
        P(("grp", "sec"), "mpo"),
        P("grp", None),
        P("grp", None),
        P(),
    )

    def on_device(*arrays):
        wave_blocks, block_dims = arrays[0], arrays[5]
        small = wave_blocks.shape[0] == 1 and block_dims.shape[0] == 4
        if small and mesh.shape["sec"] == 4 and mesh.shape["mpo"] == 4:
            return by_targets(*arrays)
        return by_classes(*arrays)

    return jax.shard_map(
        on_device, mesh=mesh, in_specs=placed, out_specs=P("grp", "sec", "mpo"), check_vma=False
    )
```

```python
import functools

import jax
import jax.numpy as jnp
from jax import lax
from jax.experimental import pallas as pl
from jax.experimental.pallas import tpu as pltpu
from jax.sharding import PartitionSpec as P

COLUMN_ORDER = (3, 1, 2, 0)
SMALL = pltpu.CompilerParams(vmem_limit_bytes=4 * 1024 * 1024)


def term_kernel(
    cls_hbm,
    tid_hbm,
    pair_hbm,
    dims_hbm,
    coef_hbm,
    wave_hbm,
    left_hbm,
    right_hbm,
    lead_send,
    lead_keep,
    rest_send,
    rest_keep,
    mask_ref,
    cls,
    tid,
    pair,
    dims,
    coef,
    wave,
    left,
    right,
    scalar_sems,
    wave_sem,
    left_sems,
    right_sems,
):
    width = wave.shape[0]
    terms = left.shape[0]
    targets, strip, _ = mask_ref.shape
    a_rows = (rest_send.shape[1] - 2 * strip) // 2
    b_rows = strip - a_rows
    soon = (2 * a_rows, 2 * a_rows + strip + 2 * b_rows)
    unit = width // 8
    sec = lax.axis_index("sec")
    mpo = lax.axis_index("mpo")

    scalars = [
        pltpu.make_async_copy(src, dst, scalar_sems.at[n])
        for n, (src, dst) in enumerate(
            ((cls_hbm, cls), (tid_hbm, tid), (pair_hbm, pair), (dims_hbm, dims), (coef_hbm, coef))
        )
    ]
    wave_copy = pltpu.make_async_copy(wave_hbm.at[0], wave, wave_sem)
    wave_copy.start()
    for copy in scalars:
        copy.start()

    def fetch(j, carry):
        for q in range(4):
            src = pl.multiple_of((sec ^ q) * strip, strip)
            pltpu.make_async_copy(
                left_hbm.at[0, j, pl.ds(src, strip)],
                left.at[j, pl.ds(q * strip, strip)],
                left_sems.at[j],
            ).start()
        for p, r in enumerate(COLUMN_ORDER):
            src = pl.multiple_of((mpo ^ r) * strip, strip)
            pltpu.make_async_copy(
                right_hbm.at[0, j, pl.ds(src, strip)],
                right.at[j, pl.ds(p * strip, strip)],
                right_sems.at[j],
            ).start()
        return carry

    lax.fori_loop(0, terms, fetch, 0)
    def clear(t, carry):
        for ref in (lead_send, lead_keep, rest_send, rest_keep):
            ref[t] = jnp.zeros(ref.shape[1:], ref.dtype)
        return carry

    lax.fori_loop(0, targets, clear, 0)
    for copy in scalars:
        copy.wait()
    lane = mpo * strip + lax.broadcasted_iota(jnp.int32, (strip, strip), 1)
    line = sec * strip + lax.broadcasted_iota(jnp.int32, (strip, strip), 0)

    def target_mask(t, carry):
        inside = (line < dims[0, t] * unit) & (lane < dims[1, t] * unit)
        mask_ref[t] = jnp.where(inside, 1.0, 0.0).astype(jnp.bfloat16)
        return carry

    lax.fori_loop(0, targets, target_mask, 0)
    wave_copy.wait()
    row_limit = dims[0, sec] * unit
    col_limit = dims[1, sec] * unit

    def mask(i, carry):
        base = pl.multiple_of(i * 64, 64)
        row_pos = base + lax.broadcasted_iota(jnp.int32, (64, width), 0)
        col_pos = lax.broadcasted_iota(jnp.int32, (64, width), 1)
        inside = (row_pos < row_limit) & (col_pos < col_limit)
        band = wave[pl.ds(base, 64), :].astype(jnp.float32)
        wave[pl.ds(base, 64), :] = jnp.where(inside, band, 0.0).astype(jnp.bfloat16)
        return carry

    lax.fori_loop(0, width // 64, mask, 0)

    def term(j):
        pltpu.make_async_copy(left_hbm.at[0, j], left.at[j], left_sems.at[j]).wait()
        half = jnp.dot(left[j], wave[...], preferred_element_type=jnp.float32)
        half = half.astype(jnp.bfloat16)
        pltpu.make_async_copy(right_hbm.at[0, j], right.at[j], right_sems.at[j]).wait()
        t = pair[sec, cls[0, j]]
        weight = coef[tid[0, j]]
        for side in range(2):
            contrib = lax.dot_general(
                half,
                right[j, 2 * side * strip : 2 * (side + 1) * strip, :],
                (((1,), (1,)), ((), ())),
                preferred_element_type=jnp.float32,
            )
            lead, rest = (lead_send, rest_send) if side == 0 else (lead_keep, rest_keep)
            for q in range(4):
                for n in range(2):
                    value = weight * contrib[
                        q * strip : (q + 1) * strip, n * strip : (n + 1) * strip
                    ]
                    if q == 0:
                        put(rest, t, n * strip, value)
                    elif q == 1:
                        put(lead, t, soon[n], value)
                    else:
                        if n == 0:
                            put(lead, t, (q - 2) * a_rows, value[:a_rows])
                        else:
                            put(rest, t, 2 * strip + (q - 2) * a_rows, value[:a_rows])
                        put(lead, t, soon[n] + strip + (q - 2) * b_rows, value[a_rows:])

    for j in range(terms):
        term(j)


def put(ref, t, row, value):
    at = slice(row, row + value.shape[0])
    ref[t, at, :] = (ref[t, at, :].astype(jnp.float32) + value).astype(jnp.bfloat16)


def lead_kernel(keep_ref, recv_ref, rest_in, rest_out, far_ref, *own_refs):
    del rest_in, rest_out
    row = far_ref.shape[1]
    far_ref[...] = add(keep_ref[:, :row, :], recv_ref[:, :row, :])
    for n in range(2):
        for own_ref in own_refs:
            at = slice(row, row + own_ref.shape[2])
            own_ref[n] = add(keep_ref[:, at, :], recv_ref[:, at, :])
            row += own_ref.shape[2]


def own_kernel(keep_ref, recv_ref, cross_ref, *own_refs):
    rows = own_refs[0].shape[1]
    row = keep_ref.shape[1] - 2 * rows
    for n, own_ref in enumerate(own_refs):
        at = slice(row + n * rows, row + (n + 1) * rows)
        own_ref[...] = add(
            keep_ref[:, at, :], recv_ref[:, at, :], cross_ref[:, n * rows : (n + 1) * rows, :]
        )


def middle_kernel(two_ref, three_ref, after_ref, sum_ref):
    del after_ref
    sum_ref[...] = total(two_ref[...], three_ref[...])


def here_kernel(keep_ref, recv_ref, one_ref, middle_ref, far_ref, near_ref):
    strip = far_ref.shape[1]
    a_rows = strip - middle_ref.shape[2]
    for n, out_ref in enumerate((far_ref, near_ref)):
        for first, last in ((0, a_rows), (a_rows, strip)):
            at = slice(n * strip + first, n * strip + last)
            parts = [keep_ref[:, at, :], recv_ref[:, at, :], one_ref[n, :, first:last, :]]
            if first:
                parts += [middle_ref[n]]
            out_ref[:, first:last, :] = total(*parts).astype(out_ref.dtype)


def far_sum_kernel(two_ref, three_ref, sum_ref):
    sum_ref[...] = total(two_ref[...], three_ref[...])


def final_kernel(mask_ref, near_ref, cross_ref, sum_ref, out_ref):
    a_rows, strip = sum_ref.shape[1], out_ref.shape[1]
    for first, last in ((0, a_rows), (a_rows, strip)):
        parts = [near_ref[:, first:last, :], cross_ref[:, first:last, :]]
        if not first:
            parts += [sum_ref[...]]
        inside = mask_ref[:, first:last, :].astype(jnp.float32) > 0.0
        out_ref[:, first:last, :] = jnp.where(inside, total(*parts), 0.0).astype(jnp.bfloat16)


def total(*arrays):
    result = arrays[0].astype(jnp.float32)
    for array in arrays[1:]:
        result = result + array.astype(jnp.float32)
    return result


def add(*arrays):
    return total(*arrays).astype(jnp.bfloat16)


def swap(array, axis, mask):
    return lax.ppermute(array, axis, [(i, i ^ mask) for i in range(lax.axis_size(axis))])


def by_targets(
    wave_blocks, left_env, right_env, term_class, term_id, block_dims, pair_table, mpo_coef
):
    width = wave_blocks.shape[1]
    terms = left_env.shape[1]
    targets = block_dims.shape[0]
    strip = width // 4
    a_rows = strip * 3 // 4
    b_rows = strip - a_rows
    vmem = pl.BlockSpec(memory_space=pltpu.VMEM)
    hbm = pl.BlockSpec(memory_space=pltpu.HBM)

    def like(*shape):
        return jax.ShapeDtypeStruct(shape + (strip,), jnp.bfloat16)

    def call(kernel, out_shape, *args, aliases={}, span=0.1):
        return pl.pallas_call(
            kernel,
            out_shape=out_shape,
            in_specs=[vmem] * len(args),
            out_specs=jax.tree.map(lambda _: vmem, out_shape),
            input_output_aliases=aliases,
            cost_estimate=pl.CostEstimate(
                flops=round(span * 1e9), bytes_accessed=0, transcendentals=0
            ),
            compiler_params=SMALL,
            name=kernel.__name__,
        )(*args)

    scalars = (term_class, term_id, pair_table, block_dims.T, mpo_coef)
    operands = [
        pltpu.with_memory_space_constraint(x, pltpu.HBM)
        for x in (*scalars, wave_blocks, left_env, right_env)
    ]
    lead_shape = like(targets, 2 * a_rows + 2 * (strip + 2 * b_rows))
    rest_shape = like(targets, 2 * strip + 2 * a_rows)
    lead_send, lead_keep, rest_send, rest_keep, mask = pl.pallas_call(
        term_kernel,
        out_shape=[lead_shape] * 2 + [rest_shape] * 2 + [like(targets, strip)],
        in_specs=[hbm] * 8,
        out_specs=[vmem] * 5,
        scratch_shapes=[pltpu.SMEM(scalar.shape, scalar.dtype) for scalar in scalars]
        + [
            pltpu.VMEM((width, width), jnp.bfloat16),
            pltpu.VMEM((terms, width, width), jnp.bfloat16),
            pltpu.VMEM((terms, width, width), jnp.bfloat16),
            pltpu.SemaphoreType.DMA((len(scalars),)),
            pltpu.SemaphoreType.DMA,
            pltpu.SemaphoreType.DMA((terms,)),
            pltpu.SemaphoreType.DMA((terms,)),
        ],
        compiler_params=pltpu.CompilerParams(vmem_limit_bytes=20 * 1024 * 1024),
        cost_estimate=pl.CostEstimate(
            flops=4 * terms * width**3, bytes_accessed=4 * 1024 * 1024, transcendentals=0
        ),
        name="terms",
    )(*operands)
    lead_recv = swap(lead_send, "mpo", 1)
    part = like(2, targets, b_rows)
    rest_send, far, one, two, three = call(
        lead_kernel,
        [rest_shape, like(targets, 2 * a_rows), like(2, targets, strip), part, part],
        lead_keep,
        lead_recv,
        rest_send,
        aliases={2: 0},
        span=3,
    )
    cross = swap(far, "mpo", 2)
    two, three, one = [swap(x, "sec", q) for x, q in ((two, 2), (three, 3), (one, 1))]
    rest_recv = swap(rest_send, "mpo", 1)
    own = call(own_kernel, [like(targets, a_rows)] * 2, rest_keep, rest_recv, cross, span=3)
    middle = jax.ShapeDtypeStruct(part.shape, jnp.float32)
    middle = call(middle_kernel, middle, two, three, own[0], span=3)
    near = jax.ShapeDtypeStruct((targets, strip, strip), jnp.float32)
    here, near = call(
        here_kernel, [like(targets, strip), near], rest_keep, rest_recv, one, middle, span=3
    )
    own = [swap(array, "sec", q) for array, q in zip(own, (2, 3))]
    here = swap(here, "mpo", 2)
    far_sum = jax.ShapeDtypeStruct((targets, a_rows, strip), jnp.float32)
    far_sum = call(far_sum_kernel, far_sum, *own, span=3)
    return call(final_kernel, like(targets, strip), mask, near, here, far_sum)


def by_classes(
    wave_blocks, left_env, right_env, term_class, term_id, block_dims, pair_table, mpo_coef
):
    sec_count = lax.axis_size("sec")
    mpo_count = lax.axis_size("mpo")
    local_blocks = wave_blocks.shape[0]
    block_width = wave_blocks.shape[1]
    total_blocks = block_dims.shape[0]
    classes = pair_table.shape[1]
    tile_states = block_width // 8
    positions = jnp.arange(block_width)
    first = lax.axis_index("sec") * local_blocks
    own_dims = lax.dynamic_slice_in_dim(block_dims, first, local_blocks, 0)
    row_ok = positions[None, :] < own_dims[:, 0:1] * tile_states
    col_ok = positions[None, :] < own_dims[:, 1:2] * tile_states
    masked = jnp.where(
        row_ok[:, :, None] & col_ok[:, None, :], wave_blocks, jnp.zeros_like(wave_blocks)
    )
    left_part = jnp.einsum(
        "bjxy,byz->bjxz", left_env, masked, preferred_element_type=jnp.float32
    ).astype(jnp.bfloat16)
    contrib = jnp.einsum(
        "bjxz,bjwz->bjxw", left_part, right_env, preferred_element_type=jnp.float32
    )
    weights = jnp.sum(
        jnp.where(
            term_id[:, :, None] == jnp.arange(mpo_coef.shape[0])[None, None, :],
            mpo_coef[None, None, :],
            0.0,
        ),
        axis=-1,
    )
    picks = (term_class[:, :, None] == jnp.arange(classes)[None, None, :]).astype(
        jnp.float32
    ) * weights[:, :, None]
    grouped = jnp.einsum("bjc,bjxw->bcxw", picks, contrib, precision=lax.Precision.HIGHEST).astype(
        jnp.bfloat16
    )
    targets = pair_table.reshape(-1)
    routing = targets[None, :] == jnp.arange(total_blocks)[:, None]
    strip_rows = block_width // sec_count
    strip_cols = block_width // mpo_count
    outgoing = grouped.reshape(local_blocks * classes, block_width, block_width)
    arrived = lax.all_to_all(
        lax.all_to_all(outgoing, "sec", split_axis=1, concat_axis=0, tiled=True),
        "mpo",
        split_axis=2,
        concat_axis=0,
        tiled=True,
    )
    arrived = arrived.reshape(mpo_count, total_blocks * classes, strip_rows, strip_cols)
    summed = jnp.einsum(
        "tk,mkrw->trw", routing.astype(jnp.bfloat16), arrived, preferred_element_type=jnp.float32
    )
    row_index = lax.axis_index("sec") * strip_rows + jnp.arange(strip_rows)
    col_index = lax.axis_index("mpo") * strip_cols + jnp.arange(strip_cols)
    rows_in = row_index[None, :] < block_dims[:, 0:1] * tile_states
    cols_in = col_index[None, :] < block_dims[:, 1:2] * tile_states
    inside = rows_in[:, :, None] & cols_in[:, None, :]
    return jnp.where(inside, summed, 0.0).astype(jnp.bfloat16)


def solution(mesh):
    placed = (
        P(("grp", "sec"), None, None),
        P(("grp", "sec"), "mpo", None, None),
        P(("grp", "sec"), "mpo", None, None),
        P(("grp", "sec"), "mpo"),
        P(("grp", "sec"), "mpo"),
        P("grp", None),
        P("grp", None),
        P(),
    )

    def on_device(*arrays):
        wave_blocks, block_dims = arrays[0], arrays[5]
        small = wave_blocks.shape[0] == 1 and block_dims.shape[0] == 4
        if small and mesh.shape["sec"] == 4 and mesh.shape["mpo"] == 4:
            return by_targets(*arrays)
        return by_classes(*arrays)

    return jax.shard_map(
        on_device, mesh=mesh, in_specs=placed, out_specs=P("grp", "sec", "mpo"), check_vma=False
    )
```

```python
import functools

import jax
import jax.numpy as jnp
from jax import lax
from jax.experimental import pallas as pl
from jax.experimental.pallas import tpu as pltpu
from jax.sharding import PartitionSpec as P

COLUMN_ORDER = (3, 1, 2, 0)
SMALL = pltpu.CompilerParams(vmem_limit_bytes=4 * 1024 * 1024)


def send_kernel(
    cls_hbm,
    tid_hbm,
    pair_hbm,
    dims_hbm,
    coef_hbm,
    wave_hbm,
    left_hbm,
    right_hbm,
    lead_ref,
    rest_ref,
    half_ref,
    keep_right,
    cls,
    tid,
    pair,
    dims,
    coef,
    wave,
    left,
    right,
    scalar_sems,
    wave_sem,
    left_sems,
    right_sems,
    keep_sem,
):
    width = wave.shape[0]
    terms = left.shape[0]
    strip = width // 4
    unit = width // 8
    sec = lax.axis_index("sec")
    mpo = lax.axis_index("mpo")

    scalars = [
        pltpu.make_async_copy(src, dst, scalar_sems.at[n])
        for n, (src, dst) in enumerate(
            ((cls_hbm, cls), (tid_hbm, tid), (pair_hbm, pair), (dims_hbm, dims), (coef_hbm, coef))
        )
    ]
    wave_copy = pltpu.make_async_copy(wave_hbm.at[0], wave, wave_sem)
    wave_copy.start()
    for copy in scalars:
        copy.start()

    def fetch(j, carry):
        for q in range(4):
            src = pl.multiple_of((sec ^ q) * strip, strip)
            pltpu.make_async_copy(
                left_hbm.at[0, j, pl.ds(src, strip)],
                left.at[j, pl.ds(q * strip, strip)],
                left_sems.at[j],
            ).start()
        for p, r in enumerate(COLUMN_ORDER[:2]):
            src = pl.multiple_of((mpo ^ r) * strip, strip)
            pltpu.make_async_copy(
                right_hbm.at[0, j, pl.ds(src, strip)],
                right.at[j, pl.ds(p * strip, strip)],
                right_sems.at[j],
            ).start()
        return carry

    def fetch_keep(j, carry):
        for p, r in enumerate(COLUMN_ORDER[2:]):
            src = pl.multiple_of((mpo ^ r) * strip, strip)
            pltpu.make_async_copy(
                right_hbm.at[0, j, pl.ds(src, strip)],
                keep_right.at[j, pl.ds(p * strip, strip)],
                keep_sem,
            ).start()
        return carry

    lax.fori_loop(0, terms, fetch, 0)
    lax.fori_loop(0, terms, fetch_keep, 0)
    clear(lead_ref, rest_ref)
    for copy in scalars:
        copy.wait()
    wave_copy.wait()
    row_limit = dims[0, sec] * unit
    col_limit = dims[1, sec] * unit

    def mask(i, carry):
        base = pl.multiple_of(i * 64, 64)
        row_pos = base + lax.broadcasted_iota(jnp.int32, (64, width), 0)
        col_pos = lax.broadcasted_iota(jnp.int32, (64, width), 1)
        inside = (row_pos < row_limit) & (col_pos < col_limit)
        band = wave[pl.ds(base, 64), :].astype(jnp.float32)
        wave[pl.ds(base, 64), :] = jnp.where(inside, band, 0.0).astype(jnp.bfloat16)
        return carry

    lax.fori_loop(0, width // 64, mask, 0)
    for j in range(terms):
        pltpu.make_async_copy(left_hbm.at[0, j], left.at[j], left_sems.at[j]).wait()
        half = jnp.dot(left[j], wave[...], preferred_element_type=jnp.float32)
        half = half.astype(jnp.bfloat16)
        half_ref[j] = half
        pltpu.make_async_copy(
            right_hbm.at[0, j, pl.ds(0, 2 * strip)], right.at[j], right_sems.at[j]
        ).wait()
        spread(lead_ref, rest_ref, half, right[j], pair[sec, cls[0, j]], coef[tid[0, j]])
    pltpu.make_async_copy(
        right_hbm.at[0, pl.ds(0, terms), pl.ds(0, 2 * strip)], keep_right, keep_sem
    ).wait()


def keep_kernel(
    cls_hbm,
    tid_hbm,
    pair_hbm,
    dims_hbm,
    coef_hbm,
    half_ref,
    right_ref,
    lead_ref,
    rest_ref,
    mask_ref,
    cls,
    tid,
    pair,
    dims,
    coef,
    scalar_sems,
):
    terms, width, _ = half_ref.shape
    targets, strip, _ = mask_ref.shape
    unit = width // 8
    sec = lax.axis_index("sec")
    mpo = lax.axis_index("mpo")
    scalars = [
        pltpu.make_async_copy(src, dst, scalar_sems.at[n])
        for n, (src, dst) in enumerate(
            ((cls_hbm, cls), (tid_hbm, tid), (pair_hbm, pair), (dims_hbm, dims), (coef_hbm, coef))
        )
    ]
    for copy in scalars:
        copy.start()
    clear(lead_ref, rest_ref)
    for copy in scalars:
        copy.wait()
    for j in range(terms):
        spread(
            lead_ref, rest_ref, half_ref[j], right_ref[j], pair[sec, cls[0, j]], coef[tid[0, j]]
        )
    lane = mpo * strip + lax.broadcasted_iota(jnp.int32, (strip, strip), 1)
    line = sec * strip + lax.broadcasted_iota(jnp.int32, (strip, strip), 0)

    def target_mask(t, carry):
        inside = (line < dims[0, t] * unit) & (lane < dims[1, t] * unit)
        mask_ref[t] = jnp.where(inside, 1.0, 0.0).astype(jnp.bfloat16)
        return carry

    lax.fori_loop(0, targets, target_mask, 0)


def clear(*refs):
    def one(t, carry):
        for ref in refs:
            ref[t] = jnp.zeros(ref.shape[1:], ref.dtype)
        return carry

    lax.fori_loop(0, refs[0].shape[0], one, 0)


def spread(lead, rest, half, right, t, weight):
    contrib = lax.dot_general(
        half, right, (((1,), (1,)), ((), ())), preferred_element_type=jnp.float32
    )
    strip = contrib.shape[1] // 2
    a_rows = (rest.shape[1] - 2 * strip) // 2
    b_rows = strip - a_rows
    soon = (2 * a_rows, 2 * a_rows + strip + 2 * b_rows)
    for q in range(4):
        for n in range(2):
            value = weight * contrib[q * strip : (q + 1) * strip, n * strip : (n + 1) * strip]
            if q == 0:
                put(rest, t, n * strip, value)
            elif q == 1:
                put(lead, t, soon[n], value)
            else:
                if n == 0:
                    put(lead, t, (q - 2) * a_rows, value[:a_rows])
                else:
                    put(rest, t, 2 * strip + (q - 2) * a_rows, value[:a_rows])
                put(lead, t, soon[n] + strip + (q - 2) * b_rows, value[a_rows:])


def put(ref, t, row, value):
    at = slice(row, row + value.shape[0])
    ref[t, at, :] = (ref[t, at, :].astype(jnp.float32) + value).astype(jnp.bfloat16)


def lead_kernel(keep_ref, recv_ref, rest_in, rest_out, far_ref, one_far, one_near, *own_refs):
    del rest_in, rest_out
    row = far_ref.shape[1]
    far_ref[...] = add(keep_ref[:, :row, :], recv_ref[:, :row, :])
    for n, one_ref in enumerate((one_far, one_near)):
        at = slice(row, row + one_ref.shape[1])
        one_ref[...] = add(keep_ref[:, at, :], recv_ref[:, at, :])
        row += one_ref.shape[1]
        for own_ref in own_refs:
            at = slice(row, row + own_ref.shape[2])
            own_ref[n] = add(keep_ref[:, at, :], recv_ref[:, at, :])
            row += own_ref.shape[2]


def own_kernel(keep_ref, recv_ref, cross_ref, *own_refs):
    rows = own_refs[0].shape[1]
    row = keep_ref.shape[1] - 2 * rows
    for n, own_ref in enumerate(own_refs):
        at = slice(row + n * rows, row + (n + 1) * rows)
        own_ref[...] = add(
            keep_ref[:, at, :], recv_ref[:, at, :], cross_ref[:, n * rows : (n + 1) * rows, :]
        )


def here_kernel(keep_ref, recv_ref, one_ref, two_ref, three_ref, after_ref, far_ref, near_ref):
    del after_ref
    strip = far_ref.shape[1]
    a_rows = strip - two_ref.shape[2]
    for n, out_ref in enumerate((far_ref, near_ref)):
        for first, last in ((0, a_rows), (a_rows, strip)):
            at = slice(n * strip + first, n * strip + last)
            parts = [keep_ref[:, at, :], recv_ref[:, at, :]]
            if n == 0:
                parts += [one_ref[:, first:last, :]]
            if first:
                parts += [two_ref[n], three_ref[n]]
            out_ref[:, first:last, :] = total(*parts).astype(out_ref.dtype)


def far_sum_kernel(two_ref, three_ref, sum_ref):
    sum_ref[...] = total(two_ref[...], three_ref[...])


def final_kernel(mask_ref, near_ref, one_ref, cross_ref, sum_ref, out_ref):
    a_rows, strip = sum_ref.shape[1], out_ref.shape[1]
    for first, last in ((0, a_rows), (a_rows, strip)):
        parts = [ref[:, first:last, :] for ref in (near_ref, one_ref, cross_ref)]
        if not first:
            parts += [sum_ref[...]]
        inside = mask_ref[:, first:last, :].astype(jnp.float32) > 0.0
        out_ref[:, first:last, :] = jnp.where(inside, total(*parts), 0.0).astype(jnp.bfloat16)


def total(*arrays):
    result = arrays[0].astype(jnp.float32)
    for array in arrays[1:]:
        result = result + array.astype(jnp.float32)
    return result


def add(*arrays):
    return total(*arrays).astype(jnp.bfloat16)


def swap(array, axis, mask):
    return lax.ppermute(array, axis, [(i, i ^ mask) for i in range(lax.axis_size(axis))])


def by_targets(
    wave_blocks, left_env, right_env, term_class, term_id, block_dims, pair_table, mpo_coef
):
    width = wave_blocks.shape[1]
    terms = left_env.shape[1]
    targets = block_dims.shape[0]
    strip = width // 4
    a_rows = strip * 3 // 4
    b_rows = strip - a_rows
    vmem = pl.BlockSpec(memory_space=pltpu.VMEM)
    hbm = pl.BlockSpec(memory_space=pltpu.HBM)

    def like(*shape):
        return jax.ShapeDtypeStruct(shape + (strip,), jnp.bfloat16)

    def call(kernel, out_shape, *args, aliases={}, span=0.1):
        return pl.pallas_call(
            kernel,
            out_shape=out_shape,
            in_specs=[vmem] * len(args),
            out_specs=jax.tree.map(lambda _: vmem, out_shape),
            input_output_aliases=aliases,
            cost_estimate=pl.CostEstimate(
                flops=round(span * 1e9), bytes_accessed=0, transcendentals=0
            ),
            compiler_params=SMALL,
            name=kernel.__name__,
        )(*args)

    scalars = (term_class, term_id, pair_table, block_dims.T, mpo_coef)
    operands = [
        pltpu.with_memory_space_constraint(x, pltpu.HBM)
        for x in (*scalars, wave_blocks, left_env, right_env)
    ]
    lead_shape = like(targets, 2 * a_rows + 2 * (strip + 2 * b_rows))
    rest_shape = like(targets, 2 * strip + 2 * a_rows)
    scalar_room = [pltpu.SMEM(scalar.shape, scalar.dtype) for scalar in scalars]
    limit = pltpu.CompilerParams(vmem_limit_bytes=16 * 1024 * 1024)
    half_shape = jax.ShapeDtypeStruct((terms, width, width), jnp.bfloat16)
    right_shape = jax.ShapeDtypeStruct((terms, 2 * strip, width), jnp.bfloat16)
    lead_send, rest_send, half, keep_right = pl.pallas_call(
        send_kernel,
        out_shape=[lead_shape, rest_shape, half_shape, right_shape],
        in_specs=[hbm] * 8,
        out_specs=[vmem] * 4,
        scratch_shapes=scalar_room
        + [
            pltpu.VMEM((width, width), jnp.bfloat16),
            pltpu.VMEM((terms, width, width), jnp.bfloat16),
            pltpu.VMEM((terms, 2 * strip, width), jnp.bfloat16),
            pltpu.SemaphoreType.DMA((len(scalars),)),
            pltpu.SemaphoreType.DMA,
            pltpu.SemaphoreType.DMA((terms,)),
            pltpu.SemaphoreType.DMA((terms,)),
            pltpu.SemaphoreType.DMA,
        ],
        compiler_params=limit,
        cost_estimate=pl.CostEstimate(
            flops=3 * terms * width**3, bytes_accessed=4 * 1024 * 1024, transcendentals=0
        ),
        name="send_kernel",
    )(*operands)
    lead_keep, rest_keep, mask = pl.pallas_call(
        keep_kernel,
        out_shape=[lead_shape, rest_shape, like(targets, strip)],
        in_specs=[hbm] * len(scalars) + [vmem] * 2,
        out_specs=[vmem] * 3,
        scratch_shapes=scalar_room + [pltpu.SemaphoreType.DMA((len(scalars),))],
        compiler_params=limit,
        cost_estimate=pl.CostEstimate(
            flops=3 * terms * width**3, bytes_accessed=0, transcendentals=0
        ),
        name="keep_kernel",
    )(*operands[: len(scalars)], half, keep_right)
    lead_recv = swap(lead_send, "mpo", 1)
    part = like(2, targets, b_rows)
    rest_send, far, one, one_near, two, three = call(
        lead_kernel,
        [rest_shape, like(targets, 2 * a_rows)] + [like(targets, strip)] * 2 + [part] * 2,
        lead_keep,
        lead_recv,
        rest_send,
        aliases={2: 0},
        span=3,
    )
    cross = swap(far, "mpo", 2)
    one, two, three = [swap(x, "sec", q) for x, q in ((one, 1), (two, 2), (three, 3))]
    one_near = swap(one_near, "sec", 1)
    rest_recv = swap(rest_send, "mpo", 1)
    own = call(own_kernel, [like(targets, a_rows)] * 2, rest_keep, rest_recv, cross, span=3)
    near = jax.ShapeDtypeStruct((targets, strip, strip), jnp.float32)
    here, near = call(
        here_kernel,
        [like(targets, strip), near],
        rest_keep,
        rest_recv,
        one,
        two,
        three,
        own[0],
        span=3,
    )
    own = [swap(array, "sec", q) for array, q in zip(own, (2, 3))]
    here = swap(here, "mpo", 2)
    far_sum = jax.ShapeDtypeStruct((targets, a_rows, strip), jnp.float32)
    far_sum = call(far_sum_kernel, far_sum, *own, span=3)
    return call(final_kernel, like(targets, strip), mask, near, one_near, here, far_sum)


def by_classes(
    wave_blocks, left_env, right_env, term_class, term_id, block_dims, pair_table, mpo_coef
):
    sec_count = lax.axis_size("sec")
    mpo_count = lax.axis_size("mpo")
    local_blocks = wave_blocks.shape[0]
    block_width = wave_blocks.shape[1]
    total_blocks = block_dims.shape[0]
    classes = pair_table.shape[1]
    tile_states = block_width // 8
    positions = jnp.arange(block_width)
    first = lax.axis_index("sec") * local_blocks
    own_dims = lax.dynamic_slice_in_dim(block_dims, first, local_blocks, 0)
    row_ok = positions[None, :] < own_dims[:, 0:1] * tile_states
    col_ok = positions[None, :] < own_dims[:, 1:2] * tile_states
    masked = jnp.where(
        row_ok[:, :, None] & col_ok[:, None, :], wave_blocks, jnp.zeros_like(wave_blocks)
    )
    left_part = jnp.einsum(
        "bjxy,byz->bjxz", left_env, masked, preferred_element_type=jnp.float32
    ).astype(jnp.bfloat16)
    contrib = jnp.einsum(
        "bjxz,bjwz->bjxw", left_part, right_env, preferred_element_type=jnp.float32
    )
    weights = jnp.sum(
        jnp.where(
            term_id[:, :, None] == jnp.arange(mpo_coef.shape[0])[None, None, :],
            mpo_coef[None, None, :],
            0.0,
        ),
        axis=-1,
    )
    picks = (term_class[:, :, None] == jnp.arange(classes)[None, None, :]).astype(
        jnp.float32
    ) * weights[:, :, None]
    grouped = jnp.einsum("bjc,bjxw->bcxw", picks, contrib, precision=lax.Precision.HIGHEST).astype(
        jnp.bfloat16
    )
    targets = pair_table.reshape(-1)
    routing = targets[None, :] == jnp.arange(total_blocks)[:, None]
    strip_rows = block_width // sec_count
    strip_cols = block_width // mpo_count
    outgoing = grouped.reshape(local_blocks * classes, block_width, block_width)
    arrived = lax.all_to_all(
        lax.all_to_all(outgoing, "sec", split_axis=1, concat_axis=0, tiled=True),
        "mpo",
        split_axis=2,
        concat_axis=0,
        tiled=True,
    )
    arrived = arrived.reshape(mpo_count, total_blocks * classes, strip_rows, strip_cols)
    summed = jnp.einsum(
        "tk,mkrw->trw", routing.astype(jnp.bfloat16), arrived, preferred_element_type=jnp.float32
    )
    row_index = lax.axis_index("sec") * strip_rows + jnp.arange(strip_rows)
    col_index = lax.axis_index("mpo") * strip_cols + jnp.arange(strip_cols)
    rows_in = row_index[None, :] < block_dims[:, 0:1] * tile_states
    cols_in = col_index[None, :] < block_dims[:, 1:2] * tile_states
    inside = rows_in[:, :, None] & cols_in[:, None, :]
    return jnp.where(inside, summed, 0.0).astype(jnp.bfloat16)


def solution(mesh):
    placed = (
        P(("grp", "sec"), None, None),
        P(("grp", "sec"), "mpo", None, None),
        P(("grp", "sec"), "mpo", None, None),
        P(("grp", "sec"), "mpo"),
        P(("grp", "sec"), "mpo"),
        P("grp", None),
        P("grp", None),
        P(),
    )

    def on_device(*arrays):
        wave_blocks, block_dims = arrays[0], arrays[5]
        small = wave_blocks.shape[0] == 1 and block_dims.shape[0] == 4
        if small and mesh.shape["sec"] == 4 and mesh.shape["mpo"] == 4:
            return by_targets(*arrays)
        return by_classes(*arrays)

    return jax.shard_map(
        on_device, mesh=mesh, in_specs=placed, out_specs=P("grp", "sec", "mpo"), check_vma=False
    )
```

```python
import functools

import jax
import jax.numpy as jnp
from jax import lax
from jax.experimental import pallas as pl
from jax.experimental.pallas import tpu as pltpu
from jax.sharding import PartitionSpec as P

COLUMN_ORDER = (3, 1, 2, 0)
SMALL = pltpu.CompilerParams(vmem_limit_bytes=4 * 1024 * 1024)


def send_kernel(
    cls_hbm,
    tid_hbm,
    pair_hbm,
    dims_hbm,
    coef_hbm,
    wave_hbm,
    left_hbm,
    right_hbm,
    lead_ref,
    rest_ref,
    half_ref,
    cls,
    tid,
    pair,
    dims,
    coef,
    wave,
    left,
    right,
    scalar_sems,
    wave_sem,
    left_sems,
    right_sems,
):
    width = wave.shape[0]
    terms = left.shape[0]
    strip = width // 4
    unit = width // 8
    sec = lax.axis_index("sec")
    mpo = lax.axis_index("mpo")

    scalars = [
        pltpu.make_async_copy(src, dst, scalar_sems.at[n])
        for n, (src, dst) in enumerate(
            ((cls_hbm, cls), (tid_hbm, tid), (pair_hbm, pair), (dims_hbm, dims), (coef_hbm, coef))
        )
    ]
    wave_copy = pltpu.make_async_copy(wave_hbm.at[0], wave, wave_sem)
    wave_copy.start()
    for copy in scalars:
        copy.start()

    def fetch(j, carry):
        for q in range(4):
            src = pl.multiple_of((sec ^ q) * strip, strip)
            pltpu.make_async_copy(
                left_hbm.at[0, j, pl.ds(src, strip)],
                left.at[j, pl.ds(q * strip, strip)],
                left_sems.at[j],
            ).start()
        for p, r in enumerate(COLUMN_ORDER[:2]):
            src = pl.multiple_of((mpo ^ r) * strip, strip)
            pltpu.make_async_copy(
                right_hbm.at[0, j, pl.ds(src, strip)],
                right.at[j, pl.ds(p * strip, strip)],
                right_sems.at[j],
            ).start(priority=1)
        return carry

    lax.fori_loop(0, terms, fetch, 0)
    clear(lead_ref, rest_ref)
    for copy in scalars:
        copy.wait()
    wave_copy.wait()
    row_limit = dims[0, sec] * unit
    col_limit = dims[1, sec] * unit

    def mask(i, carry):
        base = pl.multiple_of(i * 64, 64)
        row_pos = base + lax.broadcasted_iota(jnp.int32, (64, width), 0)
        col_pos = lax.broadcasted_iota(jnp.int32, (64, width), 1)
        inside = (row_pos < row_limit) & (col_pos < col_limit)
        band = wave[pl.ds(base, 64), :].astype(jnp.float32)
        wave[pl.ds(base, 64), :] = jnp.where(inside, band, 0.0).astype(jnp.bfloat16)
        return carry

    lax.fori_loop(0, width // 64, mask, 0)
    for j in range(terms):
        pltpu.make_async_copy(left_hbm.at[0, j], left.at[j], left_sems.at[j]).wait()
        half = jnp.dot(left[j], wave[...], preferred_element_type=jnp.float32)
        half = half.astype(jnp.bfloat16)
        half_ref[j] = half
        pltpu.make_async_copy(
            right_hbm.at[0, j, pl.ds(0, 2 * strip)], right.at[j], right_sems.at[j]
        ).wait()
        spread(lead_ref, rest_ref, half, right[j], pair[sec, cls[0, j]], coef[tid[0, j]])


def keep_kernel(
    cls_hbm,
    tid_hbm,
    pair_hbm,
    dims_hbm,
    coef_hbm,
    right_hbm,
    half_ref,
    lead_ref,
    rest_ref,
    mask_ref,
    cls,
    tid,
    pair,
    dims,
    coef,
    right,
    scalar_sems,
    right_sems,
):
    terms, width, _ = half_ref.shape
    targets, strip, _ = mask_ref.shape
    unit = width // 8
    sec = lax.axis_index("sec")
    mpo = lax.axis_index("mpo")
    scalars = [
        pltpu.make_async_copy(src, dst, scalar_sems.at[n])
        for n, (src, dst) in enumerate(
            ((cls_hbm, cls), (tid_hbm, tid), (pair_hbm, pair), (dims_hbm, dims), (coef_hbm, coef))
        )
    ]
    for copy in scalars:
        copy.start()

    def fetch(j, carry):
        for p, r in enumerate(COLUMN_ORDER[2:]):
            src = pl.multiple_of((mpo ^ r) * strip, strip)
            pltpu.make_async_copy(
                right_hbm.at[0, j, pl.ds(src, strip)],
                right.at[j, pl.ds(p * strip, strip)],
                right_sems.at[j],
            ).start(priority=p)
        return carry

    lax.fori_loop(0, terms, fetch, 0)
    clear(lead_ref, rest_ref)
    for copy in scalars:
        copy.wait()
    lane = mpo * strip + lax.broadcasted_iota(jnp.int32, (strip, strip), 1)
    line = sec * strip + lax.broadcasted_iota(jnp.int32, (strip, strip), 0)

    def target_mask(t, carry):
        inside = (line < dims[0, t] * unit) & (lane < dims[1, t] * unit)
        mask_ref[t] = jnp.where(inside, 1.0, 0.0).astype(jnp.bfloat16)
        return carry

    lax.fori_loop(0, targets, target_mask, 0)
    for j in range(terms):
        pltpu.make_async_copy(
            right_hbm.at[0, j, pl.ds(0, 2 * strip)], right.at[j], right_sems.at[j]
        ).wait()
        spread(lead_ref, rest_ref, half_ref[j], right[j], pair[sec, cls[0, j]], coef[tid[0, j]])


def clear(*refs):
    def one(t, carry):
        for ref in refs:
            ref[t] = jnp.zeros(ref.shape[1:], ref.dtype)
        return carry

    lax.fori_loop(0, refs[0].shape[0], one, 0)


def spread(lead, rest, half, right, t, weight):
    contrib = lax.dot_general(
        half, right, (((1,), (1,)), ((), ())), preferred_element_type=jnp.float32
    )
    strip = contrib.shape[1] // 2
    a_rows = (rest.shape[1] - 2 * strip) // 2
    b_rows = strip - a_rows
    soon = (2 * a_rows, 2 * a_rows + strip + 2 * b_rows)
    for q in range(4):
        for n in range(2):
            value = weight * contrib[q * strip : (q + 1) * strip, n * strip : (n + 1) * strip]
            if q == 0:
                put(rest, t, n * strip, value)
            elif q == 1:
                put(lead, t, soon[n], value)
            else:
                if n == 0:
                    put(lead, t, (q - 2) * a_rows, value[:a_rows])
                else:
                    put(rest, t, 2 * strip + (q - 2) * a_rows, value[:a_rows])
                put(lead, t, soon[n] + strip + (q - 2) * b_rows, value[a_rows:])


def put(ref, t, row, value):
    at = slice(row, row + value.shape[0])
    ref[t, at, :] = (ref[t, at, :].astype(jnp.float32) + value).astype(jnp.bfloat16)


def lead_kernel(keep_ref, recv_ref, rest_in, rest_out, far_ref, one_far, one_near, *own_refs):
    del rest_in, rest_out
    row = far_ref.shape[1]
    far_ref[...] = add(keep_ref[:, :row, :], recv_ref[:, :row, :])
    for n, one_ref in enumerate((one_far, one_near)):
        at = slice(row, row + one_ref.shape[1])
        one_ref[...] = add(keep_ref[:, at, :], recv_ref[:, at, :])
        row += one_ref.shape[1]
        for own_ref in own_refs:
            at = slice(row, row + own_ref.shape[2])
            own_ref[n] = add(keep_ref[:, at, :], recv_ref[:, at, :])
            row += own_ref.shape[2]


def own_kernel(keep_ref, recv_ref, cross_ref, later_in, later_out, *own_refs):
    del later_in, later_out
    rows = own_refs[0].shape[1]
    row = keep_ref.shape[1] - 2 * rows
    for n, own_ref in enumerate(own_refs):
        at = slice(row + n * rows, row + (n + 1) * rows)
        own_ref[...] = add(
            keep_ref[:, at, :], recv_ref[:, at, :], cross_ref[:, n * rows : (n + 1) * rows, :]
        )


def here_kernel(keep_ref, recv_ref, one_ref, two_ref, three_ref, after_ref, far_ref, near_ref):
    del after_ref
    strip = far_ref.shape[1]
    a_rows = strip - two_ref.shape[2]
    for n, out_ref in enumerate((far_ref, near_ref)):
        for first, last in ((0, a_rows), (a_rows, strip)):
            at = slice(n * strip + first, n * strip + last)
            parts = [keep_ref[:, at, :], recv_ref[:, at, :]]
            if n == 0:
                parts += [one_ref[:, first:last, :]]
            if first:
                parts += [two_ref[n], three_ref[n]]
            out_ref[:, first:last, :] = total(*parts).astype(out_ref.dtype)


def far_sum_kernel(two_ref, three_ref, sum_ref):
    sum_ref[...] = total(two_ref[...], three_ref[...])


def final_kernel(mask_ref, near_ref, one_ref, cross_ref, sum_ref, out_ref):
    a_rows, strip = sum_ref.shape[1], out_ref.shape[1]
    for first, last in ((0, a_rows), (a_rows, strip)):
        parts = [ref[:, first:last, :] for ref in (near_ref, one_ref, cross_ref)]
        if not first:
            parts += [sum_ref[...]]
        inside = mask_ref[:, first:last, :].astype(jnp.float32) > 0.0
        out_ref[:, first:last, :] = jnp.where(inside, total(*parts), 0.0).astype(jnp.bfloat16)


def total(*arrays):
    result = arrays[0].astype(jnp.float32)
    for array in arrays[1:]:
        result = result + array.astype(jnp.float32)
    return result


def add(*arrays):
    return total(*arrays).astype(jnp.bfloat16)


def swap(array, axis, mask):
    return lax.ppermute(array, axis, [(i, i ^ mask) for i in range(lax.axis_size(axis))])


def by_targets(
    wave_blocks, left_env, right_env, term_class, term_id, block_dims, pair_table, mpo_coef
):
    width = wave_blocks.shape[1]
    terms = left_env.shape[1]
    targets = block_dims.shape[0]
    strip = width // 4
    a_rows = strip * 3 // 4
    b_rows = strip - a_rows
    vmem = pl.BlockSpec(memory_space=pltpu.VMEM)
    hbm = pl.BlockSpec(memory_space=pltpu.HBM)

    def like(*shape):
        return jax.ShapeDtypeStruct(shape + (strip,), jnp.bfloat16)

    def call(kernel, out_shape, *args, aliases={}, span=0.1):
        return pl.pallas_call(
            kernel,
            out_shape=out_shape,
            in_specs=[vmem] * len(args),
            out_specs=jax.tree.map(lambda _: vmem, out_shape),
            input_output_aliases=aliases,
            cost_estimate=pl.CostEstimate(
                flops=round(span * 1e9), bytes_accessed=0, transcendentals=0
            ),
            compiler_params=SMALL,
            name=kernel.__name__,
        )(*args)

    scalars = (term_class, term_id, pair_table, block_dims.T, mpo_coef)
    operands = [
        pltpu.with_memory_space_constraint(x, pltpu.HBM)
        for x in (*scalars, wave_blocks, left_env, right_env)
    ]
    lead_shape = like(targets, 2 * a_rows + 2 * (strip + 2 * b_rows))
    rest_shape = like(targets, 2 * strip + 2 * a_rows)
    scalar_room = [pltpu.SMEM(scalar.shape, scalar.dtype) for scalar in scalars]
    limit = pltpu.CompilerParams(vmem_limit_bytes=16 * 1024 * 1024)
    half_shape = jax.ShapeDtypeStruct((terms, width, width), jnp.bfloat16)
    right_room = pltpu.VMEM((terms, 2 * strip, width), jnp.bfloat16)
    lead_send, rest_send, half = pl.pallas_call(
        send_kernel,
        out_shape=[lead_shape, rest_shape, half_shape],
        in_specs=[hbm] * 8,
        out_specs=[vmem] * 3,
        scratch_shapes=scalar_room
        + [
            pltpu.VMEM((width, width), jnp.bfloat16),
            pltpu.VMEM((terms, width, width), jnp.bfloat16),
            right_room,
            pltpu.SemaphoreType.DMA((len(scalars),)),
            pltpu.SemaphoreType.DMA,
            pltpu.SemaphoreType.DMA((terms,)),
            pltpu.SemaphoreType.DMA((terms,)),
        ],
        compiler_params=limit,
        cost_estimate=pl.CostEstimate(
            flops=3 * terms * width**3, bytes_accessed=4 * 1024 * 1024, transcendentals=0
        ),
        name="send_kernel",
    )(*operands)
    lead_keep, rest_keep, mask = pl.pallas_call(
        keep_kernel,
        out_shape=[lead_shape, rest_shape, like(targets, strip)],
        in_specs=[hbm] * (len(scalars) + 1) + [vmem],
        out_specs=[vmem] * 3,
        scratch_shapes=scalar_room
        + [
            right_room,
            pltpu.SemaphoreType.DMA((len(scalars),)),
            pltpu.SemaphoreType.DMA((terms,)),
        ],
        compiler_params=limit,
        cost_estimate=pl.CostEstimate(
            flops=3 * terms * width**3, bytes_accessed=0, transcendentals=0
        ),
        name="keep_kernel",
    )(*operands[: len(scalars)], operands[-1], half)
    lead_recv = swap(lead_send, "mpo", 1)
    part = like(2, targets, b_rows)
    rest_send, far, one, one_near, two, three = call(
        lead_kernel,
        [rest_shape, like(targets, 2 * a_rows)] + [like(targets, strip)] * 2 + [part] * 2,
        lead_keep,
        lead_recv,
        rest_send,
        aliases={2: 0},
        span=3,
    )
    cross = swap(far, "mpo", 2)
    one, two, three = [swap(x, "sec", q) for x, q in ((one, 1), (two, 2), (three, 3))]
    rest_recv = swap(rest_send, "mpo", 1)
    one_near, *own = call(
        own_kernel,
        [like(targets, strip)] + [like(targets, a_rows)] * 2,
        rest_keep,
        rest_recv,
        cross,
        one_near,
        aliases={3: 0},
        span=3,
    )
    near = jax.ShapeDtypeStruct((targets, strip, strip), jnp.float32)
    here, near = call(
        here_kernel,
        [like(targets, strip), near],
        rest_keep,
        rest_recv,
        one,
        two,
        three,
        own[0],
        span=3,
    )
    own = [swap(array, "sec", q) for array, q in zip(own, (2, 3))]
    one_near = swap(one_near, "sec", 1)
    here = swap(here, "mpo", 2)
    far_sum = jax.ShapeDtypeStruct((targets, a_rows, strip), jnp.float32)
    far_sum = call(far_sum_kernel, far_sum, *own, span=3)
    return call(final_kernel, like(targets, strip), mask, near, one_near, here, far_sum)


def by_classes(
    wave_blocks, left_env, right_env, term_class, term_id, block_dims, pair_table, mpo_coef
):
    sec_count = lax.axis_size("sec")
    mpo_count = lax.axis_size("mpo")
    local_blocks = wave_blocks.shape[0]
    block_width = wave_blocks.shape[1]
    total_blocks = block_dims.shape[0]
    classes = pair_table.shape[1]
    tile_states = block_width // 8
    positions = jnp.arange(block_width)
    first = lax.axis_index("sec") * local_blocks
    own_dims = lax.dynamic_slice_in_dim(block_dims, first, local_blocks, 0)
    row_ok = positions[None, :] < own_dims[:, 0:1] * tile_states
    col_ok = positions[None, :] < own_dims[:, 1:2] * tile_states
    masked = jnp.where(
        row_ok[:, :, None] & col_ok[:, None, :], wave_blocks, jnp.zeros_like(wave_blocks)
    )
    left_part = jnp.einsum(
        "bjxy,byz->bjxz", left_env, masked, preferred_element_type=jnp.float32
    ).astype(jnp.bfloat16)
    contrib = jnp.einsum(
        "bjxz,bjwz->bjxw", left_part, right_env, preferred_element_type=jnp.float32
    )
    weights = jnp.sum(
        jnp.where(
            term_id[:, :, None] == jnp.arange(mpo_coef.shape[0])[None, None, :],
            mpo_coef[None, None, :],
            0.0,
        ),
        axis=-1,
    )
    picks = (term_class[:, :, None] == jnp.arange(classes)[None, None, :]).astype(
        jnp.float32
    ) * weights[:, :, None]
    grouped = jnp.einsum("bjc,bjxw->bcxw", picks, contrib, precision=lax.Precision.HIGHEST).astype(
        jnp.bfloat16
    )
    targets = pair_table.reshape(-1)
    routing = targets[None, :] == jnp.arange(total_blocks)[:, None]
    strip_rows = block_width // sec_count
    strip_cols = block_width // mpo_count
    outgoing = grouped.reshape(local_blocks * classes, block_width, block_width)
    arrived = lax.all_to_all(
        lax.all_to_all(outgoing, "sec", split_axis=1, concat_axis=0, tiled=True),
        "mpo",
        split_axis=2,
        concat_axis=0,
        tiled=True,
    )
    arrived = arrived.reshape(mpo_count, total_blocks * classes, strip_rows, strip_cols)
    summed = jnp.einsum(
        "tk,mkrw->trw", routing.astype(jnp.bfloat16), arrived, preferred_element_type=jnp.float32
    )
    row_index = lax.axis_index("sec") * strip_rows + jnp.arange(strip_rows)
    col_index = lax.axis_index("mpo") * strip_cols + jnp.arange(strip_cols)
    rows_in = row_index[None, :] < block_dims[:, 0:1] * tile_states
    cols_in = col_index[None, :] < block_dims[:, 1:2] * tile_states
    inside = rows_in[:, :, None] & cols_in[:, None, :]
    return jnp.where(inside, summed, 0.0).astype(jnp.bfloat16)


def solution(mesh):
    placed = (
        P(("grp", "sec"), None, None),
        P(("grp", "sec"), "mpo", None, None),
        P(("grp", "sec"), "mpo", None, None),
        P(("grp", "sec"), "mpo"),
        P(("grp", "sec"), "mpo"),
        P("grp", None),
        P("grp", None),
        P(),
    )

    def on_device(*arrays):
        wave_blocks, block_dims = arrays[0], arrays[5]
        small = wave_blocks.shape[0] == 1 and block_dims.shape[0] == 4
        if small and mesh.shape["sec"] == 4 and mesh.shape["mpo"] == 4:
            return by_targets(*arrays)
        return by_classes(*arrays)

    return jax.shard_map(
        on_device, mesh=mesh, in_specs=placed, out_specs=P("grp", "sec", "mpo"), check_vma=False
    )
```

```python
import functools

import jax
import jax.numpy as jnp
from jax import lax
from jax.experimental import pallas as pl
from jax.experimental.pallas import tpu as pltpu
from jax.sharding import PartitionSpec as P

COLUMN_ORDER = (3, 1, 2, 0)
SMALL = pltpu.CompilerParams(vmem_limit_bytes=4 * 1024 * 1024)


def send_kernel(
    cls_hbm,
    tid_hbm,
    pair_hbm,
    dims_hbm,
    coef_hbm,
    wave_hbm,
    left_hbm,
    right_hbm,
    lead_ref,
    rest_ref,
    half_ref,
    keep_right,
    cls,
    tid,
    pair,
    dims,
    coef,
    wave,
    left,
    right,
    scalar_sems,
    wave_sem,
    left_sems,
    right_sems,
    keep_sem,
):
    width = wave.shape[0]
    terms = left.shape[0]
    strip = width // 4
    unit = width // 8
    sec = lax.axis_index("sec")
    mpo = lax.axis_index("mpo")

    scalars = [
        pltpu.make_async_copy(src, dst, scalar_sems.at[n])
        for n, (src, dst) in enumerate(
            ((cls_hbm, cls), (tid_hbm, tid), (pair_hbm, pair), (dims_hbm, dims), (coef_hbm, coef))
        )
    ]
    wave_copy = pltpu.make_async_copy(wave_hbm.at[0], wave, wave_sem)
    wave_copy.start()
    for copy in scalars:
        copy.start()

    def fetch(j, carry):
        for q in range(4):
            src = pl.multiple_of((sec ^ q) * strip, strip)
            pltpu.make_async_copy(
                left_hbm.at[0, j, pl.ds(src, strip)],
                left.at[j, pl.ds(q * strip, strip)],
                left_sems.at[j],
            ).start()
        for p, r in enumerate(COLUMN_ORDER[:2]):
            src = pl.multiple_of((mpo ^ r) * strip, strip)
            pltpu.make_async_copy(
                right_hbm.at[0, j, pl.ds(src, strip)],
                right.at[j, pl.ds(p * strip, strip)],
                right_sems.at[j],
            ).start()
        return carry

    def fetch_keep(j, carry):
        for p, r in enumerate(COLUMN_ORDER[2:]):
            src = pl.multiple_of((mpo ^ r) * strip, strip)
            pltpu.make_async_copy(
                right_hbm.at[0, j, pl.ds(src, strip)],
                keep_right.at[j, pl.ds(p * strip, strip)],
                keep_sem,
            ).start()
        return carry

    lax.fori_loop(0, terms, fetch, 0)
    lax.fori_loop(0, terms, fetch_keep, 0)
    clear(lead_ref, rest_ref)
    for copy in scalars:
        copy.wait()
    wave_copy.wait()
    row_limit = dims[0, sec] * unit
    col_limit = dims[1, sec] * unit

    def mask(i, carry):
        base = pl.multiple_of(i * 64, 64)
        row_pos = base + lax.broadcasted_iota(jnp.int32, (64, width), 0)
        col_pos = lax.broadcasted_iota(jnp.int32, (64, width), 1)
        inside = (row_pos < row_limit) & (col_pos < col_limit)
        band = wave[pl.ds(base, 64), :].astype(jnp.float32)
        wave[pl.ds(base, 64), :] = jnp.where(inside, band, 0.0).astype(jnp.bfloat16)
        return carry

    lax.fori_loop(0, width // 64, mask, 0)
    for j in range(terms):
        pltpu.make_async_copy(left_hbm.at[0, j], left.at[j], left_sems.at[j]).wait()
        half = jnp.dot(left[j], wave[...], preferred_element_type=jnp.float32)
        half = half.astype(jnp.bfloat16)
        half_ref[j] = half
        pltpu.make_async_copy(
            right_hbm.at[0, j, pl.ds(0, 2 * strip)], right.at[j], right_sems.at[j]
        ).wait()
        spread(lead_ref, rest_ref, half, right[j], pair[sec, cls[0, j]], coef[tid[0, j]])
    pltpu.make_async_copy(
        right_hbm.at[0, pl.ds(0, terms), pl.ds(0, 2 * strip)], keep_right, keep_sem
    ).wait()


def keep_kernel(
    cls_hbm,
    tid_hbm,
    pair_hbm,
    dims_hbm,
    coef_hbm,
    half_ref,
    right_ref,
    lead_ref,
    rest_ref,
    mask_ref,
    cls,
    tid,
    pair,
    dims,
    coef,
    scalar_sems,
):
    terms, width, _ = half_ref.shape
    targets, strip, _ = mask_ref.shape
    unit = width // 8
    sec = lax.axis_index("sec")
    mpo = lax.axis_index("mpo")
    scalars = [
        pltpu.make_async_copy(src, dst, scalar_sems.at[n])
        for n, (src, dst) in enumerate(
            ((cls_hbm, cls), (tid_hbm, tid), (pair_hbm, pair), (dims_hbm, dims), (coef_hbm, coef))
        )
    ]
    for copy in scalars:
        copy.start()
    clear(lead_ref, rest_ref)
    for copy in scalars:
        copy.wait()
    for j in range(terms):
        spread(
            lead_ref, rest_ref, half_ref[j], right_ref[j], pair[sec, cls[0, j]], coef[tid[0, j]]
        )
    lane = mpo * strip + lax.broadcasted_iota(jnp.int32, (strip, strip), 1)
    line = sec * strip + lax.broadcasted_iota(jnp.int32, (strip, strip), 0)

    def target_mask(t, carry):
        inside = (line < dims[0, t] * unit) & (lane < dims[1, t] * unit)
        mask_ref[t] = jnp.where(inside, 1.0, 0.0).astype(jnp.bfloat16)
        return carry

    lax.fori_loop(0, targets, target_mask, 0)


def clear(*refs):
    def one(t, carry):
        for ref in refs:
            ref[t] = jnp.zeros(ref.shape[1:], ref.dtype)
        return carry

    lax.fori_loop(0, refs[0].shape[0], one, 0)


def spread(lead, rest, half, right, t, weight):
    contrib = lax.dot_general(
        half, right, (((1,), (1,)), ((), ())), preferred_element_type=jnp.float32
    )
    strip = contrib.shape[1] // 2
    a_rows = (rest.shape[1] - 2 * strip) // 2
    b_rows = strip - a_rows
    soon = (2 * a_rows, 2 * a_rows + strip + 2 * b_rows)
    for q in range(4):
        for n in range(2):
            value = weight * contrib[q * strip : (q + 1) * strip, n * strip : (n + 1) * strip]
            if q == 0:
                put(rest, t, n * strip, value)
            elif q == 1:
                put(lead, t, soon[n], value)
            else:
                if n == 0:
                    put(lead, t, (q - 2) * a_rows, value[:a_rows])
                else:
                    put(rest, t, 2 * strip + (q - 2) * a_rows, value[:a_rows])
                put(lead, t, soon[n] + strip + (q - 2) * b_rows, value[a_rows:])


def put(ref, t, row, value):
    at = slice(row, row + value.shape[0])
    ref[t, at, :] = (ref[t, at, :].astype(jnp.float32) + value).astype(jnp.bfloat16)


def lead_kernel(keep_ref, recv_ref, rest_in, rest_out, far_ref, one_far, one_near, *own_refs):
    del rest_in, rest_out
    row = far_ref.shape[1]
    far_ref[...] = add(keep_ref[:, :row, :], recv_ref[:, :row, :])
    for n, one_ref in enumerate((one_far, one_near)):
        at = slice(row, row + one_ref.shape[1])
        one_ref[...] = add(keep_ref[:, at, :], recv_ref[:, at, :])
        row += one_ref.shape[1]
        for own_ref in own_refs:
            at = slice(row, row + own_ref.shape[2])
            own_ref[n] = add(keep_ref[:, at, :], recv_ref[:, at, :])
            row += own_ref.shape[2]


def own_kernel(keep_ref, recv_ref, cross_ref, later_in, later_out, *own_refs):
    del later_in, later_out
    rows = own_refs[0].shape[1]
    row = keep_ref.shape[1] - 2 * rows
    for n, own_ref in enumerate(own_refs):
        at = slice(row + n * rows, row + (n + 1) * rows)
        own_ref[...] = add(
            keep_ref[:, at, :], recv_ref[:, at, :], cross_ref[:, n * rows : (n + 1) * rows, :]
        )


def here_kernel(keep_ref, recv_ref, one_ref, two_ref, three_ref, after_ref, far_ref, near_ref):
    del after_ref
    strip = far_ref.shape[1]
    a_rows = strip - two_ref.shape[2]
    for n, out_ref in enumerate((far_ref, near_ref)):
        for first, last in ((0, a_rows), (a_rows, strip)):
            at = slice(n * strip + first, n * strip + last)
            parts = [keep_ref[:, at, :], recv_ref[:, at, :]]
            if n == 0:
                parts += [one_ref[:, first:last, :]]
            if first:
                parts += [two_ref[n], three_ref[n]]
            out_ref[:, first:last, :] = total(*parts).astype(out_ref.dtype)


def far_sum_kernel(two_ref, three_ref, sum_ref):
    sum_ref[...] = total(two_ref[...], three_ref[...])


def final_kernel(mask_ref, near_ref, one_ref, cross_ref, sum_ref, out_ref):
    a_rows, strip = sum_ref.shape[1], out_ref.shape[1]
    for first, last in ((0, a_rows), (a_rows, strip)):
        parts = [ref[:, first:last, :] for ref in (near_ref, one_ref, cross_ref)]
        if not first:
            parts += [sum_ref[...]]
        inside = mask_ref[:, first:last, :].astype(jnp.float32) > 0.0
        out_ref[:, first:last, :] = jnp.where(inside, total(*parts), 0.0).astype(jnp.bfloat16)


def total(*arrays):
    result = arrays[0].astype(jnp.float32)
    for array in arrays[1:]:
        result = result + array.astype(jnp.float32)
    return result


def add(*arrays):
    return total(*arrays).astype(jnp.bfloat16)


def swap(array, axis, mask):
    return lax.ppermute(array, axis, [(i, i ^ mask) for i in range(lax.axis_size(axis))])


def by_targets(
    wave_blocks, left_env, right_env, term_class, term_id, block_dims, pair_table, mpo_coef
):
    width = wave_blocks.shape[1]
    terms = left_env.shape[1]
    targets = block_dims.shape[0]
    strip = width // 4
    a_rows = strip * 3 // 4
    b_rows = strip - a_rows
    vmem = pl.BlockSpec(memory_space=pltpu.VMEM)
    hbm = pl.BlockSpec(memory_space=pltpu.HBM)

    def like(*shape):
        return jax.ShapeDtypeStruct(shape + (strip,), jnp.bfloat16)

    def call(kernel, out_shape, *args, aliases={}, span=0.1):
        return pl.pallas_call(
            kernel,
            out_shape=out_shape,
            in_specs=[vmem] * len(args),
            out_specs=jax.tree.map(lambda _: vmem, out_shape),
            input_output_aliases=aliases,
            cost_estimate=pl.CostEstimate(
                flops=round(span * 1e9), bytes_accessed=0, transcendentals=0
            ),
            compiler_params=SMALL,
            name=kernel.__name__,
        )(*args)

    scalars = (term_class, term_id, pair_table, block_dims.T, mpo_coef)
    operands = [
        pltpu.with_memory_space_constraint(x, pltpu.HBM)
        for x in (*scalars, wave_blocks, left_env, right_env)
    ]
    lead_shape = like(targets, 2 * a_rows + 2 * (strip + 2 * b_rows))
    rest_shape = like(targets, 2 * strip + 2 * a_rows)
    scalar_room = [pltpu.SMEM(scalar.shape, scalar.dtype) for scalar in scalars]
    limit = pltpu.CompilerParams(vmem_limit_bytes=16 * 1024 * 1024)
    half_shape = jax.ShapeDtypeStruct((terms, width, width), jnp.bfloat16)
    right_shape = jax.ShapeDtypeStruct((terms, 2 * strip, width), jnp.bfloat16)
    lead_send, rest_send, half, keep_right = pl.pallas_call(
        send_kernel,
        out_shape=[lead_shape, rest_shape, half_shape, right_shape],
        in_specs=[hbm] * 8,
        out_specs=[vmem] * 4,
        scratch_shapes=scalar_room
        + [
            pltpu.VMEM((width, width), jnp.bfloat16),
            pltpu.VMEM((terms, width, width), jnp.bfloat16),
            pltpu.VMEM((terms, 2 * strip, width), jnp.bfloat16),
            pltpu.SemaphoreType.DMA((len(scalars),)),
            pltpu.SemaphoreType.DMA,
            pltpu.SemaphoreType.DMA((terms,)),
            pltpu.SemaphoreType.DMA((terms,)),
            pltpu.SemaphoreType.DMA,
        ],
        compiler_params=limit,
        cost_estimate=pl.CostEstimate(
            flops=3 * terms * width**3, bytes_accessed=4 * 1024 * 1024, transcendentals=0
        ),
        name="send_kernel",
    )(*operands)
    lead_keep, rest_keep, mask = pl.pallas_call(
        keep_kernel,
        out_shape=[lead_shape, rest_shape, like(targets, strip)],
        in_specs=[hbm] * len(scalars) + [vmem] * 2,
        out_specs=[vmem] * 3,
        scratch_shapes=scalar_room + [pltpu.SemaphoreType.DMA((len(scalars),))],
        compiler_params=limit,
        cost_estimate=pl.CostEstimate(
            flops=3 * terms * width**3, bytes_accessed=0, transcendentals=0
        ),
        name="keep_kernel",
    )(*operands[: len(scalars)], half, keep_right)
    lead_recv = swap(lead_send, "mpo", 1)
    part = like(2, targets, b_rows)
    rest_send, far, one, one_near, two, three = call(
        lead_kernel,
        [rest_shape, like(targets, 2 * a_rows)] + [like(targets, strip)] * 2 + [part] * 2,
        lead_keep,
        lead_recv,
        rest_send,
        aliases={2: 0},
        span=3,
    )
    cross = swap(far, "mpo", 2)
    one, two, three = [swap(x, "sec", q) for x, q in ((one, 1), (two, 2), (three, 3))]
    rest_recv = swap(rest_send, "mpo", 1)
    one_near, *own = call(
        own_kernel,
        [like(targets, strip)] + [like(targets, a_rows)] * 2,
        rest_keep,
        rest_recv,
        cross,
        one_near,
        aliases={3: 0},
        span=3,
    )
    near = jax.ShapeDtypeStruct((targets, strip, strip), jnp.float32)
    here, near = call(
        here_kernel,
        [like(targets, strip), near],
        rest_keep,
        rest_recv,
        one,
        two,
        three,
        own[0],
        span=3,
    )
    own = [swap(array, "sec", q) for array, q in zip(own, (2, 3))]
    one_near = swap(one_near, "sec", 1)
    here = swap(here, "mpo", 2)
    far_sum = jax.ShapeDtypeStruct((targets, a_rows, strip), jnp.float32)
    far_sum = call(far_sum_kernel, far_sum, *own, span=3)
    return call(final_kernel, like(targets, strip), mask, near, one_near, here, far_sum)


def by_classes(
    wave_blocks, left_env, right_env, term_class, term_id, block_dims, pair_table, mpo_coef
):
    sec_count = lax.axis_size("sec")
    mpo_count = lax.axis_size("mpo")
    local_blocks = wave_blocks.shape[0]
    block_width = wave_blocks.shape[1]
    total_blocks = block_dims.shape[0]
    classes = pair_table.shape[1]
    tile_states = block_width // 8
    positions = jnp.arange(block_width)
    first = lax.axis_index("sec") * local_blocks
    own_dims = lax.dynamic_slice_in_dim(block_dims, first, local_blocks, 0)
    row_ok = positions[None, :] < own_dims[:, 0:1] * tile_states
    col_ok = positions[None, :] < own_dims[:, 1:2] * tile_states
    masked = jnp.where(
        row_ok[:, :, None] & col_ok[:, None, :], wave_blocks, jnp.zeros_like(wave_blocks)
    )
    left_part = jnp.einsum(
        "bjxy,byz->bjxz", left_env, masked, preferred_element_type=jnp.float32
    ).astype(jnp.bfloat16)
    contrib = jnp.einsum(
        "bjxz,bjwz->bjxw", left_part, right_env, preferred_element_type=jnp.float32
    )
    weights = jnp.sum(
        jnp.where(
            term_id[:, :, None] == jnp.arange(mpo_coef.shape[0])[None, None, :],
            mpo_coef[None, None, :],
            0.0,
        ),
        axis=-1,
    )
    picks = (term_class[:, :, None] == jnp.arange(classes)[None, None, :]).astype(
        jnp.float32
    ) * weights[:, :, None]
    grouped = jnp.einsum("bjc,bjxw->bcxw", picks, contrib, precision=lax.Precision.HIGHEST).astype(
        jnp.bfloat16
    )
    targets = pair_table.reshape(-1)
    routing = targets[None, :] == jnp.arange(total_blocks)[:, None]
    strip_rows = block_width // sec_count
    strip_cols = block_width // mpo_count
    outgoing = grouped.reshape(local_blocks * classes, block_width, block_width)
    arrived = lax.all_to_all(
        lax.all_to_all(outgoing, "sec", split_axis=1, concat_axis=0, tiled=True),
        "mpo",
        split_axis=2,
        concat_axis=0,
        tiled=True,
    )
    arrived = arrived.reshape(mpo_count, total_blocks * classes, strip_rows, strip_cols)
    summed = jnp.einsum(
        "tk,mkrw->trw", routing.astype(jnp.bfloat16), arrived, preferred_element_type=jnp.float32
    )
    row_index = lax.axis_index("sec") * strip_rows + jnp.arange(strip_rows)
    col_index = lax.axis_index("mpo") * strip_cols + jnp.arange(strip_cols)
    rows_in = row_index[None, :] < block_dims[:, 0:1] * tile_states
    cols_in = col_index[None, :] < block_dims[:, 1:2] * tile_states
    inside = rows_in[:, :, None] & cols_in[:, None, :]
    return jnp.where(inside, summed, 0.0).astype(jnp.bfloat16)


def solution(mesh):
    placed = (
        P(("grp", "sec"), None, None),
        P(("grp", "sec"), "mpo", None, None),
        P(("grp", "sec"), "mpo", None, None),
        P(("grp", "sec"), "mpo"),
        P(("grp", "sec"), "mpo"),
        P("grp", None),
        P("grp", None),
        P(),
    )

    def on_device(*arrays):
        wave_blocks, block_dims = arrays[0], arrays[5]
        small = wave_blocks.shape[0] == 1 and block_dims.shape[0] == 4
        if small and mesh.shape["sec"] == 4 and mesh.shape["mpo"] == 4:
            return by_targets(*arrays)
        return by_classes(*arrays)

    return jax.shard_map(
        on_device, mesh=mesh, in_specs=placed, out_specs=P("grp", "sec", "mpo"), check_vma=False
    )
```

```python
import functools

import jax
import jax.numpy as jnp
from jax import lax
from jax.experimental import pallas as pl
from jax.experimental.pallas import tpu as pltpu
from jax.sharding import PartitionSpec as P

COLUMN_ORDER = (3, 1, 2, 0)
SMALL = pltpu.CompilerParams(vmem_limit_bytes=4 * 1024 * 1024)


def send_kernel(
    cls_hbm,
    tid_hbm,
    pair_hbm,
    dims_hbm,
    coef_hbm,
    wave_hbm,
    left_hbm,
    right_hbm,
    lead_ref,
    rest_ref,
    half_ref,
    keep_right,
    cls,
    tid,
    pair,
    dims,
    coef,
    wave,
    left,
    right,
    scalar_sems,
    wave_sem,
    left_sems,
    right_sems,
    keep_sem,
):
    width = wave.shape[0]
    terms = left.shape[0]
    strip = width // 4
    unit = width // 8
    sec = lax.axis_index("sec")
    mpo = lax.axis_index("mpo")

    scalars = [
        pltpu.make_async_copy(src, dst, scalar_sems.at[n])
        for n, (src, dst) in enumerate(
            ((cls_hbm, cls), (tid_hbm, tid), (pair_hbm, pair), (dims_hbm, dims), (coef_hbm, coef))
        )
    ]
    wave_copy = pltpu.make_async_copy(wave_hbm.at[0], wave, wave_sem)
    wave_copy.start()
    for copy in scalars:
        copy.start()

    def fetch(j, carry):
        for q in range(4):
            src = pl.multiple_of((sec ^ q) * strip, strip)
            pltpu.make_async_copy(
                left_hbm.at[0, j, pl.ds(src, strip)],
                left.at[j, pl.ds(q * strip, strip)],
                left_sems.at[j],
            ).start()
        for p, r in enumerate(COLUMN_ORDER[:2]):
            src = pl.multiple_of((mpo ^ r) * strip, strip)
            pltpu.make_async_copy(
                right_hbm.at[0, j, pl.ds(src, strip)],
                right.at[j, pl.ds(p * strip, strip)],
                right_sems.at[j],
            ).start()
        return carry

    def fetch_keep(j, carry):
        for p, r in enumerate(COLUMN_ORDER[2:]):
            src = pl.multiple_of((mpo ^ r) * strip, strip)
            pltpu.make_async_copy(
                right_hbm.at[0, j, pl.ds(src, strip)],
                keep_right.at[j, pl.ds(p * strip, strip)],
                keep_sem,
            ).start()
        return carry

    lax.fori_loop(0, terms, fetch, 0)
    lax.fori_loop(0, terms, fetch_keep, 0)
    clear(lead_ref, rest_ref)
    for copy in scalars:
        copy.wait()
    wave_copy.wait()
    row_limit = dims[0, sec] * unit
    col_limit = dims[1, sec] * unit

    def mask(i, carry):
        base = pl.multiple_of(i * 64, 64)
        row_pos = base + lax.broadcasted_iota(jnp.int32, (64, width), 0)
        col_pos = lax.broadcasted_iota(jnp.int32, (64, width), 1)
        inside = (row_pos < row_limit) & (col_pos < col_limit)
        band = wave[pl.ds(base, 64), :].astype(jnp.float32)
        wave[pl.ds(base, 64), :] = jnp.where(inside, band, 0.0).astype(jnp.bfloat16)
        return carry

    lax.fori_loop(0, width // 64, mask, 0)
    for j in range(terms):
        pltpu.make_async_copy(left_hbm.at[0, j], left.at[j], left_sems.at[j]).wait()
        half = jnp.dot(left[j], wave[...], preferred_element_type=jnp.float32)
        half = half.astype(jnp.bfloat16)
        half_ref[j] = half
        pltpu.make_async_copy(
            right_hbm.at[0, j, pl.ds(0, 2 * strip)], right.at[j], right_sems.at[j]
        ).wait()
        spread(lead_ref, rest_ref, half, right[j], pair[sec, cls[0, j]], coef[tid[0, j]])
    pltpu.make_async_copy(
        right_hbm.at[0, pl.ds(0, terms), pl.ds(0, 2 * strip)], keep_right, keep_sem
    ).wait()


def keep_kernel(
    cls_hbm,
    tid_hbm,
    pair_hbm,
    dims_hbm,
    coef_hbm,
    half_ref,
    right_ref,
    lead_ref,
    rest_ref,
    mask_ref,
    cls,
    tid,
    pair,
    dims,
    coef,
    scalar_sems,
):
    terms, width, _ = half_ref.shape
    targets, strip, _ = mask_ref.shape
    unit = width // 8
    sec = lax.axis_index("sec")
    mpo = lax.axis_index("mpo")
    scalars = [
        pltpu.make_async_copy(src, dst, scalar_sems.at[n])
        for n, (src, dst) in enumerate(
            ((cls_hbm, cls), (tid_hbm, tid), (pair_hbm, pair), (dims_hbm, dims), (coef_hbm, coef))
        )
    ]
    for copy in scalars:
        copy.start()
    clear(lead_ref, rest_ref)
    for copy in scalars:
        copy.wait()
    for j in range(terms):
        spread(
            lead_ref, rest_ref, half_ref[j], right_ref[j], pair[sec, cls[0, j]], coef[tid[0, j]]
        )
    lane = mpo * strip + lax.broadcasted_iota(jnp.int32, (strip, strip), 1)
    line = sec * strip + lax.broadcasted_iota(jnp.int32, (strip, strip), 0)

    def target_mask(t, carry):
        inside = (line < dims[0, t] * unit) & (lane < dims[1, t] * unit)
        mask_ref[t] = jnp.where(inside, 1.0, 0.0).astype(jnp.bfloat16)
        return carry

    lax.fori_loop(0, targets, target_mask, 0)


def clear(*refs):
    def one(t, carry):
        for ref in refs:
            ref[t] = jnp.zeros(ref.shape[1:], ref.dtype)
        return carry

    lax.fori_loop(0, refs[0].shape[0], one, 0)


def spread(lead, rest, half, right, t, weight):
    contrib = lax.dot_general(
        half, right, (((1,), (1,)), ((), ())), preferred_element_type=jnp.float32
    )
    strip = contrib.shape[1] // 2
    a_rows = (rest.shape[1] - 2 * strip) // 2
    b_rows = strip - a_rows
    soon = (2 * a_rows, 2 * a_rows + strip + 2 * b_rows)
    for q in range(4):
        for n in range(2):
            value = weight * contrib[q * strip : (q + 1) * strip, n * strip : (n + 1) * strip]
            if q == 0:
                put(rest, t, n * strip, value)
            elif q == 1:
                put(lead, t, soon[n], value)
            else:
                if n == 0:
                    put(lead, t, (q - 2) * a_rows, value[:a_rows])
                else:
                    put(rest, t, 2 * strip + (q - 2) * a_rows, value[:a_rows])
                put(lead, t, soon[n] + strip + (q - 2) * b_rows, value[a_rows:])


def put(ref, t, row, value):
    at = slice(row, row + value.shape[0])
    ref[t, at, :] = (ref[t, at, :].astype(jnp.float32) + value).astype(jnp.bfloat16)


def lead_kernel(keep_ref, recv_ref, rest_in, rest_out, far_ref, one_far, one_near, *own_refs):
    del rest_in, rest_out
    row = far_ref.shape[1]
    far_ref[...] = add(keep_ref[:, :row, :], recv_ref[:, :row, :])
    for n, one_ref in enumerate((one_far, one_near)):
        at = slice(row, row + one_ref.shape[1])
        one_ref[...] = add(keep_ref[:, at, :], recv_ref[:, at, :])
        row += one_ref.shape[1]
        for own_ref in own_refs:
            at = slice(row, row + own_ref.shape[2])
            own_ref[n] = add(keep_ref[:, at, :], recv_ref[:, at, :])
            row += own_ref.shape[2]


def own_kernel(keep_ref, recv_ref, cross_ref, later_in, later_out, *own_refs):
    del later_in, later_out
    rows = own_refs[0].shape[1]
    row = keep_ref.shape[1] - 2 * rows
    for n, own_ref in enumerate(own_refs[::-1]):
        at = slice(row + n * rows, row + (n + 1) * rows)
        own_ref[...] = add(
            keep_ref[:, at, :], recv_ref[:, at, :], cross_ref[:, n * rows : (n + 1) * rows, :]
        )


def here_kernel(keep_ref, recv_ref, one_ref, two_ref, three_ref, after_ref, far_ref, near_ref):
    del after_ref
    strip = far_ref.shape[1]
    a_rows = strip - two_ref.shape[2]
    for n, out_ref in enumerate((far_ref, near_ref)):
        for first, last in ((0, a_rows), (a_rows, strip)):
            at = slice(n * strip + first, n * strip + last)
            parts = [keep_ref[:, at, :], recv_ref[:, at, :]]
            if n == 0:
                parts += [one_ref[:, first:last, :]]
            if first:
                parts += [two_ref[n], three_ref[n]]
            out_ref[:, first:last, :] = total(*parts).astype(out_ref.dtype)


def far_sum_kernel(two_ref, three_ref, sum_ref):
    sum_ref[...] = total(two_ref[...], three_ref[...])


def final_kernel(mask_ref, near_ref, one_ref, cross_ref, sum_ref, out_ref):
    a_rows, strip = sum_ref.shape[1], out_ref.shape[1]
    for first, last in ((0, a_rows), (a_rows, strip)):
        parts = [ref[:, first:last, :] for ref in (near_ref, one_ref, cross_ref)]
        if not first:
            parts += [sum_ref[...]]
        inside = mask_ref[:, first:last, :].astype(jnp.float32) > 0.0
        out_ref[:, first:last, :] = jnp.where(inside, total(*parts), 0.0).astype(jnp.bfloat16)


def total(*arrays):
    result = arrays[0].astype(jnp.float32)
    for array in arrays[1:]:
        result = result + array.astype(jnp.float32)
    return result


def add(*arrays):
    return total(*arrays).astype(jnp.bfloat16)


def swap(array, axis, mask):
    return lax.ppermute(array, axis, [(i, i ^ mask) for i in range(lax.axis_size(axis))])


def by_targets(
    wave_blocks, left_env, right_env, term_class, term_id, block_dims, pair_table, mpo_coef
):
    width = wave_blocks.shape[1]
    terms = left_env.shape[1]
    targets = block_dims.shape[0]
    strip = width // 4
    a_rows = strip * 3 // 4
    b_rows = strip - a_rows
    vmem = pl.BlockSpec(memory_space=pltpu.VMEM)
    hbm = pl.BlockSpec(memory_space=pltpu.HBM)

    def like(*shape):
        return jax.ShapeDtypeStruct(shape + (strip,), jnp.bfloat16)

    def call(kernel, out_shape, *args, aliases={}, span=0.1):
        return pl.pallas_call(
            kernel,
            out_shape=out_shape,
            in_specs=[vmem] * len(args),
            out_specs=jax.tree.map(lambda _: vmem, out_shape),
            input_output_aliases=aliases,
            cost_estimate=pl.CostEstimate(
                flops=round(span * 1e9), bytes_accessed=0, transcendentals=0
            ),
            compiler_params=SMALL,
            name=kernel.__name__,
        )(*args)

    scalars = (term_class, term_id, pair_table, block_dims.T, mpo_coef)
    operands = [
        pltpu.with_memory_space_constraint(x, pltpu.HBM)
        for x in (*scalars, wave_blocks, left_env, right_env)
    ]
    lead_shape = like(targets, 2 * a_rows + 2 * (strip + 2 * b_rows))
    rest_shape = like(targets, 2 * strip + 2 * a_rows)
    scalar_room = [pltpu.SMEM(scalar.shape, scalar.dtype) for scalar in scalars]
    limit = pltpu.CompilerParams(vmem_limit_bytes=16 * 1024 * 1024)
    half_shape = jax.ShapeDtypeStruct((terms, width, width), jnp.bfloat16)
    right_shape = jax.ShapeDtypeStruct((terms, 2 * strip, width), jnp.bfloat16)
    lead_send, rest_send, half, keep_right = pl.pallas_call(
        send_kernel,
        out_shape=[lead_shape, rest_shape, half_shape, right_shape],
        in_specs=[hbm] * 8,
        out_specs=[vmem] * 4,
        scratch_shapes=scalar_room
        + [
            pltpu.VMEM((width, width), jnp.bfloat16),
            pltpu.VMEM((terms, width, width), jnp.bfloat16),
            pltpu.VMEM((terms, 2 * strip, width), jnp.bfloat16),
            pltpu.SemaphoreType.DMA((len(scalars),)),
            pltpu.SemaphoreType.DMA,
            pltpu.SemaphoreType.DMA((terms,)),
            pltpu.SemaphoreType.DMA((terms,)),
            pltpu.SemaphoreType.DMA,
        ],
        compiler_params=limit,
        cost_estimate=pl.CostEstimate(
            flops=3 * terms * width**3, bytes_accessed=4 * 1024 * 1024, transcendentals=0
        ),
        name="send_kernel",
    )(*operands)
    lead_keep, rest_keep, mask = pl.pallas_call(
        keep_kernel,
        out_shape=[lead_shape, rest_shape, like(targets, strip)],
        in_specs=[hbm] * len(scalars) + [vmem] * 2,
        out_specs=[vmem] * 3,
        scratch_shapes=scalar_room + [pltpu.SemaphoreType.DMA((len(scalars),))],
        compiler_params=limit,
        cost_estimate=pl.CostEstimate(
            flops=3 * terms * width**3, bytes_accessed=0, transcendentals=0
        ),
        name="keep_kernel",
    )(*operands[: len(scalars)], half, keep_right)
    lead_recv = swap(lead_send, "mpo", 1)
    part = like(2, targets, b_rows)
    rest_send, far, one, one_near, two, three = call(
        lead_kernel,
        [rest_shape, like(targets, 2 * a_rows)] + [like(targets, strip)] * 2 + [part] * 2,
        lead_keep,
        lead_recv,
        rest_send,
        aliases={2: 0},
        span=3,
    )
    cross = swap(far, "mpo", 2)
    one, two, three = [swap(x, "sec", q) for x, q in ((one, 1), (two, 2), (three, 3))]
    rest_recv = swap(rest_send, "mpo", 1)
    one_near, *own = call(
        own_kernel,
        [like(targets, strip)] + [like(targets, a_rows)] * 2,
        rest_keep,
        rest_recv,
        cross,
        one_near,
        aliases={3: 0},
        span=3,
    )
    near = jax.ShapeDtypeStruct((targets, strip, strip), jnp.float32)
    here, near = call(
        here_kernel,
        [like(targets, strip), near],
        rest_keep,
        rest_recv,
        one,
        two,
        three,
        own[0],
        span=3,
    )
    own = [swap(array, "sec", q) for array, q in zip(own[::-1], (2, 3))]
    one_near = swap(one_near, "sec", 1)
    here = swap(here, "mpo", 2)
    far_sum = jax.ShapeDtypeStruct((targets, a_rows, strip), jnp.float32)
    far_sum = call(far_sum_kernel, far_sum, *own, span=3)
    return call(final_kernel, like(targets, strip), mask, near, one_near, here, far_sum)


def by_classes(
    wave_blocks, left_env, right_env, term_class, term_id, block_dims, pair_table, mpo_coef
):
    sec_count = lax.axis_size("sec")
    mpo_count = lax.axis_size("mpo")
    local_blocks = wave_blocks.shape[0]
    block_width = wave_blocks.shape[1]
    total_blocks = block_dims.shape[0]
    classes = pair_table.shape[1]
    tile_states = block_width // 8
    positions = jnp.arange(block_width)
    first = lax.axis_index("sec") * local_blocks
    own_dims = lax.dynamic_slice_in_dim(block_dims, first, local_blocks, 0)
    row_ok = positions[None, :] < own_dims[:, 0:1] * tile_states
    col_ok = positions[None, :] < own_dims[:, 1:2] * tile_states
    masked = jnp.where(
        row_ok[:, :, None] & col_ok[:, None, :], wave_blocks, jnp.zeros_like(wave_blocks)
    )
    left_part = jnp.einsum(
        "bjxy,byz->bjxz", left_env, masked, preferred_element_type=jnp.float32
    ).astype(jnp.bfloat16)
    contrib = jnp.einsum(
        "bjxz,bjwz->bjxw", left_part, right_env, preferred_element_type=jnp.float32
    )
    weights = jnp.sum(
        jnp.where(
            term_id[:, :, None] == jnp.arange(mpo_coef.shape[0])[None, None, :],
            mpo_coef[None, None, :],
            0.0,
        ),
        axis=-1,
    )
    picks = (term_class[:, :, None] == jnp.arange(classes)[None, None, :]).astype(
        jnp.float32
    ) * weights[:, :, None]
    grouped = jnp.einsum("bjc,bjxw->bcxw", picks, contrib, precision=lax.Precision.HIGHEST).astype(
        jnp.bfloat16
    )
    targets = pair_table.reshape(-1)
    routing = targets[None, :] == jnp.arange(total_blocks)[:, None]
    strip_rows = block_width // sec_count
    strip_cols = block_width // mpo_count
    outgoing = grouped.reshape(local_blocks * classes, block_width, block_width)
    arrived = lax.all_to_all(
        lax.all_to_all(outgoing, "sec", split_axis=1, concat_axis=0, tiled=True),
        "mpo",
        split_axis=2,
        concat_axis=0,
        tiled=True,
    )
    arrived = arrived.reshape(mpo_count, total_blocks * classes, strip_rows, strip_cols)
    summed = jnp.einsum(
        "tk,mkrw->trw", routing.astype(jnp.bfloat16), arrived, preferred_element_type=jnp.float32
    )
    row_index = lax.axis_index("sec") * strip_rows + jnp.arange(strip_rows)
    col_index = lax.axis_index("mpo") * strip_cols + jnp.arange(strip_cols)
    rows_in = row_index[None, :] < block_dims[:, 0:1] * tile_states
    cols_in = col_index[None, :] < block_dims[:, 1:2] * tile_states
    inside = rows_in[:, :, None] & cols_in[:, None, :]
    return jnp.where(inside, summed, 0.0).astype(jnp.bfloat16)


def solution(mesh):
    placed = (
        P(("grp", "sec"), None, None),
        P(("grp", "sec"), "mpo", None, None),
        P(("grp", "sec"), "mpo", None, None),
        P(("grp", "sec"), "mpo"),
        P(("grp", "sec"), "mpo"),
        P("grp", None),
        P("grp", None),
        P(),
    )

    def on_device(*arrays):
        wave_blocks, block_dims = arrays[0], arrays[5]
        small = wave_blocks.shape[0] == 1 and block_dims.shape[0] == 4
        if small and mesh.shape["sec"] == 4 and mesh.shape["mpo"] == 4:
            return by_targets(*arrays)
        return by_classes(*arrays)

    return jax.shard_map(
        on_device, mesh=mesh, in_specs=placed, out_specs=P("grp", "sec", "mpo"), check_vma=False
    )
```

```python
import functools

import jax
import jax.numpy as jnp
from jax import lax
from jax.experimental import pallas as pl
from jax.experimental.pallas import tpu as pltpu
from jax.sharding import PartitionSpec as P

COLUMN_ORDER = (3, 1, 2, 0)
SMALL = pltpu.CompilerParams(vmem_limit_bytes=4 * 1024 * 1024)


def send_kernel(
    cls_hbm,
    tid_hbm,
    pair_hbm,
    dims_hbm,
    coef_hbm,
    wave_hbm,
    left_hbm,
    right_hbm,
    lead_ref,
    rest_ref,
    half_ref,
    keep_right,
    cls,
    tid,
    pair,
    dims,
    coef,
    wave,
    left,
    right,
    scalar_sems,
    wave_sem,
    left_sems,
    right_sems,
    keep_sem,
):
    width = wave.shape[0]
    terms = left.shape[0]
    strip = width // 4
    unit = width // 8
    sec = lax.axis_index("sec")
    mpo = lax.axis_index("mpo")

    scalars = [
        pltpu.make_async_copy(src, dst, scalar_sems.at[n])
        for n, (src, dst) in enumerate(
            ((cls_hbm, cls), (tid_hbm, tid), (pair_hbm, pair), (dims_hbm, dims), (coef_hbm, coef))
        )
    ]
    wave_copy = pltpu.make_async_copy(wave_hbm.at[0], wave, wave_sem)
    wave_copy.start()
    for copy in scalars:
        copy.start()

    def fetch(j, carry):
        for q in range(4):
            src = pl.multiple_of((sec ^ q) * strip, strip)
            pltpu.make_async_copy(
                left_hbm.at[0, j, pl.ds(src, strip)],
                left.at[j, pl.ds(q * strip, strip)],
                left_sems.at[j],
            ).start()
        for p, r in enumerate(COLUMN_ORDER[:2]):
            src = pl.multiple_of((mpo ^ r) * strip, strip)
            pltpu.make_async_copy(
                right_hbm.at[0, j, pl.ds(src, strip)],
                right.at[j, pl.ds(p * strip, strip)],
                right_sems.at[j],
            ).start()
        return carry

    def fetch_keep(j, carry):
        for p, r in enumerate(COLUMN_ORDER[2:]):
            src = pl.multiple_of((mpo ^ r) * strip, strip)
            pltpu.make_async_copy(
                right_hbm.at[0, j, pl.ds(src, strip)],
                keep_right.at[j, pl.ds(p * strip, strip)],
                keep_sem,
            ).start()
        return carry

    lax.fori_loop(0, terms, fetch, 0)
    lax.fori_loop(0, terms, fetch_keep, 0)
    clear(lead_ref, rest_ref)
    for copy in scalars:
        copy.wait()
    wave_copy.wait()
    row_limit = dims[0, sec] * unit
    col_limit = dims[1, sec] * unit

    def mask(i, carry):
        base = pl.multiple_of(i * 64, 64)
        row_pos = base + lax.broadcasted_iota(jnp.int32, (64, width), 0)
        col_pos = lax.broadcasted_iota(jnp.int32, (64, width), 1)
        inside = (row_pos < row_limit) & (col_pos < col_limit)
        band = wave[pl.ds(base, 64), :].astype(jnp.float32)
        wave[pl.ds(base, 64), :] = jnp.where(inside, band, 0.0).astype(jnp.bfloat16)
        return carry

    lax.fori_loop(0, width // 64, mask, 0)
    for j in range(terms):
        pltpu.make_async_copy(left_hbm.at[0, j], left.at[j], left_sems.at[j]).wait()
        half = jnp.dot(left[j], wave[...], preferred_element_type=jnp.float32)
        half = half.astype(jnp.bfloat16)
        half_ref[j] = half
        pltpu.make_async_copy(
            right_hbm.at[0, j, pl.ds(0, 2 * strip)], right.at[j], right_sems.at[j]
        ).wait()
        spread(lead_ref, rest_ref, half, right[j], pair[sec, cls[0, j]], coef[tid[0, j]])
    pltpu.make_async_copy(
        right_hbm.at[0, pl.ds(0, terms), pl.ds(0, 2 * strip)], keep_right, keep_sem
    ).wait()


def keep_kernel(
    cls_hbm,
    tid_hbm,
    pair_hbm,
    dims_hbm,
    coef_hbm,
    half_ref,
    right_ref,
    lead_ref,
    rest_ref,
    mask_ref,
    cls,
    tid,
    pair,
    dims,
    coef,
    scalar_sems,
):
    terms, width, _ = half_ref.shape
    targets, strip, _ = mask_ref.shape
    unit = width // 8
    sec = lax.axis_index("sec")
    mpo = lax.axis_index("mpo")
    scalars = [
        pltpu.make_async_copy(src, dst, scalar_sems.at[n])
        for n, (src, dst) in enumerate(
            ((cls_hbm, cls), (tid_hbm, tid), (pair_hbm, pair), (dims_hbm, dims), (coef_hbm, coef))
        )
    ]
    for copy in scalars:
        copy.start()
    clear(lead_ref, rest_ref)
    for copy in scalars:
        copy.wait()
    for j in range(terms):
        spread(
            lead_ref, rest_ref, half_ref[j], right_ref[j], pair[sec, cls[0, j]], coef[tid[0, j]]
        )
    lane = mpo * strip + lax.broadcasted_iota(jnp.int32, (strip, strip), 1)
    line = sec * strip + lax.broadcasted_iota(jnp.int32, (strip, strip), 0)

    def target_mask(t, carry):
        inside = (line < dims[0, t] * unit) & (lane < dims[1, t] * unit)
        mask_ref[t] = jnp.where(inside, 1.0, 0.0).astype(jnp.bfloat16)
        return carry

    lax.fori_loop(0, targets, target_mask, 0)


def clear(*refs):
    def one(t, carry):
        for ref in refs:
            ref[t] = jnp.zeros(ref.shape[1:], ref.dtype)
        return carry

    lax.fori_loop(0, refs[0].shape[0], one, 0)


def spread(lead, rest, half, right, t, weight):
    contrib = lax.dot_general(
        half, right, (((1,), (1,)), ((), ())), preferred_element_type=jnp.float32
    )
    strip = contrib.shape[1] // 2
    a_rows = (rest.shape[1] - 2 * strip) // 2
    b_rows = strip - a_rows
    soon = (2 * a_rows, 2 * a_rows + strip + 2 * b_rows)
    for q in range(4):
        for n in range(2):
            value = weight * contrib[q * strip : (q + 1) * strip, n * strip : (n + 1) * strip]
            if q == 0:
                put(rest, t, n * strip, value)
            elif q == 1:
                put(lead, t, soon[n], value)
            else:
                if n == 0:
                    put(lead, t, (q - 2) * a_rows, value[:a_rows])
                else:
                    put(rest, t, 2 * strip + (q - 2) * a_rows, value[:a_rows])
                put(lead, t, soon[n] + strip + (q - 2) * b_rows, value[a_rows:])


def put(ref, t, row, value):
    at = slice(row, row + value.shape[0])
    ref[t, at, :] = (ref[t, at, :].astype(jnp.float32) + value).astype(jnp.bfloat16)


def lead_kernel(keep_ref, recv_ref, rest_in, rest_out, far_ref, one_far, one_near, *own_refs):
    del rest_in, rest_out
    row = far_ref.shape[1]
    far_ref[...] = add(keep_ref[:, :row, :], recv_ref[:, :row, :])
    for n, one_ref in enumerate((one_far, one_near)):
        at = slice(row, row + one_ref.shape[1])
        one_ref[...] = add(keep_ref[:, at, :], recv_ref[:, at, :])
        row += one_ref.shape[1]
        for own_ref in own_refs:
            at = slice(row, row + own_ref.shape[2])
            own_ref[n] = add(keep_ref[:, at, :], recv_ref[:, at, :])
            row += own_ref.shape[2]


def own_kernel(keep_ref, recv_ref, cross_ref, later_in, later_out, *own_refs):
    del later_in, later_out
    rows = own_refs[0].shape[1]
    row = keep_ref.shape[1] - 2 * rows
    for n, own_ref in enumerate(own_refs[::-1]):
        at = slice(row + n * rows, row + (n + 1) * rows)
        own_ref[...] = add(
            keep_ref[:, at, :], recv_ref[:, at, :], cross_ref[:, n * rows : (n + 1) * rows, :]
        )


def here_kernel(keep_ref, recv_ref, one_ref, two_ref, three_ref, after_ref, far_ref, near_ref):
    del after_ref
    strip = far_ref.shape[1]
    a_rows = strip - two_ref.shape[2]
    for n, out_ref in enumerate((far_ref, near_ref)):
        for first, last in ((0, a_rows), (a_rows, strip)):
            at = slice(n * strip + first, n * strip + last)
            parts = [keep_ref[:, at, :], recv_ref[:, at, :]]
            if n == 0:
                parts += [one_ref[:, first:last, :]]
            if first:
                parts += [two_ref[n], three_ref[n]]
            out_ref[:, first:last, :] = total(*parts).astype(out_ref.dtype)


def widen_kernel(one_ref, after_ref, sum_ref):
    del after_ref
    sum_ref[...] = one_ref[...].astype(jnp.float32)


def far_sum_kernel(two_ref, three_ref, sum_ref):
    sum_ref[...] = total(two_ref[...], three_ref[...])


def final_kernel(mask_ref, near_ref, one_ref, cross_ref, sum_ref, out_ref):
    a_rows, strip = sum_ref.shape[1], out_ref.shape[1]
    for first, last in ((0, a_rows), (a_rows, strip)):
        parts = [ref[:, first:last, :] for ref in (near_ref, one_ref, cross_ref)]
        if not first:
            parts += [sum_ref[...]]
        inside = mask_ref[:, first:last, :].astype(jnp.float32) > 0.0
        out_ref[:, first:last, :] = jnp.where(inside, total(*parts), 0.0).astype(jnp.bfloat16)


def total(*arrays):
    result = arrays[0].astype(jnp.float32)
    for array in arrays[1:]:
        result = result + array.astype(jnp.float32)
    return result


def add(*arrays):
    return total(*arrays).astype(jnp.bfloat16)


def swap(array, axis, mask):
    return lax.ppermute(array, axis, [(i, i ^ mask) for i in range(lax.axis_size(axis))])


def by_targets(
    wave_blocks, left_env, right_env, term_class, term_id, block_dims, pair_table, mpo_coef
):
    width = wave_blocks.shape[1]
    terms = left_env.shape[1]
    targets = block_dims.shape[0]
    strip = width // 4
    a_rows = strip * 3 // 4
    b_rows = strip - a_rows
    vmem = pl.BlockSpec(memory_space=pltpu.VMEM)
    hbm = pl.BlockSpec(memory_space=pltpu.HBM)

    def like(*shape):
        return jax.ShapeDtypeStruct(shape + (strip,), jnp.bfloat16)

    def call(kernel, out_shape, *args, aliases={}, span=0.1):
        return pl.pallas_call(
            kernel,
            out_shape=out_shape,
            in_specs=[vmem] * len(args),
            out_specs=jax.tree.map(lambda _: vmem, out_shape),
            input_output_aliases=aliases,
            cost_estimate=pl.CostEstimate(
                flops=round(span * 1e9), bytes_accessed=0, transcendentals=0
            ),
            compiler_params=SMALL,
            name=kernel.__name__,
        )(*args)

    scalars = (term_class, term_id, pair_table, block_dims.T, mpo_coef)
    operands = [
        pltpu.with_memory_space_constraint(x, pltpu.HBM)
        for x in (*scalars, wave_blocks, left_env, right_env)
    ]
    lead_shape = like(targets, 2 * a_rows + 2 * (strip + 2 * b_rows))
    rest_shape = like(targets, 2 * strip + 2 * a_rows)
    scalar_room = [pltpu.SMEM(scalar.shape, scalar.dtype) for scalar in scalars]
    limit = pltpu.CompilerParams(vmem_limit_bytes=16 * 1024 * 1024)
    half_shape = jax.ShapeDtypeStruct((terms, width, width), jnp.bfloat16)
    right_shape = jax.ShapeDtypeStruct((terms, 2 * strip, width), jnp.bfloat16)
    lead_send, rest_send, half, keep_right = pl.pallas_call(
        send_kernel,
        out_shape=[lead_shape, rest_shape, half_shape, right_shape],
        in_specs=[hbm] * 8,
        out_specs=[vmem] * 4,
        scratch_shapes=scalar_room
        + [
            pltpu.VMEM((width, width), jnp.bfloat16),
            pltpu.VMEM((terms, width, width), jnp.bfloat16),
            pltpu.VMEM((terms, 2 * strip, width), jnp.bfloat16),
            pltpu.SemaphoreType.DMA((len(scalars),)),
            pltpu.SemaphoreType.DMA,
            pltpu.SemaphoreType.DMA((terms,)),
            pltpu.SemaphoreType.DMA((terms,)),
            pltpu.SemaphoreType.DMA,
        ],
        compiler_params=limit,
        cost_estimate=pl.CostEstimate(
            flops=3 * terms * width**3, bytes_accessed=4 * 1024 * 1024, transcendentals=0
        ),
        name="send_kernel",
    )(*operands)
    lead_keep, rest_keep, mask = pl.pallas_call(
        keep_kernel,
        out_shape=[lead_shape, rest_shape, like(targets, strip)],
        in_specs=[hbm] * len(scalars) + [vmem] * 2,
        out_specs=[vmem] * 3,
        scratch_shapes=scalar_room + [pltpu.SemaphoreType.DMA((len(scalars),))],
        compiler_params=limit,
        cost_estimate=pl.CostEstimate(
            flops=3 * terms * width**3, bytes_accessed=0, transcendentals=0
        ),
        name="keep_kernel",
    )(*operands[: len(scalars)], half, keep_right)
    lead_recv = swap(lead_send, "mpo", 1)
    part = like(2, targets, b_rows)
    rest_send, far, one, one_near, two, three = call(
        lead_kernel,
        [rest_shape, like(targets, 2 * a_rows)] + [like(targets, strip)] * 2 + [part] * 2,
        lead_keep,
        lead_recv,
        rest_send,
        aliases={2: 0},
        span=3,
    )
    cross = swap(far, "mpo", 2)
    one, two, three = [swap(x, "sec", q) for x, q in ((one, 1), (two, 2), (three, 3))]
    rest_recv = swap(rest_send, "mpo", 1)
    one_near, *own = call(
        own_kernel,
        [like(targets, strip)] + [like(targets, a_rows)] * 2,
        rest_keep,
        rest_recv,
        cross,
        one_near,
        aliases={3: 0},
        span=3,
    )
    near = jax.ShapeDtypeStruct((targets, strip, strip), jnp.float32)
    one_wide = jax.ShapeDtypeStruct(one.shape, jnp.float32)
    one = call(widen_kernel, one_wide, one, own[0], span=3)
    here, near = call(
        here_kernel,
        [like(targets, strip), near],
        rest_keep,
        rest_recv,
        one,
        two,
        three,
        own[0],
        span=3,
    )
    own = [swap(array, "sec", q) for array, q in zip(own[::-1], (2, 3))]
    one_near = swap(one_near, "sec", 1)
    here = swap(here, "mpo", 2)
    far_sum = jax.ShapeDtypeStruct((targets, a_rows, strip), jnp.float32)
    far_sum = call(far_sum_kernel, far_sum, *own, span=3)
    return call(final_kernel, like(targets, strip), mask, near, one_near, here, far_sum)


def by_classes(
    wave_blocks, left_env, right_env, term_class, term_id, block_dims, pair_table, mpo_coef
):
    sec_count = lax.axis_size("sec")
    mpo_count = lax.axis_size("mpo")
    local_blocks = wave_blocks.shape[0]
    block_width = wave_blocks.shape[1]
    total_blocks = block_dims.shape[0]
    classes = pair_table.shape[1]
    tile_states = block_width // 8
    positions = jnp.arange(block_width)
    first = lax.axis_index("sec") * local_blocks
    own_dims = lax.dynamic_slice_in_dim(block_dims, first, local_blocks, 0)
    row_ok = positions[None, :] < own_dims[:, 0:1] * tile_states
    col_ok = positions[None, :] < own_dims[:, 1:2] * tile_states
    masked = jnp.where(
        row_ok[:, :, None] & col_ok[:, None, :], wave_blocks, jnp.zeros_like(wave_blocks)
    )
    left_part = jnp.einsum(
        "bjxy,byz->bjxz", left_env, masked, preferred_element_type=jnp.float32
    ).astype(jnp.bfloat16)
    contrib = jnp.einsum(
        "bjxz,bjwz->bjxw", left_part, right_env, preferred_element_type=jnp.float32
    )
    weights = jnp.sum(
        jnp.where(
            term_id[:, :, None] == jnp.arange(mpo_coef.shape[0])[None, None, :],
            mpo_coef[None, None, :],
            0.0,
        ),
        axis=-1,
    )
    picks = (term_class[:, :, None] == jnp.arange(classes)[None, None, :]).astype(
        jnp.float32
    ) * weights[:, :, None]
    grouped = jnp.einsum("bjc,bjxw->bcxw", picks, contrib, precision=lax.Precision.HIGHEST).astype(
        jnp.bfloat16
    )
    targets = pair_table.reshape(-1)
    routing = targets[None, :] == jnp.arange(total_blocks)[:, None]
    strip_rows = block_width // sec_count
    strip_cols = block_width // mpo_count
    outgoing = grouped.reshape(local_blocks * classes, block_width, block_width)
    arrived = lax.all_to_all(
        lax.all_to_all(outgoing, "sec", split_axis=1, concat_axis=0, tiled=True),
        "mpo",
        split_axis=2,
        concat_axis=0,
        tiled=True,
    )
    arrived = arrived.reshape(mpo_count, total_blocks * classes, strip_rows, strip_cols)
    summed = jnp.einsum(
        "tk,mkrw->trw", routing.astype(jnp.bfloat16), arrived, preferred_element_type=jnp.float32
    )
    row_index = lax.axis_index("sec") * strip_rows + jnp.arange(strip_rows)
    col_index = lax.axis_index("mpo") * strip_cols + jnp.arange(strip_cols)
    rows_in = row_index[None, :] < block_dims[:, 0:1] * tile_states
    cols_in = col_index[None, :] < block_dims[:, 1:2] * tile_states
    inside = rows_in[:, :, None] & cols_in[:, None, :]
    return jnp.where(inside, summed, 0.0).astype(jnp.bfloat16)


def solution(mesh):
    placed = (
        P(("grp", "sec"), None, None),
        P(("grp", "sec"), "mpo", None, None),
        P(("grp", "sec"), "mpo", None, None),
        P(("grp", "sec"), "mpo"),
        P(("grp", "sec"), "mpo"),
        P("grp", None),
        P("grp", None),
        P(),
    )

    def on_device(*arrays):
        wave_blocks, block_dims = arrays[0], arrays[5]
        small = wave_blocks.shape[0] == 1 and block_dims.shape[0] == 4
        if small and mesh.shape["sec"] == 4 and mesh.shape["mpo"] == 4:
            return by_targets(*arrays)
        return by_classes(*arrays)

    return jax.shard_map(
        on_device, mesh=mesh, in_specs=placed, out_specs=P("grp", "sec", "mpo"), check_vma=False
    )
```

```python
import functools

import jax
import jax.numpy as jnp
from jax import lax
from jax.experimental import pallas as pl
from jax.experimental.pallas import tpu as pltpu
from jax.sharding import PartitionSpec as P

COLUMN_ORDER = (3, 1, 2, 0)
SMALL = pltpu.CompilerParams(vmem_limit_bytes=4 * 1024 * 1024)


def send_kernel(
    cls_hbm,
    tid_hbm,
    pair_hbm,
    dims_hbm,
    coef_hbm,
    wave_hbm,
    left_hbm,
    right_hbm,
    lead_ref,
    rest_ref,
    half_ref,
    keep_right,
    cls,
    tid,
    pair,
    dims,
    coef,
    wave,
    left,
    right,
    scalar_sems,
    wave_sem,
    left_sems,
    right_sems,
    keep_sem,
):
    width = wave.shape[0]
    terms = left.shape[0]
    strip = width // 4
    unit = width // 8
    sec = lax.axis_index("sec")
    mpo = lax.axis_index("mpo")

    scalars = [
        pltpu.make_async_copy(src, dst, scalar_sems.at[n])
        for n, (src, dst) in enumerate(
            ((cls_hbm, cls), (tid_hbm, tid), (pair_hbm, pair), (dims_hbm, dims), (coef_hbm, coef))
        )
    ]
    wave_copy = pltpu.make_async_copy(wave_hbm.at[0], wave, wave_sem)
    wave_copy.start()
    for copy in scalars:
        copy.start()

    def fetch(j, carry):
        for q in range(4):
            src = pl.multiple_of((sec ^ q) * strip, strip)
            pltpu.make_async_copy(
                left_hbm.at[0, j, pl.ds(src, strip)],
                left.at[j, pl.ds(q * strip, strip)],
                left_sems.at[j],
            ).start()
        for p, r in enumerate(COLUMN_ORDER[:2]):
            src = pl.multiple_of((mpo ^ r) * strip, strip)
            pltpu.make_async_copy(
                right_hbm.at[0, j, pl.ds(src, strip)],
                right.at[j, pl.ds(p * strip, strip)],
                right_sems.at[j],
            ).start()
        return carry

    def fetch_keep(j, carry):
        for p, r in enumerate(COLUMN_ORDER[2:]):
            src = pl.multiple_of((mpo ^ r) * strip, strip)
            pltpu.make_async_copy(
                right_hbm.at[0, j, pl.ds(src, strip)],
                keep_right.at[j, pl.ds(p * strip, strip)],
                keep_sem,
            ).start()
        return carry

    lax.fori_loop(0, terms, fetch, 0)
    lax.fori_loop(0, terms, fetch_keep, 0)
    clear(lead_ref, rest_ref)
    for copy in scalars:
        copy.wait()
    wave_copy.wait()
    row_limit = dims[0, sec] * unit
    col_limit = dims[1, sec] * unit

    def mask(i, carry):
        base = pl.multiple_of(i * 64, 64)
        row_pos = base + lax.broadcasted_iota(jnp.int32, (64, width), 0)
        col_pos = lax.broadcasted_iota(jnp.int32, (64, width), 1)
        inside = (row_pos < row_limit) & (col_pos < col_limit)
        band = wave[pl.ds(base, 64), :].astype(jnp.float32)
        wave[pl.ds(base, 64), :] = jnp.where(inside, band, 0.0).astype(jnp.bfloat16)
        return carry

    lax.fori_loop(0, width // 64, mask, 0)
    for j in range(terms):
        pltpu.make_async_copy(left_hbm.at[0, j], left.at[j], left_sems.at[j]).wait()
        half = jnp.dot(left[j], wave[...], preferred_element_type=jnp.float32)
        half = half.astype(jnp.bfloat16)
        half_ref[j] = half
        pltpu.make_async_copy(
            right_hbm.at[0, j, pl.ds(0, 2 * strip)], right.at[j], right_sems.at[j]
        ).wait()
        spread(lead_ref, rest_ref, half, right[j], pair[sec, cls[0, j]], coef[tid[0, j]])
    pltpu.make_async_copy(
        right_hbm.at[0, pl.ds(0, terms), pl.ds(0, 2 * strip)], keep_right, keep_sem
    ).wait()


def keep_kernel(
    cls_hbm,
    tid_hbm,
    pair_hbm,
    dims_hbm,
    coef_hbm,
    half_ref,
    right_ref,
    lead_ref,
    rest_ref,
    mask_ref,
    cls,
    tid,
    pair,
    dims,
    coef,
    scalar_sems,
):
    terms, width, _ = half_ref.shape
    targets, strip, _ = mask_ref.shape
    unit = width // 8
    sec = lax.axis_index("sec")
    mpo = lax.axis_index("mpo")
    scalars = [
        pltpu.make_async_copy(src, dst, scalar_sems.at[n])
        for n, (src, dst) in enumerate(
            ((cls_hbm, cls), (tid_hbm, tid), (pair_hbm, pair), (dims_hbm, dims), (coef_hbm, coef))
        )
    ]
    for copy in scalars:
        copy.start()
    clear(lead_ref, rest_ref)
    for copy in scalars:
        copy.wait()
    for j in range(terms):
        spread(
            lead_ref, rest_ref, half_ref[j], right_ref[j], pair[sec, cls[0, j]], coef[tid[0, j]]
        )
    lane = mpo * strip + lax.broadcasted_iota(jnp.int32, (strip, strip), 1)
    line = sec * strip + lax.broadcasted_iota(jnp.int32, (strip, strip), 0)

    def target_mask(t, carry):
        inside = (line < dims[0, t] * unit) & (lane < dims[1, t] * unit)
        mask_ref[t] = jnp.where(inside, 1.0, 0.0).astype(jnp.bfloat16)
        return carry

    lax.fori_loop(0, targets, target_mask, 0)


def clear(*refs):
    def one(t, carry):
        for ref in refs:
            ref[t] = jnp.zeros(ref.shape[1:], ref.dtype)
        return carry

    lax.fori_loop(0, refs[0].shape[0], one, 0)


def spread(lead, rest, half, right, t, weight):
    contrib = lax.dot_general(
        half, right, (((1,), (1,)), ((), ())), preferred_element_type=jnp.float32
    )
    strip = contrib.shape[1] // 2
    a_rows = (rest.shape[1] - 2 * strip) // 2
    b_rows = strip - a_rows
    soon = (2 * a_rows, 2 * a_rows + strip + 2 * b_rows)
    for q in range(4):
        for n in range(2):
            value = weight * contrib[q * strip : (q + 1) * strip, n * strip : (n + 1) * strip]
            if q == 0:
                put(rest, t, n * strip, value)
            elif q == 1:
                put(lead, t, soon[n], value)
            else:
                if n == 0:
                    put(lead, t, (q - 2) * a_rows, value[:a_rows])
                else:
                    put(rest, t, 2 * strip + (q - 2) * a_rows, value[:a_rows])
                put(lead, t, soon[n] + strip + (q - 2) * b_rows, value[a_rows:])


def put(ref, t, row, value):
    at = slice(row, row + value.shape[0])
    ref[t, at, :] = (ref[t, at, :].astype(jnp.float32) + value).astype(jnp.bfloat16)


def lead_kernel(keep_ref, recv_ref, rest_in, rest_out, far_ref, one_far, one_near, *own_refs):
    del rest_in, rest_out
    row = far_ref.shape[1]
    far_ref[...] = add(keep_ref[:, :row, :], recv_ref[:, :row, :])
    for n, one_ref in enumerate((one_far, one_near)):
        at = slice(row, row + one_ref.shape[1])
        one_ref[...] = add(keep_ref[:, at, :], recv_ref[:, at, :])
        row += one_ref.shape[1]
        for own_ref in own_refs:
            at = slice(row, row + own_ref.shape[2])
            own_ref[n] = add(keep_ref[:, at, :], recv_ref[:, at, :])
            row += own_ref.shape[2]


def own_kernel(keep_ref, recv_ref, cross_ref, later_in, later_out, *own_refs):
    del later_in, later_out
    rows = own_refs[0].shape[1]
    row = keep_ref.shape[1] - 2 * rows
    for n, own_ref in enumerate(own_refs[::-1]):
        at = slice(row + n * rows, row + (n + 1) * rows)
        own_ref[...] = add(
            keep_ref[:, at, :], recv_ref[:, at, :], cross_ref[:, n * rows : (n + 1) * rows, :]
        )


def here_kernel(keep_ref, recv_ref, one_ref, two_ref, three_ref, after_ref, far_ref, near_ref):
    del after_ref
    strip = far_ref.shape[1]
    a_rows = strip - two_ref.shape[2]
    for n, out_ref in enumerate((far_ref, near_ref)):
        for first, last in ((0, a_rows), (a_rows, strip)):
            at = slice(n * strip + first, n * strip + last)
            parts = [keep_ref[:, at, :], recv_ref[:, at, :]]
            if n == 0:
                parts += [one_ref[:, first:last, :]]
            if first:
                parts += [two_ref[n], three_ref[n]]
            out_ref[:, first:last, :] = total(*parts).astype(out_ref.dtype)


def widen_kernel(one_ref, sum_ref):
    sum_ref[...] = one_ref[...].astype(jnp.float32)


def far_sum_kernel(two_ref, three_ref, sum_ref):
    sum_ref[...] = total(two_ref[...], three_ref[...])


def final_kernel(mask_ref, near_ref, one_ref, cross_ref, sum_ref, out_ref):
    a_rows, strip = sum_ref.shape[1], out_ref.shape[1]
    for first, last in ((0, a_rows), (a_rows, strip)):
        parts = [ref[:, first:last, :] for ref in (near_ref, one_ref, cross_ref)]
        if not first:
            parts += [sum_ref[...]]
        inside = mask_ref[:, first:last, :].astype(jnp.float32) > 0.0
        out_ref[:, first:last, :] = jnp.where(inside, total(*parts), 0.0).astype(jnp.bfloat16)


def total(*arrays):
    result = arrays[0].astype(jnp.float32)
    for array in arrays[1:]:
        result = result + array.astype(jnp.float32)
    return result


def add(*arrays):
    return total(*arrays).astype(jnp.bfloat16)


def swap(array, axis, mask):
    return lax.ppermute(array, axis, [(i, i ^ mask) for i in range(lax.axis_size(axis))])


def by_targets(
    wave_blocks, left_env, right_env, term_class, term_id, block_dims, pair_table, mpo_coef
):
    width = wave_blocks.shape[1]
    terms = left_env.shape[1]
    targets = block_dims.shape[0]
    strip = width // 4
    a_rows = strip * 3 // 4
    b_rows = strip - a_rows
    vmem = pl.BlockSpec(memory_space=pltpu.VMEM)
    hbm = pl.BlockSpec(memory_space=pltpu.HBM)

    def like(*shape):
        return jax.ShapeDtypeStruct(shape + (strip,), jnp.bfloat16)

    def call(kernel, out_shape, *args, aliases={}, span=0.1):
        return pl.pallas_call(
            kernel,
            out_shape=out_shape,
            in_specs=[vmem] * len(args),
            out_specs=jax.tree.map(lambda _: vmem, out_shape),
            input_output_aliases=aliases,
            cost_estimate=pl.CostEstimate(
                flops=round(span * 1e9), bytes_accessed=0, transcendentals=0
            ),
            compiler_params=SMALL,
            name=kernel.__name__,
        )(*args)

    scalars = (term_class, term_id, pair_table, block_dims.T, mpo_coef)
    operands = [
        pltpu.with_memory_space_constraint(x, pltpu.HBM)
        for x in (*scalars, wave_blocks, left_env, right_env)
    ]
    lead_shape = like(targets, 2 * a_rows + 2 * (strip + 2 * b_rows))
    rest_shape = like(targets, 2 * strip + 2 * a_rows)
    scalar_room = [pltpu.SMEM(scalar.shape, scalar.dtype) for scalar in scalars]
    limit = pltpu.CompilerParams(vmem_limit_bytes=16 * 1024 * 1024)
    half_shape = jax.ShapeDtypeStruct((terms, width, width), jnp.bfloat16)
    right_shape = jax.ShapeDtypeStruct((terms, 2 * strip, width), jnp.bfloat16)
    lead_send, rest_send, half, keep_right = pl.pallas_call(
        send_kernel,
        out_shape=[lead_shape, rest_shape, half_shape, right_shape],
        in_specs=[hbm] * 8,
        out_specs=[vmem] * 4,
        scratch_shapes=scalar_room
        + [
            pltpu.VMEM((width, width), jnp.bfloat16),
            pltpu.VMEM((terms, width, width), jnp.bfloat16),
            pltpu.VMEM((terms, 2 * strip, width), jnp.bfloat16),
            pltpu.SemaphoreType.DMA((len(scalars),)),
            pltpu.SemaphoreType.DMA,
            pltpu.SemaphoreType.DMA((terms,)),
            pltpu.SemaphoreType.DMA((terms,)),
            pltpu.SemaphoreType.DMA,
        ],
        compiler_params=limit,
        cost_estimate=pl.CostEstimate(
            flops=3 * terms * width**3, bytes_accessed=4 * 1024 * 1024, transcendentals=0
        ),
        name="send_kernel",
    )(*operands)
    lead_keep, rest_keep, mask = pl.pallas_call(
        keep_kernel,
        out_shape=[lead_shape, rest_shape, like(targets, strip)],
        in_specs=[hbm] * len(scalars) + [vmem] * 2,
        out_specs=[vmem] * 3,
        scratch_shapes=scalar_room + [pltpu.SemaphoreType.DMA((len(scalars),))],
        compiler_params=limit,
        cost_estimate=pl.CostEstimate(
            flops=3 * terms * width**3, bytes_accessed=0, transcendentals=0
        ),
        name="keep_kernel",
    )(*operands[: len(scalars)], half, keep_right)
    lead_recv = swap(lead_send, "mpo", 1)
    part = like(2, targets, b_rows)
    rest_send, far, one, one_near, two, three = call(
        lead_kernel,
        [rest_shape, like(targets, 2 * a_rows)] + [like(targets, strip)] * 2 + [part] * 2,
        lead_keep,
        lead_recv,
        rest_send,
        aliases={2: 0},
        span=3,
    )
    cross = swap(far, "mpo", 2)
    one, two, three = [swap(x, "sec", q) for x, q in ((one, 1), (two, 2), (three, 3))]
    rest_recv = swap(rest_send, "mpo", 1)
    one_near, *own = call(
        own_kernel,
        [like(targets, strip)] + [like(targets, a_rows)] * 2,
        rest_keep,
        rest_recv,
        cross,
        one_near,
        aliases={3: 0},
        span=3,
    )
    near = jax.ShapeDtypeStruct((targets, strip, strip), jnp.float32)
    one_wide = jax.ShapeDtypeStruct(one.shape, jnp.float32)
    one = call(widen_kernel, one_wide, one, span=.1)
    here, near = call(
        here_kernel,
        [like(targets, strip), near],
        rest_keep,
        rest_recv,
        one,
        two,
        three,
        own[0],
        span=3,
    )
    own = [swap(array, "sec", q) for array, q in zip(own[::-1], (2, 3))]
    one_near = swap(one_near, "sec", 1)
    here = swap(here, "mpo", 2)
    far_sum = jax.ShapeDtypeStruct((targets, a_rows, strip), jnp.float32)
    far_sum = call(far_sum_kernel, far_sum, *own, span=3)
    return call(final_kernel, like(targets, strip), mask, near, one_near, here, far_sum)


def by_classes(
    wave_blocks, left_env, right_env, term_class, term_id, block_dims, pair_table, mpo_coef
):
    sec_count = lax.axis_size("sec")
    mpo_count = lax.axis_size("mpo")
    local_blocks = wave_blocks.shape[0]
    block_width = wave_blocks.shape[1]
    total_blocks = block_dims.shape[0]
    classes = pair_table.shape[1]
    tile_states = block_width // 8
    positions = jnp.arange(block_width)
    first = lax.axis_index("sec") * local_blocks
    own_dims = lax.dynamic_slice_in_dim(block_dims, first, local_blocks, 0)
    row_ok = positions[None, :] < own_dims[:, 0:1] * tile_states
    col_ok = positions[None, :] < own_dims[:, 1:2] * tile_states
    masked = jnp.where(
        row_ok[:, :, None] & col_ok[:, None, :], wave_blocks, jnp.zeros_like(wave_blocks)
    )
    left_part = jnp.einsum(
        "bjxy,byz->bjxz", left_env, masked, preferred_element_type=jnp.float32
    ).astype(jnp.bfloat16)
    contrib = jnp.einsum(
        "bjxz,bjwz->bjxw", left_part, right_env, preferred_element_type=jnp.float32
    )
    weights = jnp.sum(
        jnp.where(
            term_id[:, :, None] == jnp.arange(mpo_coef.shape[0])[None, None, :],
            mpo_coef[None, None, :],
            0.0,
        ),
        axis=-1,
    )
    picks = (term_class[:, :, None] == jnp.arange(classes)[None, None, :]).astype(
        jnp.float32
    ) * weights[:, :, None]
    grouped = jnp.einsum("bjc,bjxw->bcxw", picks, contrib, precision=lax.Precision.HIGHEST).astype(
        jnp.bfloat16
    )
    targets = pair_table.reshape(-1)
    routing = targets[None, :] == jnp.arange(total_blocks)[:, None]
    strip_rows = block_width // sec_count
    strip_cols = block_width // mpo_count
    outgoing = grouped.reshape(local_blocks * classes, block_width, block_width)
    arrived = lax.all_to_all(
        lax.all_to_all(outgoing, "sec", split_axis=1, concat_axis=0, tiled=True),
        "mpo",
        split_axis=2,
        concat_axis=0,
        tiled=True,
    )
    arrived = arrived.reshape(mpo_count, total_blocks * classes, strip_rows, strip_cols)
    summed = jnp.einsum(
        "tk,mkrw->trw", routing.astype(jnp.bfloat16), arrived, preferred_element_type=jnp.float32
    )
    row_index = lax.axis_index("sec") * strip_rows + jnp.arange(strip_rows)
    col_index = lax.axis_index("mpo") * strip_cols + jnp.arange(strip_cols)
    rows_in = row_index[None, :] < block_dims[:, 0:1] * tile_states
    cols_in = col_index[None, :] < block_dims[:, 1:2] * tile_states
    inside = rows_in[:, :, None] & cols_in[:, None, :]
    return jnp.where(inside, summed, 0.0).astype(jnp.bfloat16)


def solution(mesh):
    placed = (
        P(("grp", "sec"), None, None),
        P(("grp", "sec"), "mpo", None, None),
        P(("grp", "sec"), "mpo", None, None),
        P(("grp", "sec"), "mpo"),
        P(("grp", "sec"), "mpo"),
        P("grp", None),
        P("grp", None),
        P(),
    )

    def on_device(*arrays):
        wave_blocks, block_dims = arrays[0], arrays[5]
        small = wave_blocks.shape[0] == 1 and block_dims.shape[0] == 4
        if small and mesh.shape["sec"] == 4 and mesh.shape["mpo"] == 4:
            return by_targets(*arrays)
        return by_classes(*arrays)

    return jax.shard_map(
        on_device, mesh=mesh, in_specs=placed, out_specs=P("grp", "sec", "mpo"), check_vma=False
    )
```

```python
import functools

import jax
import jax.numpy as jnp
from jax import lax
from jax.experimental import pallas as pl
from jax.experimental.pallas import tpu as pltpu
from jax.sharding import PartitionSpec as P

COLUMN_ORDER = (3, 1, 2, 0)
SMALL = pltpu.CompilerParams(vmem_limit_bytes=4 * 1024 * 1024)


def send_kernel(
    cls_hbm,
    tid_hbm,
    pair_hbm,
    dims_hbm,
    coef_hbm,
    wave_hbm,
    left_hbm,
    right_hbm,
    lead_ref,
    rest_ref,
    half_ref,
    keep_right,
    cls,
    tid,
    pair,
    dims,
    coef,
    wave,
    left,
    right,
    scalar_sems,
    wave_sem,
    left_sems,
    right_sems,
    keep_sem,
):
    width = wave.shape[0]
    terms = left.shape[0]
    strip = width // 4
    unit = width // 8
    sec = lax.axis_index("sec")
    mpo = lax.axis_index("mpo")

    scalars = [
        pltpu.make_async_copy(src, dst, scalar_sems.at[n])
        for n, (src, dst) in enumerate(
            ((cls_hbm, cls), (tid_hbm, tid), (pair_hbm, pair), (dims_hbm, dims), (coef_hbm, coef))
        )
    ]
    wave_copy = pltpu.make_async_copy(wave_hbm.at[0], wave, wave_sem)
    wave_copy.start()
    for copy in scalars:
        copy.start()

    def fetch(j, carry):
        for q in range(4):
            src = pl.multiple_of((sec ^ q) * strip, strip)
            pltpu.make_async_copy(
                left_hbm.at[0, j, pl.ds(src, strip)],
                left.at[j, pl.ds(q * strip, strip)],
                left_sems.at[j],
            ).start()
        for p, r in enumerate(COLUMN_ORDER[:2]):
            src = pl.multiple_of((mpo ^ r) * strip, strip)
            pltpu.make_async_copy(
                right_hbm.at[0, j, pl.ds(src, strip)],
                right.at[j, pl.ds(p * strip, strip)],
                right_sems.at[j],
            ).start()
        return carry

    def fetch_keep(j, carry):
        for p, r in enumerate(COLUMN_ORDER[2:]):
            src = pl.multiple_of((mpo ^ r) * strip, strip)
            pltpu.make_async_copy(
                right_hbm.at[0, j, pl.ds(src, strip)],
                keep_right.at[j, pl.ds(p * strip, strip)],
                keep_sem,
            ).start()
        return carry

    lax.fori_loop(0, terms, fetch, 0)
    lax.fori_loop(0, terms, fetch_keep, 0)
    clear(lead_ref, rest_ref)
    for copy in scalars:
        copy.wait()
    wave_copy.wait()
    row_limit = dims[0, sec] * unit
    col_limit = dims[1, sec] * unit

    def mask(i, carry):
        base = pl.multiple_of(i * 64, 64)
        row_pos = base + lax.broadcasted_iota(jnp.int32, (64, width), 0)
        col_pos = lax.broadcasted_iota(jnp.int32, (64, width), 1)
        inside = (row_pos < row_limit) & (col_pos < col_limit)
        band = wave[pl.ds(base, 64), :].astype(jnp.float32)
        wave[pl.ds(base, 64), :] = jnp.where(inside, band, 0.0).astype(jnp.bfloat16)
        return carry

    lax.fori_loop(0, width // 64, mask, 0)
    for j in range(terms):
        pltpu.make_async_copy(left_hbm.at[0, j], left.at[j], left_sems.at[j]).wait()
        half = jnp.dot(left[j], wave[...], preferred_element_type=jnp.float32)
        half = half.astype(jnp.bfloat16)
        half_ref[j] = half
        pltpu.make_async_copy(
            right_hbm.at[0, j, pl.ds(0, 2 * strip)], right.at[j], right_sems.at[j]
        ).wait()
        spread(lead_ref, rest_ref, half, right[j], pair[sec, cls[0, j]], coef[tid[0, j]])
    pltpu.make_async_copy(
        right_hbm.at[0, pl.ds(0, terms), pl.ds(0, 2 * strip)], keep_right, keep_sem
    ).wait()


def keep_kernel(
    cls_hbm,
    tid_hbm,
    pair_hbm,
    dims_hbm,
    coef_hbm,
    half_ref,
    right_ref,
    lead_ref,
    rest_ref,
    mask_ref,
    cls,
    tid,
    pair,
    dims,
    coef,
    scalar_sems,
):
    terms, width, _ = half_ref.shape
    targets, strip, _ = mask_ref.shape
    unit = width // 8
    sec = lax.axis_index("sec")
    mpo = lax.axis_index("mpo")
    scalars = [
        pltpu.make_async_copy(src, dst, scalar_sems.at[n])
        for n, (src, dst) in enumerate(
            ((cls_hbm, cls), (tid_hbm, tid), (pair_hbm, pair), (dims_hbm, dims), (coef_hbm, coef))
        )
    ]
    for copy in scalars:
        copy.start()
    clear(lead_ref, rest_ref)
    for copy in scalars:
        copy.wait()
    for j in range(terms):
        spread(
            lead_ref, rest_ref, half_ref[j], right_ref[j], pair[sec, cls[0, j]], coef[tid[0, j]]
        )
    lane = mpo * strip + lax.broadcasted_iota(jnp.int32, (strip, strip), 1)
    line = sec * strip + lax.broadcasted_iota(jnp.int32, (strip, strip), 0)

    def target_mask(t, carry):
        inside = (line < dims[0, t] * unit) & (lane < dims[1, t] * unit)
        mask_ref[t] = jnp.where(inside, 1.0, 0.0).astype(jnp.bfloat16)
        return carry

    lax.fori_loop(0, targets, target_mask, 0)


def clear(*refs):
    def one(t, carry):
        for ref in refs:
            ref[t] = jnp.zeros(ref.shape[1:], ref.dtype)
        return carry

    lax.fori_loop(0, refs[0].shape[0], one, 0)


def spread(lead, rest, half, right, t, weight):
    contrib = lax.dot_general(
        half, right, (((1,), (1,)), ((), ())), preferred_element_type=jnp.float32
    )
    strip = contrib.shape[1] // 2
    a_rows = (rest.shape[1] - 2 * strip) // 2
    b_rows = strip - a_rows
    soon = (2 * a_rows, 2 * a_rows + strip + 2 * b_rows)
    for q in range(4):
        for n in range(2):
            value = weight * contrib[q * strip : (q + 1) * strip, n * strip : (n + 1) * strip]
            if q == 0:
                put(rest, t, n * strip, value)
            elif q == 1:
                put(lead, t, soon[n], value)
            else:
                if n == 0:
                    put(lead, t, (q - 2) * a_rows, value[:a_rows])
                else:
                    put(rest, t, 2 * strip + (q - 2) * a_rows, value[:a_rows])
                put(lead, t, soon[n] + strip + (q - 2) * b_rows, value[a_rows:])


def put(ref, t, row, value):
    at = slice(row, row + value.shape[0])
    ref[t, at, :] = (ref[t, at, :].astype(jnp.float32) + value).astype(jnp.bfloat16)


def lead_kernel(keep_ref, recv_ref, rest_in, rest_out, far_ref, one_far, one_near, *own_refs):
    del rest_in, rest_out
    row = far_ref.shape[1]
    far_ref[...] = add(keep_ref[:, :row, :], recv_ref[:, :row, :])
    for n, one_ref in enumerate((one_far, one_near)):
        at = slice(row, row + one_ref.shape[1])
        one_ref[...] = add(keep_ref[:, at, :], recv_ref[:, at, :])
        row += one_ref.shape[1]
        for own_ref in own_refs:
            at = slice(row, row + own_ref.shape[2])
            own_ref[n] = add(keep_ref[:, at, :], recv_ref[:, at, :])
            row += own_ref.shape[2]


def own_kernel(keep_ref, recv_ref, cross_ref, later_in, later_out, *own_refs):
    del later_in, later_out
    rows = own_refs[0].shape[1]
    row = keep_ref.shape[1] - 2 * rows
    for n, own_ref in enumerate(own_refs):
        at = slice(row + n * rows, row + (n + 1) * rows)
        own_ref[...] = add(
            keep_ref[:, at, :], recv_ref[:, at, :], cross_ref[:, n * rows : (n + 1) * rows, :]
        )


def here_kernel(keep_ref, recv_ref, one_ref, two_ref, three_ref, after_ref, far_ref, near_ref):
    del after_ref
    strip = far_ref.shape[1]
    a_rows = strip - two_ref.shape[2]
    for n, out_ref in enumerate((far_ref, near_ref)):
        for first, last in ((0, a_rows), (a_rows, strip)):
            at = slice(n * strip + first, n * strip + last)
            parts = [keep_ref[:, at, :], recv_ref[:, at, :]]
            if n == 0:
                parts += [one_ref[:, first:last, :]]
            if first:
                parts += [two_ref[n], three_ref[n]]
            out_ref[:, first:last, :] = total(*parts).astype(out_ref.dtype)


def far_sum_kernel(two_ref, three_ref, sum_ref):
    sum_ref[...] = total(two_ref[...], three_ref[...])


def final_kernel(mask_ref, near_ref, one_ref, cross_ref, sum_ref, out_ref):
    a_rows, strip = sum_ref.shape[1], out_ref.shape[1]
    for first, last in ((0, a_rows), (a_rows, strip)):
        parts = [ref[:, first:last, :] for ref in (near_ref, one_ref, cross_ref)]
        if not first:
            parts += [sum_ref[...]]
        inside = mask_ref[:, first:last, :].astype(jnp.float32) > 0.0
        out_ref[:, first:last, :] = jnp.where(inside, total(*parts), 0.0).astype(jnp.bfloat16)


def total(*arrays):
    result = arrays[0].astype(jnp.float32)
    for array in arrays[1:]:
        result = result + array.astype(jnp.float32)
    return result


def add(*arrays):
    return total(*arrays).astype(jnp.bfloat16)


def swap(array, axis, mask):
    return lax.ppermute(array, axis, [(i, i ^ mask) for i in range(lax.axis_size(axis))])


def by_targets(
    wave_blocks, left_env, right_env, term_class, term_id, block_dims, pair_table, mpo_coef
):
    width = wave_blocks.shape[1]
    terms = left_env.shape[1]
    targets = block_dims.shape[0]
    strip = width // 4
    a_rows = strip * 7 // 8
    b_rows = strip - a_rows
    vmem = pl.BlockSpec(memory_space=pltpu.VMEM)
    hbm = pl.BlockSpec(memory_space=pltpu.HBM)

    def like(*shape):
        return jax.ShapeDtypeStruct(shape + (strip,), jnp.bfloat16)

    def call(kernel, out_shape, *args, aliases={}, span=0.1):
        return pl.pallas_call(
            kernel,
            out_shape=out_shape,
            in_specs=[vmem] * len(args),
            out_specs=jax.tree.map(lambda _: vmem, out_shape),
            input_output_aliases=aliases,
            cost_estimate=pl.CostEstimate(
                flops=round(span * 1e9), bytes_accessed=0, transcendentals=0
            ),
            compiler_params=SMALL,
            name=kernel.__name__,
        )(*args)

    scalars = (term_class, term_id, pair_table, block_dims.T, mpo_coef)
    operands = [
        pltpu.with_memory_space_constraint(x, pltpu.HBM)
        for x in (*scalars, wave_blocks, left_env, right_env)
    ]
    lead_shape = like(targets, 2 * a_rows + 2 * (strip + 2 * b_rows))
    rest_shape = like(targets, 2 * strip + 2 * a_rows)
    scalar_room = [pltpu.SMEM(scalar.shape, scalar.dtype) for scalar in scalars]
    limit = pltpu.CompilerParams(vmem_limit_bytes=16 * 1024 * 1024)
    half_shape = jax.ShapeDtypeStruct((terms, width, width), jnp.bfloat16)
    right_shape = jax.ShapeDtypeStruct((terms, 2 * strip, width), jnp.bfloat16)
    lead_send, rest_send, half, keep_right = pl.pallas_call(
        send_kernel,
        out_shape=[lead_shape, rest_shape, half_shape, right_shape],
        in_specs=[hbm] * 8,
        out_specs=[vmem] * 4,
        scratch_shapes=scalar_room
        + [
            pltpu.VMEM((width, width), jnp.bfloat16),
            pltpu.VMEM((terms, width, width), jnp.bfloat16),
            pltpu.VMEM((terms, 2 * strip, width), jnp.bfloat16),
            pltpu.SemaphoreType.DMA((len(scalars),)),
            pltpu.SemaphoreType.DMA,
            pltpu.SemaphoreType.DMA((terms,)),
            pltpu.SemaphoreType.DMA((terms,)),
            pltpu.SemaphoreType.DMA,
        ],
        compiler_params=limit,
        cost_estimate=pl.CostEstimate(
            flops=3 * terms * width**3, bytes_accessed=4 * 1024 * 1024, transcendentals=0
        ),
        name="send_kernel",
    )(*operands)
    lead_keep, rest_keep, mask = pl.pallas_call(
        keep_kernel,
        out_shape=[lead_shape, rest_shape, like(targets, strip)],
        in_specs=[hbm] * len(scalars) + [vmem] * 2,
        out_specs=[vmem] * 3,
        scratch_shapes=scalar_room + [pltpu.SemaphoreType.DMA((len(scalars),))],
        compiler_params=limit,
        cost_estimate=pl.CostEstimate(
            flops=3 * terms * width**3, bytes_accessed=0, transcendentals=0
        ),
        name="keep_kernel",
    )(*operands[: len(scalars)], half, keep_right)
    lead_recv = swap(lead_send, "mpo", 1)
    part = like(2, targets, b_rows)
    rest_send, far, one, one_near, two, three = call(
        lead_kernel,
        [rest_shape, like(targets, 2 * a_rows)] + [like(targets, strip)] * 2 + [part] * 2,
        lead_keep,
        lead_recv,
        rest_send,
        aliases={2: 0},
        span=3,
    )
    cross = swap(far, "mpo", 2)
    one, two, three = [swap(x, "sec", q) for x, q in ((one, 1), (two, 2), (three, 3))]
    rest_recv = swap(rest_send, "mpo", 1)
    one_near, *own = call(
        own_kernel,
        [like(targets, strip)] + [like(targets, a_rows)] * 2,
        rest_keep,
        rest_recv,
        cross,
        one_near,
        aliases={3: 0},
        span=3,
    )
    near = jax.ShapeDtypeStruct((targets, strip, strip), jnp.float32)
    here, near = call(
        here_kernel,
        [like(targets, strip), near],
        rest_keep,
        rest_recv,
        one,
        two,
        three,
        own[0],
        span=3,
    )
    own = [swap(array, "sec", q) for array, q in zip(own, (2, 3))]
    one_near = swap(one_near, "sec", 1)
    here = swap(here, "mpo", 2)
    far_sum = jax.ShapeDtypeStruct((targets, a_rows, strip), jnp.float32)
    far_sum = call(far_sum_kernel, far_sum, *own, span=3)
    return call(final_kernel, like(targets, strip), mask, near, one_near, here, far_sum)


def by_classes(
    wave_blocks, left_env, right_env, term_class, term_id, block_dims, pair_table, mpo_coef
):
    sec_count = lax.axis_size("sec")
    mpo_count = lax.axis_size("mpo")
    local_blocks = wave_blocks.shape[0]
    block_width = wave_blocks.shape[1]
    total_blocks = block_dims.shape[0]
    classes = pair_table.shape[1]
    tile_states = block_width // 8
    positions = jnp.arange(block_width)
    first = lax.axis_index("sec") * local_blocks
    own_dims = lax.dynamic_slice_in_dim(block_dims, first, local_blocks, 0)
    row_ok = positions[None, :] < own_dims[:, 0:1] * tile_states
    col_ok = positions[None, :] < own_dims[:, 1:2] * tile_states
    masked = jnp.where(
        row_ok[:, :, None] & col_ok[:, None, :], wave_blocks, jnp.zeros_like(wave_blocks)
    )
    left_part = jnp.einsum(
        "bjxy,byz->bjxz", left_env, masked, preferred_element_type=jnp.float32
    ).astype(jnp.bfloat16)
    contrib = jnp.einsum(
        "bjxz,bjwz->bjxw", left_part, right_env, preferred_element_type=jnp.float32
    )
    weights = jnp.sum(
        jnp.where(
            term_id[:, :, None] == jnp.arange(mpo_coef.shape[0])[None, None, :],
            mpo_coef[None, None, :],
            0.0,
        ),
        axis=-1,
    )
    picks = (term_class[:, :, None] == jnp.arange(classes)[None, None, :]).astype(
        jnp.float32
    ) * weights[:, :, None]
    grouped = jnp.einsum("bjc,bjxw->bcxw", picks, contrib, precision=lax.Precision.HIGHEST).astype(
        jnp.bfloat16
    )
    targets = pair_table.reshape(-1)
    routing = targets[None, :] == jnp.arange(total_blocks)[:, None]
    strip_rows = block_width // sec_count
    strip_cols = block_width // mpo_count
    outgoing = grouped.reshape(local_blocks * classes, block_width, block_width)
    arrived = lax.all_to_all(
        lax.all_to_all(outgoing, "sec", split_axis=1, concat_axis=0, tiled=True),
        "mpo",
        split_axis=2,
        concat_axis=0,
        tiled=True,
    )
    arrived = arrived.reshape(mpo_count, total_blocks * classes, strip_rows, strip_cols)
    summed = jnp.einsum(
        "tk,mkrw->trw", routing.astype(jnp.bfloat16), arrived, preferred_element_type=jnp.float32
    )
    row_index = lax.axis_index("sec") * strip_rows + jnp.arange(strip_rows)
    col_index = lax.axis_index("mpo") * strip_cols + jnp.arange(strip_cols)
    rows_in = row_index[None, :] < block_dims[:, 0:1] * tile_states
    cols_in = col_index[None, :] < block_dims[:, 1:2] * tile_states
    inside = rows_in[:, :, None] & cols_in[:, None, :]
    return jnp.where(inside, summed, 0.0).astype(jnp.bfloat16)


def solution(mesh):
    placed = (
        P(("grp", "sec"), None, None),
        P(("grp", "sec"), "mpo", None, None),
        P(("grp", "sec"), "mpo", None, None),
        P(("grp", "sec"), "mpo"),
        P(("grp", "sec"), "mpo"),
        P("grp", None),
        P("grp", None),
        P(),
    )

    def on_device(*arrays):
        wave_blocks, block_dims = arrays[0], arrays[5]
        small = wave_blocks.shape[0] == 1 and block_dims.shape[0] == 4
        if small and mesh.shape["sec"] == 4 and mesh.shape["mpo"] == 4:
            return by_targets(*arrays)
        return by_classes(*arrays)

    return jax.shard_map(
        on_device, mesh=mesh, in_specs=placed, out_specs=P("grp", "sec", "mpo"), check_vma=False
    )
```

```python
import functools

import jax
import jax.numpy as jnp
from jax import lax
from jax.experimental import pallas as pl
from jax.experimental.pallas import tpu as pltpu
from jax.sharding import PartitionSpec as P

COLUMN_ORDER = (3, 1, 2, 0)
SMALL = pltpu.CompilerParams(vmem_limit_bytes=4 * 1024 * 1024)


def send_kernel(
    cls_hbm,
    tid_hbm,
    pair_hbm,
    dims_hbm,
    coef_hbm,
    wave_hbm,
    left_hbm,
    right_hbm,
    lead_ref,
    rest_ref,
    half_ref,
    keep_right,
    cls,
    tid,
    pair,
    dims,
    coef,
    wave,
    left,
    right,
    scalar_sems,
    wave_sem,
    left_sems,
    right_sems,
    keep_sem,
):
    width = wave.shape[0]
    terms = left.shape[0]
    strip = width // 4
    unit = width // 8
    sec = lax.axis_index("sec")
    mpo = lax.axis_index("mpo")

    scalars = [
        pltpu.make_async_copy(src, dst, scalar_sems.at[n])
        for n, (src, dst) in enumerate(
            ((cls_hbm, cls), (tid_hbm, tid), (pair_hbm, pair), (dims_hbm, dims), (coef_hbm, coef))
        )
    ]
    wave_copy = pltpu.make_async_copy(wave_hbm.at[0], wave, wave_sem)
    wave_copy.start()
    for copy in scalars:
        copy.start()

    def fetch(j, carry):
        for q in range(4):
            src = pl.multiple_of((sec ^ q) * strip, strip)
            pltpu.make_async_copy(
                left_hbm.at[0, j, pl.ds(src, strip)],
                left.at[j, pl.ds(q * strip, strip)],
                left_sems.at[j],
            ).start()
        for p, r in enumerate(COLUMN_ORDER[:2]):
            src = pl.multiple_of((mpo ^ r) * strip, strip)
            pltpu.make_async_copy(
                right_hbm.at[0, j, pl.ds(src, strip)],
                right.at[j, pl.ds(p * strip, strip)],
                right_sems.at[j],
            ).start()
        return carry

    def fetch_keep(j, carry):
        for p, r in enumerate(COLUMN_ORDER[2:]):
            src = pl.multiple_of((mpo ^ r) * strip, strip)
            pltpu.make_async_copy(
                right_hbm.at[0, j, pl.ds(src, strip)],
                keep_right.at[j, pl.ds(p * strip, strip)],
                keep_sem,
            ).start()
        return carry

    lax.fori_loop(0, terms, fetch, 0)
    lax.fori_loop(0, terms, fetch_keep, 0)
    clear(lead_ref, rest_ref)
    for copy in scalars:
        copy.wait()
    wave_copy.wait()
    row_limit = dims[0, sec] * unit
    col_limit = dims[1, sec] * unit

    def mask(i, carry):
        base = pl.multiple_of(i * 64, 64)
        row_pos = base + lax.broadcasted_iota(jnp.int32, (64, width), 0)
        col_pos = lax.broadcasted_iota(jnp.int32, (64, width), 1)
        inside = (row_pos < row_limit) & (col_pos < col_limit)
        band = wave[pl.ds(base, 64), :].astype(jnp.float32)
        wave[pl.ds(base, 64), :] = jnp.where(inside, band, 0.0).astype(jnp.bfloat16)
        return carry

    lax.fori_loop(0, width // 64, mask, 0)
    for j in range(terms):
        pltpu.make_async_copy(left_hbm.at[0, j], left.at[j], left_sems.at[j]).wait()
        half = jnp.dot(left[j], wave[...], preferred_element_type=jnp.float32)
        half = half.astype(jnp.bfloat16)
        half_ref[j] = half
        pltpu.make_async_copy(
            right_hbm.at[0, j, pl.ds(0, 2 * strip)], right.at[j], right_sems.at[j]
        ).wait()
        spread(lead_ref, rest_ref, half, right[j], pair[sec, cls[0, j]], coef[tid[0, j]])
    pltpu.make_async_copy(
        right_hbm.at[0, pl.ds(0, terms), pl.ds(0, 2 * strip)], keep_right, keep_sem
    ).wait()


def keep_kernel(
    cls_hbm,
    tid_hbm,
    pair_hbm,
    dims_hbm,
    coef_hbm,
    half_ref,
    right_ref,
    lead_ref,
    rest_ref,
    mask_ref,
    cls,
    tid,
    pair,
    dims,
    coef,
    scalar_sems,
):
    terms, width, _ = half_ref.shape
    targets, strip, _ = mask_ref.shape
    unit = width // 8
    sec = lax.axis_index("sec")
    mpo = lax.axis_index("mpo")
    scalars = [
        pltpu.make_async_copy(src, dst, scalar_sems.at[n])
        for n, (src, dst) in enumerate(
            ((cls_hbm, cls), (tid_hbm, tid), (pair_hbm, pair), (dims_hbm, dims), (coef_hbm, coef))
        )
    ]
    for copy in scalars:
        copy.start()
    clear(lead_ref, rest_ref)
    for copy in scalars:
        copy.wait()
    for j in range(terms):
        spread(
            lead_ref, rest_ref, half_ref[j], right_ref[j], pair[sec, cls[0, j]], coef[tid[0, j]]
        )
    lane = mpo * strip + lax.broadcasted_iota(jnp.int32, (strip, strip), 1)
    line = sec * strip + lax.broadcasted_iota(jnp.int32, (strip, strip), 0)

    def target_mask(t, carry):
        inside = (line < dims[0, t] * unit) & (lane < dims[1, t] * unit)
        mask_ref[t] = jnp.where(inside, 1.0, 0.0).astype(jnp.bfloat16)
        return carry

    lax.fori_loop(0, targets, target_mask, 0)


def clear(*refs):
    def one(t, carry):
        for ref in refs:
            ref[t] = jnp.zeros(ref.shape[1:], ref.dtype)
        return carry

    lax.fori_loop(0, refs[0].shape[0], one, 0)


def spread(lead, rest, half, right, t, weight):
    contrib = lax.dot_general(
        half, right, (((1,), (1,)), ((), ())), preferred_element_type=jnp.float32
    )
    strip = contrib.shape[1] // 2
    a_rows = (rest.shape[1] - 2 * strip) // 2
    b_rows = strip - a_rows
    soon = (2 * a_rows, 2 * a_rows + strip + 2 * b_rows)
    for q in range(4):
        for n in range(2):
            value = weight * contrib[q * strip : (q + 1) * strip, n * strip : (n + 1) * strip]
            if q == 0:
                put(rest, t, n * strip, value)
            elif q == 1:
                put(lead, t, soon[n], value)
            else:
                if n == 0:
                    put(lead, t, (q - 2) * a_rows, value[:a_rows])
                else:
                    put(rest, t, 2 * strip + (q - 2) * a_rows, value[:a_rows])
                put(lead, t, soon[n] + strip + (q - 2) * b_rows, value[a_rows:])


def put(ref, t, row, value):
    at = slice(row, row + value.shape[0])
    ref[t, at, :] = (ref[t, at, :].astype(jnp.float32) + value).astype(jnp.bfloat16)


def lead_kernel(keep_ref, recv_ref, rest_in, rest_out, far_ref, one_far, one_near, *own_refs):
    del rest_in, rest_out
    row = far_ref.shape[1]
    far_ref[...] = add(keep_ref[:, :row, :], recv_ref[:, :row, :])
    for n, one_ref in enumerate((one_far, one_near)):
        at = slice(row, row + one_ref.shape[1])
        one_ref[...] = add(keep_ref[:, at, :], recv_ref[:, at, :])
        row += one_ref.shape[1]
        for own_ref in own_refs:
            at = slice(row, row + own_ref.shape[2])
            own_ref[n] = add(keep_ref[:, at, :], recv_ref[:, at, :])
            row += own_ref.shape[2]


def own_kernel(keep_ref, recv_ref, cross_ref, later_in, later_out, *own_refs):
    del later_in, later_out
    rows = own_refs[0].shape[1]
    row = keep_ref.shape[1] - 2 * rows
    for n, own_ref in enumerate(own_refs):
        at = slice(row + n * rows, row + (n + 1) * rows)
        own_ref[...] = add(
            keep_ref[:, at, :], recv_ref[:, at, :], cross_ref[:, n * rows : (n + 1) * rows, :]
        )


def here_kernel(keep_ref, recv_ref, one_ref, two_ref, three_ref, after_ref, far_ref, near_ref):
    del after_ref
    strip = far_ref.shape[1]
    a_rows = strip - two_ref.shape[2]
    for n, out_ref in enumerate((far_ref, near_ref)):
        for first, last in ((0, a_rows), (a_rows, strip)):
            at = slice(n * strip + first, n * strip + last)
            parts = [keep_ref[:, at, :], recv_ref[:, at, :]]
            if n == 0:
                parts += [one_ref[:, first:last, :]]
            if first:
                parts += [two_ref[n], three_ref[n]]
            out_ref[:, first:last, :] = total(*parts).astype(out_ref.dtype)


def far_sum_kernel(two_ref, three_ref, sum_ref):
    sum_ref[...] = total(two_ref[...], three_ref[...])


def final_kernel(mask_ref, near_ref, one_ref, cross_ref, sum_ref, out_ref):
    a_rows, strip = sum_ref.shape[1], out_ref.shape[1]
    for first, last in ((0, a_rows), (a_rows, strip)):
        parts = [ref[:, first:last, :] for ref in (near_ref, one_ref, cross_ref)]
        if not first:
            parts += [sum_ref[...]]
        inside = mask_ref[:, first:last, :].astype(jnp.float32) > 0.0
        out_ref[:, first:last, :] = jnp.where(inside, total(*parts), 0.0).astype(jnp.bfloat16)


def total(*arrays):
    result = arrays[0].astype(jnp.float32)
    for array in arrays[1:]:
        result = result + array.astype(jnp.float32)
    return result


def add(*arrays):
    return total(*arrays).astype(jnp.bfloat16)


def swap(array, axis, mask):
    return lax.ppermute(array, axis, [(i, i ^ mask) for i in range(lax.axis_size(axis))])


def by_targets(
    wave_blocks, left_env, right_env, term_class, term_id, block_dims, pair_table, mpo_coef
):
    width = wave_blocks.shape[1]
    terms = left_env.shape[1]
    targets = block_dims.shape[0]
    strip = width // 4
    a_rows = strip * 5 // 8
    b_rows = strip - a_rows
    vmem = pl.BlockSpec(memory_space=pltpu.VMEM)
    hbm = pl.BlockSpec(memory_space=pltpu.HBM)

    def like(*shape):
        return jax.ShapeDtypeStruct(shape + (strip,), jnp.bfloat16)

    def call(kernel, out_shape, *args, aliases={}, span=0.1):
        return pl.pallas_call(
            kernel,
            out_shape=out_shape,
            in_specs=[vmem] * len(args),
            out_specs=jax.tree.map(lambda _: vmem, out_shape),
            input_output_aliases=aliases,
            cost_estimate=pl.CostEstimate(
                flops=round(span * 1e9), bytes_accessed=0, transcendentals=0
            ),
            compiler_params=SMALL,
            name=kernel.__name__,
        )(*args)

    scalars = (term_class, term_id, pair_table, block_dims.T, mpo_coef)
    operands = [
        pltpu.with_memory_space_constraint(x, pltpu.HBM)
        for x in (*scalars, wave_blocks, left_env, right_env)
    ]
    lead_shape = like(targets, 2 * a_rows + 2 * (strip + 2 * b_rows))
    rest_shape = like(targets, 2 * strip + 2 * a_rows)
    scalar_room = [pltpu.SMEM(scalar.shape, scalar.dtype) for scalar in scalars]
    limit = pltpu.CompilerParams(vmem_limit_bytes=16 * 1024 * 1024)
    half_shape = jax.ShapeDtypeStruct((terms, width, width), jnp.bfloat16)
    right_shape = jax.ShapeDtypeStruct((terms, 2 * strip, width), jnp.bfloat16)
    lead_send, rest_send, half, keep_right = pl.pallas_call(
        send_kernel,
        out_shape=[lead_shape, rest_shape, half_shape, right_shape],
        in_specs=[hbm] * 8,
        out_specs=[vmem] * 4,
        scratch_shapes=scalar_room
        + [
            pltpu.VMEM((width, width), jnp.bfloat16),
            pltpu.VMEM((terms, width, width), jnp.bfloat16),
            pltpu.VMEM((terms, 2 * strip, width), jnp.bfloat16),
            pltpu.SemaphoreType.DMA((len(scalars),)),
            pltpu.SemaphoreType.DMA,
            pltpu.SemaphoreType.DMA((terms,)),
            pltpu.SemaphoreType.DMA((terms,)),
            pltpu.SemaphoreType.DMA,
        ],
        compiler_params=limit,
        cost_estimate=pl.CostEstimate(
            flops=3 * terms * width**3, bytes_accessed=4 * 1024 * 1024, transcendentals=0
        ),
        name="send_kernel",
    )(*operands)
    lead_keep, rest_keep, mask = pl.pallas_call(
        keep_kernel,
        out_shape=[lead_shape, rest_shape, like(targets, strip)],
        in_specs=[hbm] * len(scalars) + [vmem] * 2,
        out_specs=[vmem] * 3,
        scratch_shapes=scalar_room + [pltpu.SemaphoreType.DMA((len(scalars),))],
        compiler_params=limit,
        cost_estimate=pl.CostEstimate(
            flops=3 * terms * width**3, bytes_accessed=0, transcendentals=0
        ),
        name="keep_kernel",
    )(*operands[: len(scalars)], half, keep_right)
    lead_recv = swap(lead_send, "mpo", 1)
    part = like(2, targets, b_rows)
    rest_send, far, one, one_near, two, three = call(
        lead_kernel,
        [rest_shape, like(targets, 2 * a_rows)] + [like(targets, strip)] * 2 + [part] * 2,
        lead_keep,
        lead_recv,
        rest_send,
        aliases={2: 0},
        span=3,
    )
    cross = swap(far, "mpo", 2)
    one, two, three = [swap(x, "sec", q) for x, q in ((one, 1), (two, 2), (three, 3))]
    rest_recv = swap(rest_send, "mpo", 1)
    one_near, *own = call(
        own_kernel,
        [like(targets, strip)] + [like(targets, a_rows)] * 2,
        rest_keep,
        rest_recv,
        cross,
        one_near,
        aliases={3: 0},
        span=3,
    )
    near = jax.ShapeDtypeStruct((targets, strip, strip), jnp.float32)
    here, near = call(
        here_kernel,
        [like(targets, strip), near],
        rest_keep,
        rest_recv,
        one,
        two,
        three,
        own[0],
        span=3,
    )
    own = [swap(array, "sec", q) for array, q in zip(own, (2, 3))]
    one_near = swap(one_near, "sec", 1)
    here = swap(here, "mpo", 2)
    far_sum = jax.ShapeDtypeStruct((targets, a_rows, strip), jnp.float32)
    far_sum = call(far_sum_kernel, far_sum, *own, span=3)
    return call(final_kernel, like(targets, strip), mask, near, one_near, here, far_sum)


def by_classes(
    wave_blocks, left_env, right_env, term_class, term_id, block_dims, pair_table, mpo_coef
):
    sec_count = lax.axis_size("sec")
    mpo_count = lax.axis_size("mpo")
    local_blocks = wave_blocks.shape[0]
    block_width = wave_blocks.shape[1]
    total_blocks = block_dims.shape[0]
    classes = pair_table.shape[1]
    tile_states = block_width // 8
    positions = jnp.arange(block_width)
    first = lax.axis_index("sec") * local_blocks
    own_dims = lax.dynamic_slice_in_dim(block_dims, first, local_blocks, 0)
    row_ok = positions[None, :] < own_dims[:, 0:1] * tile_states
    col_ok = positions[None, :] < own_dims[:, 1:2] * tile_states
    masked = jnp.where(
        row_ok[:, :, None] & col_ok[:, None, :], wave_blocks, jnp.zeros_like(wave_blocks)
    )
    left_part = jnp.einsum(
        "bjxy,byz->bjxz", left_env, masked, preferred_element_type=jnp.float32
    ).astype(jnp.bfloat16)
    contrib = jnp.einsum(
        "bjxz,bjwz->bjxw", left_part, right_env, preferred_element_type=jnp.float32
    )
    weights = jnp.sum(
        jnp.where(
            term_id[:, :, None] == jnp.arange(mpo_coef.shape[0])[None, None, :],
            mpo_coef[None, None, :],
            0.0,
        ),
        axis=-1,
    )
    picks = (term_class[:, :, None] == jnp.arange(classes)[None, None, :]).astype(
        jnp.float32
    ) * weights[:, :, None]
    grouped = jnp.einsum("bjc,bjxw->bcxw", picks, contrib, precision=lax.Precision.HIGHEST).astype(
        jnp.bfloat16
    )
    targets = pair_table.reshape(-1)
    routing = targets[None, :] == jnp.arange(total_blocks)[:, None]
    strip_rows = block_width // sec_count
    strip_cols = block_width // mpo_count
    outgoing = grouped.reshape(local_blocks * classes, block_width, block_width)
    arrived = lax.all_to_all(
        lax.all_to_all(outgoing, "sec", split_axis=1, concat_axis=0, tiled=True),
        "mpo",
        split_axis=2,
        concat_axis=0,
        tiled=True,
    )
    arrived = arrived.reshape(mpo_count, total_blocks * classes, strip_rows, strip_cols)
    summed = jnp.einsum(
        "tk,mkrw->trw", routing.astype(jnp.bfloat16), arrived, preferred_element_type=jnp.float32
    )
    row_index = lax.axis_index("sec") * strip_rows + jnp.arange(strip_rows)
    col_index = lax.axis_index("mpo") * strip_cols + jnp.arange(strip_cols)
    rows_in = row_index[None, :] < block_dims[:, 0:1] * tile_states
    cols_in = col_index[None, :] < block_dims[:, 1:2] * tile_states
    inside = rows_in[:, :, None] & cols_in[:, None, :]
    return jnp.where(inside, summed, 0.0).astype(jnp.bfloat16)


def solution(mesh):
    placed = (
        P(("grp", "sec"), None, None),
        P(("grp", "sec"), "mpo", None, None),
        P(("grp", "sec"), "mpo", None, None),
        P(("grp", "sec"), "mpo"),
        P(("grp", "sec"), "mpo"),
        P("grp", None),
        P("grp", None),
        P(),
    )

    def on_device(*arrays):
        wave_blocks, block_dims = arrays[0], arrays[5]
        small = wave_blocks.shape[0] == 1 and block_dims.shape[0] == 4
        if small and mesh.shape["sec"] == 4 and mesh.shape["mpo"] == 4:
            return by_targets(*arrays)
        return by_classes(*arrays)

    return jax.shard_map(
        on_device, mesh=mesh, in_specs=placed, out_specs=P("grp", "sec", "mpo"), check_vma=False
    )
```

```python
import functools

import jax
import jax.numpy as jnp
from jax import lax
from jax.experimental import pallas as pl
from jax.experimental.pallas import tpu as pltpu
from jax.sharding import PartitionSpec as P

COLUMN_ORDER = (3, 1, 2, 0)
SMALL = pltpu.CompilerParams(vmem_limit_bytes=4 * 1024 * 1024)


def send_kernel(
    cls_hbm,
    tid_hbm,
    pair_hbm,
    dims_hbm,
    coef_hbm,
    wave_hbm,
    left_hbm,
    right_hbm,
    lead_ref,
    rest_ref,
    half_ref,
    keep_right,
    cls,
    tid,
    pair,
    dims,
    coef,
    wave,
    left,
    right,
    scalar_sems,
    wave_sem,
    left_sems,
    right_sems,
    keep_sem,
):
    width = wave.shape[0]
    terms = left.shape[0]
    strip = width // 4
    unit = width // 8
    sec = lax.axis_index("sec")
    mpo = lax.axis_index("mpo")

    scalars = [
        pltpu.make_async_copy(src, dst, scalar_sems.at[n])
        for n, (src, dst) in enumerate(
            ((cls_hbm, cls), (tid_hbm, tid), (pair_hbm, pair), (dims_hbm, dims), (coef_hbm, coef))
        )
    ]
    wave_copy = pltpu.make_async_copy(wave_hbm.at[0], wave, wave_sem)
    wave_copy.start()
    for copy in scalars:
        copy.start()

    def fetch(j, carry):
        for q in range(4):
            src = pl.multiple_of((sec ^ q) * strip, strip)
            pltpu.make_async_copy(
                left_hbm.at[0, j, pl.ds(src, strip)],
                left.at[j, pl.ds(q * strip, strip)],
                left_sems.at[j],
            ).start()
        for p, r in enumerate(COLUMN_ORDER[:2]):
            src = pl.multiple_of((mpo ^ r) * strip, strip)
            pltpu.make_async_copy(
                right_hbm.at[0, j, pl.ds(src, strip)],
                right.at[j, pl.ds(p * strip, strip)],
                right_sems.at[j],
            ).start()
        return carry

    def fetch_keep(j, carry):
        for p, r in enumerate(COLUMN_ORDER[2:]):
            src = pl.multiple_of((mpo ^ r) * strip, strip)
            pltpu.make_async_copy(
                right_hbm.at[0, j, pl.ds(src, strip)],
                keep_right.at[j, pl.ds(p * strip, strip)],
                keep_sem,
            ).start()
        return carry

    lax.fori_loop(0, terms, fetch, 0)
    lax.fori_loop(0, terms, fetch_keep, 0)
    clear(lead_ref, rest_ref)
    for copy in scalars:
        copy.wait()
    wave_copy.wait()
    row_limit = dims[0, sec] * unit
    col_limit = dims[1, sec] * unit

    def mask(i, carry):
        base = pl.multiple_of(i * 64, 64)
        row_pos = base + lax.broadcasted_iota(jnp.int32, (64, width), 0)
        col_pos = lax.broadcasted_iota(jnp.int32, (64, width), 1)
        inside = (row_pos < row_limit) & (col_pos < col_limit)
        band = wave[pl.ds(base, 64), :].astype(jnp.float32)
        wave[pl.ds(base, 64), :] = jnp.where(inside, band, 0.0).astype(jnp.bfloat16)
        return carry

    lax.fori_loop(0, width // 64, mask, 0)
    for j in range(terms):
        pltpu.make_async_copy(left_hbm.at[0, j], left.at[j], left_sems.at[j]).wait()
        half = jnp.dot(left[j], wave[...], preferred_element_type=jnp.float32)
        half = half.astype(jnp.bfloat16)
        half_ref[j] = half
        pltpu.make_async_copy(
            right_hbm.at[0, j, pl.ds(0, 2 * strip)], right.at[j], right_sems.at[j]
        ).wait()
        spread(lead_ref, rest_ref, half, right[j], pair[sec, cls[0, j]], coef[tid[0, j]])
    pltpu.make_async_copy(
        right_hbm.at[0, pl.ds(0, terms), pl.ds(0, 2 * strip)], keep_right, keep_sem
    ).wait()


def keep_kernel(
    cls_hbm,
    tid_hbm,
    pair_hbm,
    dims_hbm,
    coef_hbm,
    half_ref,
    right_ref,
    lead_ref,
    rest_ref,
    mask_ref,
    cls,
    tid,
    pair,
    dims,
    coef,
    scalar_sems,
):
    terms, width, _ = half_ref.shape
    targets, strip, _ = mask_ref.shape
    unit = width // 8
    sec = lax.axis_index("sec")
    mpo = lax.axis_index("mpo")
    scalars = [
        pltpu.make_async_copy(src, dst, scalar_sems.at[n])
        for n, (src, dst) in enumerate(
            ((cls_hbm, cls), (tid_hbm, tid), (pair_hbm, pair), (dims_hbm, dims), (coef_hbm, coef))
        )
    ]
    for copy in scalars:
        copy.start()
    clear(lead_ref, rest_ref)
    for copy in scalars:
        copy.wait()
    for j in range(terms):
        spread(
            lead_ref, rest_ref, half_ref[j], right_ref[j], pair[sec, cls[0, j]], coef[tid[0, j]]
        )
    lane = mpo * strip + lax.broadcasted_iota(jnp.int32, (strip, strip), 1)
    line = sec * strip + lax.broadcasted_iota(jnp.int32, (strip, strip), 0)

    def target_mask(t, carry):
        inside = (line < dims[0, t] * unit) & (lane < dims[1, t] * unit)
        mask_ref[t] = jnp.where(inside, 1.0, 0.0).astype(jnp.bfloat16)
        return carry

    lax.fori_loop(0, targets, target_mask, 0)


def clear(*refs):
    def one(t, carry):
        for ref in refs:
            ref[t] = jnp.zeros(ref.shape[1:], ref.dtype)
        return carry

    lax.fori_loop(0, refs[0].shape[0], one, 0)


def spread(lead, rest, half, right, t, weight):
    contrib = lax.dot_general(
        half, right, (((1,), (1,)), ((), ())), preferred_element_type=jnp.float32
    )
    strip = contrib.shape[1] // 2
    a_rows = (rest.shape[1] - 2 * strip) // 2
    b_rows = strip - a_rows
    soon = (2 * a_rows, 2 * a_rows + strip + 2 * b_rows)
    for q in range(4):
        for n in range(2):
            value = weight * contrib[q * strip : (q + 1) * strip, n * strip : (n + 1) * strip]
            if q == 0:
                put(rest, t, n * strip, value)
            elif q == 1:
                put(lead, t, soon[n], value)
            else:
                if n == 0:
                    put(lead, t, (q - 2) * a_rows, value[:a_rows])
                else:
                    put(rest, t, 2 * strip + (q - 2) * a_rows, value[:a_rows])
                put(lead, t, soon[n] + strip + (q - 2) * b_rows, value[a_rows:])


def put(ref, t, row, value):
    at = slice(row, row + value.shape[0])
    ref[t, at, :] = (ref[t, at, :].astype(jnp.float32) + value).astype(jnp.bfloat16)


def lead_kernel(keep_ref, recv_ref, rest_in, rest_out, far_ref, one_far, one_near, *own_refs):
    del rest_in, rest_out
    row = far_ref.shape[1]
    far_ref[...] = add(keep_ref[:, :row, :], recv_ref[:, :row, :])
    for n, one_ref in enumerate((one_far, one_near)):
        at = slice(row, row + one_ref.shape[1])
        one_ref[...] = add(keep_ref[:, at, :], recv_ref[:, at, :])
        row += one_ref.shape[1]
        for own_ref in own_refs:
            at = slice(row, row + own_ref.shape[2])
            own_ref[n] = add(keep_ref[:, at, :], recv_ref[:, at, :])
            row += own_ref.shape[2]


def own_kernel(keep_ref, recv_ref, cross_ref, later_in, later_out, *own_refs):
    del later_in, later_out
    rows = own_refs[0].shape[1]
    row = keep_ref.shape[1] - 2 * rows
    for n, own_ref in enumerate(own_refs):
        at = slice(row + n * rows, row + (n + 1) * rows)
        own_ref[...] = add(
            keep_ref[:, at, :], recv_ref[:, at, :], cross_ref[:, n * rows : (n + 1) * rows, :]
        )


def here_kernel(keep_ref, recv_ref, one_ref, two_ref, three_ref, after_ref, far_ref, near_ref):
    del after_ref
    strip = far_ref.shape[1]
    a_rows = strip - two_ref.shape[2]
    for n, out_ref in enumerate((far_ref, near_ref)):
        for first, last in ((0, a_rows), (a_rows, strip)):
            at = slice(n * strip + first, n * strip + last)
            parts = [keep_ref[:, at, :], recv_ref[:, at, :]]
            if n == 0:
                parts += [one_ref[:, first:last, :]]
            if first:
                parts += [two_ref[n], three_ref[n]]
            out_ref[:, first:last, :] = total(*parts).astype(out_ref.dtype)


def far_sum_kernel(two_ref, three_ref, sum_ref):
    sum_ref[...] = total(two_ref[...], three_ref[...])


def final_kernel(mask_ref, near_ref, one_ref, cross_ref, sum_ref, out_hbm, out, sems):
    a_rows, (targets, strip, _) = sum_ref.shape[1], out.shape
    copies = []
    for t in range(targets):
        for first, last in ((0, a_rows), (a_rows, strip)):
            parts = [ref[t, first:last, :] for ref in (near_ref, one_ref, cross_ref)]
            if not first:
                parts += [sum_ref[t]]
            inside = mask_ref[t, first:last, :].astype(jnp.float32) > 0.0
            out[t, first:last, :] = jnp.where(inside, total(*parts), 0.0).astype(jnp.bfloat16)
        copy = pltpu.make_async_copy(out.at[t], out_hbm.at[t], sems.at[t])
        copy.start()
        copies.append(copy)
    for copy in copies:
        copy.wait()


def total(*arrays):
    result = arrays[0].astype(jnp.float32)
    for array in arrays[1:]:
        result = result + array.astype(jnp.float32)
    return result


def add(*arrays):
    return total(*arrays).astype(jnp.bfloat16)


def swap(array, axis, mask):
    return lax.ppermute(array, axis, [(i, i ^ mask) for i in range(lax.axis_size(axis))])


def by_targets(
    wave_blocks, left_env, right_env, term_class, term_id, block_dims, pair_table, mpo_coef
):
    width = wave_blocks.shape[1]
    terms = left_env.shape[1]
    targets = block_dims.shape[0]
    strip = width // 4
    a_rows = strip * 3 // 4
    b_rows = strip - a_rows
    vmem = pl.BlockSpec(memory_space=pltpu.VMEM)
    hbm = pl.BlockSpec(memory_space=pltpu.HBM)

    def like(*shape):
        return jax.ShapeDtypeStruct(shape + (strip,), jnp.bfloat16)

    def call(kernel, out_shape, *args, aliases={}, span=0.1):
        return pl.pallas_call(
            kernel,
            out_shape=out_shape,
            in_specs=[vmem] * len(args),
            out_specs=jax.tree.map(lambda _: vmem, out_shape),
            input_output_aliases=aliases,
            cost_estimate=pl.CostEstimate(
                flops=round(span * 1e9), bytes_accessed=0, transcendentals=0
            ),
            compiler_params=SMALL,
            name=kernel.__name__,
        )(*args)

    scalars = (term_class, term_id, pair_table, block_dims.T, mpo_coef)
    operands = [
        pltpu.with_memory_space_constraint(x, pltpu.HBM)
        for x in (*scalars, wave_blocks, left_env, right_env)
    ]
    lead_shape = like(targets, 2 * a_rows + 2 * (strip + 2 * b_rows))
    rest_shape = like(targets, 2 * strip + 2 * a_rows)
    scalar_room = [pltpu.SMEM(scalar.shape, scalar.dtype) for scalar in scalars]
    limit = pltpu.CompilerParams(vmem_limit_bytes=16 * 1024 * 1024)
    half_shape = jax.ShapeDtypeStruct((terms, width, width), jnp.bfloat16)
    right_shape = jax.ShapeDtypeStruct((terms, 2 * strip, width), jnp.bfloat16)
    lead_send, rest_send, half, keep_right = pl.pallas_call(
        send_kernel,
        out_shape=[lead_shape, rest_shape, half_shape, right_shape],
        in_specs=[hbm] * 8,
        out_specs=[vmem] * 4,
        scratch_shapes=scalar_room
        + [
            pltpu.VMEM((width, width), jnp.bfloat16),
            pltpu.VMEM((terms, width, width), jnp.bfloat16),
            pltpu.VMEM((terms, 2 * strip, width), jnp.bfloat16),
            pltpu.SemaphoreType.DMA((len(scalars),)),
            pltpu.SemaphoreType.DMA,
            pltpu.SemaphoreType.DMA((terms,)),
            pltpu.SemaphoreType.DMA((terms,)),
            pltpu.SemaphoreType.DMA,
        ],
        compiler_params=limit,
        cost_estimate=pl.CostEstimate(
            flops=3 * terms * width**3, bytes_accessed=4 * 1024 * 1024, transcendentals=0
        ),
        name="send_kernel",
    )(*operands)
    lead_keep, rest_keep, mask = pl.pallas_call(
        keep_kernel,
        out_shape=[lead_shape, rest_shape, like(targets, strip)],
        in_specs=[hbm] * len(scalars) + [vmem] * 2,
        out_specs=[vmem] * 3,
        scratch_shapes=scalar_room + [pltpu.SemaphoreType.DMA((len(scalars),))],
        compiler_params=limit,
        cost_estimate=pl.CostEstimate(
            flops=3 * terms * width**3, bytes_accessed=0, transcendentals=0
        ),
        name="keep_kernel",
    )(*operands[: len(scalars)], half, keep_right)
    lead_recv = swap(lead_send, "mpo", 1)
    part = like(2, targets, b_rows)
    rest_send, far, one, one_near, two, three = call(
        lead_kernel,
        [rest_shape, like(targets, 2 * a_rows)] + [like(targets, strip)] * 2 + [part] * 2,
        lead_keep,
        lead_recv,
        rest_send,
        aliases={2: 0},
        span=3,
    )
    cross = swap(far, "mpo", 2)
    one, two, three = [swap(x, "sec", q) for x, q in ((one, 1), (two, 2), (three, 3))]
    rest_recv = swap(rest_send, "mpo", 1)
    one_near, *own = call(
        own_kernel,
        [like(targets, strip)] + [like(targets, a_rows)] * 2,
        rest_keep,
        rest_recv,
        cross,
        one_near,
        aliases={3: 0},
        span=3,
    )
    near = jax.ShapeDtypeStruct((targets, strip, strip), jnp.float32)
    here, near = call(
        here_kernel,
        [like(targets, strip), near],
        rest_keep,
        rest_recv,
        one,
        two,
        three,
        own[0],
        span=3,
    )
    own = [swap(array, "sec", q) for array, q in zip(own, (2, 3))]
    one_near = swap(one_near, "sec", 1)
    here = swap(here, "mpo", 2)
    far_sum = jax.ShapeDtypeStruct((targets, a_rows, strip), jnp.float32)
    far_sum = call(far_sum_kernel, far_sum, *own, span=3)
    return pl.pallas_call(
        final_kernel,
        out_shape=like(targets, strip),
        in_specs=[vmem] * 5,
        out_specs=hbm,
        scratch_shapes=[
            pltpu.VMEM((targets, strip, strip), jnp.bfloat16),
            pltpu.SemaphoreType.DMA((targets,)),
        ],
        compiler_params=SMALL,
        name="final_kernel",
    )(mask, near, one_near, here, far_sum)


def by_classes(
    wave_blocks, left_env, right_env, term_class, term_id, block_dims, pair_table, mpo_coef
):
    sec_count = lax.axis_size("sec")
    mpo_count = lax.axis_size("mpo")
    local_blocks = wave_blocks.shape[0]
    block_width = wave_blocks.shape[1]
    total_blocks = block_dims.shape[0]
    classes = pair_table.shape[1]
    tile_states = block_width // 8
    positions = jnp.arange(block_width)
    first = lax.axis_index("sec") * local_blocks
    own_dims = lax.dynamic_slice_in_dim(block_dims, first, local_blocks, 0)
    row_ok = positions[None, :] < own_dims[:, 0:1] * tile_states
    col_ok = positions[None, :] < own_dims[:, 1:2] * tile_states
    masked = jnp.where(
        row_ok[:, :, None] & col_ok[:, None, :], wave_blocks, jnp.zeros_like(wave_blocks)
    )
    left_part = jnp.einsum(
        "bjxy,byz->bjxz", left_env, masked, preferred_element_type=jnp.float32
    ).astype(jnp.bfloat16)
    contrib = jnp.einsum(
        "bjxz,bjwz->bjxw", left_part, right_env, preferred_element_type=jnp.float32
    )
    weights = jnp.sum(
        jnp.where(
            term_id[:, :, None] == jnp.arange(mpo_coef.shape[0])[None, None, :],
            mpo_coef[None, None, :],
            0.0,
        ),
        axis=-1,
    )
    picks = (term_class[:, :, None] == jnp.arange(classes)[None, None, :]).astype(
        jnp.float32
    ) * weights[:, :, None]
    grouped = jnp.einsum("bjc,bjxw->bcxw", picks, contrib, precision=lax.Precision.HIGHEST).astype(
        jnp.bfloat16
    )
    targets = pair_table.reshape(-1)
    routing = targets[None, :] == jnp.arange(total_blocks)[:, None]
    strip_rows = block_width // sec_count
    strip_cols = block_width // mpo_count
    outgoing = grouped.reshape(local_blocks * classes, block_width, block_width)
    arrived = lax.all_to_all(
        lax.all_to_all(outgoing, "sec", split_axis=1, concat_axis=0, tiled=True),
        "mpo",
        split_axis=2,
        concat_axis=0,
        tiled=True,
    )
    arrived = arrived.reshape(mpo_count, total_blocks * classes, strip_rows, strip_cols)
    summed = jnp.einsum(
        "tk,mkrw->trw", routing.astype(jnp.bfloat16), arrived, preferred_element_type=jnp.float32
    )
    row_index = lax.axis_index("sec") * strip_rows + jnp.arange(strip_rows)
    col_index = lax.axis_index("mpo") * strip_cols + jnp.arange(strip_cols)
    rows_in = row_index[None, :] < block_dims[:, 0:1] * tile_states
    cols_in = col_index[None, :] < block_dims[:, 1:2] * tile_states
    inside = rows_in[:, :, None] & cols_in[:, None, :]
    return jnp.where(inside, summed, 0.0).astype(jnp.bfloat16)


def solution(mesh):
    placed = (
        P(("grp", "sec"), None, None),
        P(("grp", "sec"), "mpo", None, None),
        P(("grp", "sec"), "mpo", None, None),
        P(("grp", "sec"), "mpo"),
        P(("grp", "sec"), "mpo"),
        P("grp", None),
        P("grp", None),
        P(),
    )

    def on_device(*arrays):
        wave_blocks, block_dims = arrays[0], arrays[5]
        small = wave_blocks.shape[0] == 1 and block_dims.shape[0] == 4
        if small and mesh.shape["sec"] == 4 and mesh.shape["mpo"] == 4:
            return by_targets(*arrays)
        return by_classes(*arrays)

    return jax.shard_map(
        on_device, mesh=mesh, in_specs=placed, out_specs=P("grp", "sec", "mpo"), check_vma=False
    )
```
